32 devices in a mesh: fsdp: 16 (over z, y, x), tp: 2 (over core).
Axes of the slice: x: 2, y: 2, z: 4, core: 2. Of those that a mesh axis runs over, the one named last changes fastest.
Arguments:
- hidden_in: bfloat16 [8192, 2048], P(('fsdp', 'tp')), may hold values from -6 to 6
- out_grad: bfloat16 [8192, 2048], P(('fsdp', 'tp')), may hold values from -6 to 6
- segments: int32 [8192], P('fsdp'), may hold values from 0 to 16, as said below
- positions: int32 [8192], P('fsdp'), may hold values from 0 to 2047, as said below
- w_query: bfloat16 [2048, 2048], P('fsdp', 'tp'), may hold values from -0.125 to 0.125
- key_weight: bfloat16 [2048, 1024], P('fsdp', 'tp'), may hold values from -0.125 to 0.125
- value_weight: bfloat16 [2048, 1024], P('fsdp', 'tp'), may hold values from -0.125 to 0.125
- w_output: bfloat16 [2048, 2048], P('tp', 'fsdp'), may hold values from -1 to 1
- w_gate: bfloat16 [2048, 6144], P('fsdp', 'tp'), may hold values from -0.125 to 0.125
- w_up: bfloat16 [2048, 6144], P('fsdp', 'tp'), may hold values from -0.125 to 0.125
- w_down: bfloat16 [6144, 2048], P('tp', 'fsdp'), may hold values from -0.078125 to 0.078125
- attn_gain: bfloat16 [2048], P('fsdp'), may hold values from 0.5 to 1.5
- mlp_gain: bfloat16 [2048], P('fsdp'), may hold values from 0.5 to 1.5
- query_gain: bfloat16 [128], P('fsdp'), may hold values from 0.5 to 1.5
- key_gain: bfloat16 [128], P('fsdp'), may hold values from 0.5 to 1.5
Outputs:
- hidden_out: bfloat16 [8192, 2048], P(('fsdp', 'tp'))
- grad_in: float32 [8192, 2048], P(('fsdp', 'tp'))
- grad_query: float32 [2048, 2048], P('fsdp', 'tp')
- grad_key: float32 [2048, 1024], P('fsdp', 'tp')
- grad_value: float32 [2048, 1024], P('fsdp', 'tp')
- grad_output: float32 [2048, 2048], P('tp', 'fsdp')
- grad_gate: float32 [2048, 6144], P('fsdp', 'tp')
- grad_up: float32 [2048, 6144], P('fsdp', 'tp')
- grad_down: float32 [6144, 2048], P('tp', 'fsdp')
- grad_attn_gain: float32 [2048], P('fsdp')
- grad_mlp_gain: float32 [2048], P('fsdp')
- grad_query_gain: float32 [128], P('fsdp')
- grad_key_gain: float32 [128], P('fsdp')
The draws below stay inside these ranges and needn't reach their ends.
Inputs may be any that keep to these rules, and one draw needn't show every extreme that they name: `segments`: numbers start at 0 in each sequence of 512 tokens and never fall along it; every sequence reaches the largest number; one document of each sequence covers all of its middle half. `positions`: each token's place within its document, the first document of a sequence counting from an offset below 2048.
All inputs are finite; a program needn't handle non-finite values.
Results may differ from the reference program's by a relative error of at most 0.013.
Values may be sent and summed in bfloat16 or wider, within the bound.
No kernel may reach another device: no remote copies, remote signals or barrier semaphores. Data moves between devices by JAX's collectives and lax.ppermute only.
A program may use at most 320 MiB of HBM per device.

```python
import math
import jax
import jax.numpy as jnp
from jax import lax

MODEL_WIDTH = 2048
QUERY_HEADS = 16
KEY_VALUE_HEADS = 8
HEAD_DIM = 128
FF = 6144
TOK_DEV = 512
TOKENS = 8192


def layout(key):
    seq_total = TOKENS // TOK_DEV
    cut_count = max(2, TOK_DEV // 32)
    places = jnp.arange(TOK_DEV).astype(jnp.int32)
    outer = ((places < TOK_DEV // 4) | (places >= 3 * TOK_DEV // 4)) & (places > 0)
    raw_scores = jax.random.randint(jax.random.fold_in(key, 11), (seq_total, TOK_DEV), 0, 65536).astype(jnp.int32)
    scores = jnp.where(outer[None, :], raw_scores * TOK_DEV + places[None, :], -1).astype(jnp.int32)
    chosen = lax.top_k(scores, cut_count)[1].astype(jnp.int32)
    cuts = jnp.any(chosen[:, :, None] == places[None, None, :], axis=1)
    document_labels = jnp.cumsum(cuts.astype(jnp.int32), axis=1).astype(jnp.int32)
    starts = lax.cummax(jnp.where(cuts, places[None, :], 0).astype(jnp.int32), axis=1)
    first_cut = jnp.min(chosen, axis=1, keepdims=True).astype(jnp.int32)
    last_place = jax.random.randint(jax.random.fold_in(key, 12), (seq_total, 1), 0, 2048).astype(jnp.int32)
    last_place = jnp.maximum(last_place, first_cut - 1)
    forced = jax.random.randint(jax.random.fold_in(key, 13), (), 0, seq_total).astype(jnp.int32)
    rows = jnp.arange(seq_total).astype(jnp.int32)[:, None]
    last_place = jnp.where(rows == forced, 2047, last_place).astype(jnp.int32)
    offsets = (last_place - (first_cut - 1)).astype(jnp.int32)
    places_out = (places[None, :] - starts + jnp.where(document_labels == 0, offsets, 0)).astype(jnp.int32)
    return (document_labels.reshape(-1), places_out.reshape(-1))


def draw_segments(key, part):
    shared = layout(key)
    return shared[0]


def draw_positions(key, part):
    shared = layout(key)
    return shared[1]


def block_scale(own_key, dims, shards, smallest, top_value):
    def one(dim, shards_of):
        draws = jax.random.uniform(jax.random.fold_in(jax.random.fold_in(own_key, 6), dim), (shards_of,), jnp.float32, smallest / len(shards), top_value / len(shards))
        return jnp.repeat(jnp.exp(draws), dims[dim] // shards_of).reshape((-1,) + (1,) * (len(dims) - dim - 1))

    gain = one(*shards[0])
    for cut in shards[1:]:
        gain = gain * one(*cut)
    return gain


def gaussian(own_key, shape, width, reach, shards=(), dtype=jnp.bfloat16):
    drawn = width * jax.random.normal(own_key, shape, jnp.float32)
    if shards:
        drawn = drawn * block_scale(own_key, shape, shards, -0.22, 0.18)
    return jnp.clip(drawn, -reach, reach).astype(dtype)


def setup_inputs(seed: int = 0) -> dict:
    arg_keys = jax.random.split(jax.random.key(seed), 16)
    return {
        "hidden_in": gaussian(arg_keys[0], (TOKENS, MODEL_WIDTH), 1.0, 6.0, ((0, 32),)),
        "out_grad": gaussian(arg_keys[1], (TOKENS, MODEL_WIDTH), 1.0, 6.0, ((0, 32),)),
        "segments": draw_segments(jax.random.fold_in(arg_keys[15], 71), 0),
        "positions": draw_positions(jax.random.fold_in(arg_keys[15], 71), 0),
        "w_query": gaussian(arg_keys[4], (MODEL_WIDTH, QUERY_HEADS * HEAD_DIM), MODEL_WIDTH ** -0.5, 0.125, ((0, 16), (1, 2))),
        "key_weight": gaussian(arg_keys[5], (MODEL_WIDTH, KEY_VALUE_HEADS * HEAD_DIM), MODEL_WIDTH ** -0.5, 0.125, ((0, 16), (1, 2))),
        "value_weight": gaussian(arg_keys[6], (MODEL_WIDTH, KEY_VALUE_HEADS * HEAD_DIM), MODEL_WIDTH ** -0.5, 0.125, ((0, 16), (1, 2))),
        "w_output": gaussian(arg_keys[7], (QUERY_HEADS * HEAD_DIM, MODEL_WIDTH), (QUERY_HEADS * HEAD_DIM // 64) ** -0.5, 1.0, ((0, 2), (1, 16))),
        "w_gate": gaussian(arg_keys[8], (MODEL_WIDTH, FF), MODEL_WIDTH ** -0.5, 0.125, ((0, 16), (1, 2))),
        "w_up": gaussian(arg_keys[9], (MODEL_WIDTH, FF), MODEL_WIDTH ** -0.5, 0.125, ((0, 16), (1, 2))),
        "w_down": gaussian(arg_keys[10], (FF, MODEL_WIDTH), FF ** -0.5, 0.078125, ((0, 2), (1, 16))),
        "attn_gain": jnp.clip(1.0 + 0.1 * jax.random.normal(arg_keys[11], (MODEL_WIDTH,), jnp.float32), 0.5, 1.5).astype(jnp.bfloat16),
        "mlp_gain": jnp.clip(1.0 + 0.1 * jax.random.normal(arg_keys[12], (MODEL_WIDTH,), jnp.float32), 0.5, 1.5).astype(jnp.bfloat16),
        "query_gain": jnp.clip(1.0 + 0.1 * jax.random.normal(arg_keys[13], (HEAD_DIM,), jnp.float32), 0.5, 1.5).astype(jnp.bfloat16),
        "key_gain": jnp.clip(1.0 + 0.1 * jax.random.normal(arg_keys[14], (HEAD_DIM,), jnp.float32), 0.5, 1.5).astype(jnp.bfloat16),
    }


@jax.custom_vjp
def lowered_forward(v):
    return lax.optimization_barrier(v.astype(jnp.bfloat16)).astype(jnp.float32)

@jax.custom_vjp
def lowered_backward(v):
    return v

def low_keep(v):
    return (lowered_forward(v), None)

def low_pass(kept, grad):
    return (grad,)

def back_keep(v):
    return (v, None)

def back_low(kept, grad):
    return (lowered_forward(grad),)
lowered_forward.defvjp(low_keep, low_pass)
lowered_backward.defvjp(back_keep, back_low)
epsilon = 1e-06
rope_base = 1000000.0
highest = lax.Precision.HIGHEST

def matrix_product(left_side, right_side):
    return jnp.dot(left_side, right_side, precision=highest)

def normalize(operand, norm_gain):
    return operand * lax.rsqrt(lax.optimization_barrier(jnp.mean(operand * operand, axis=-1, keepdims=True)) + epsilon) * norm_gain

def rotate(operand, cosine_table, sine_table):
    half_size = operand.shape[-1] // 2
    lead_half = operand[..., :half_size]
    tail_half = operand[..., half_size:]
    return jnp.concatenate([lead_half * cosine_table - tail_half * sine_table, tail_half * cosine_table + lead_half * sine_table], axis=-1)

def tables(positions, head_size):
    indices = jnp.arange(head_size // 2).astype(jnp.float32)
    frequency = rope_base ** (-2.0 * indices / head_size)
    angles = positions.astype(jnp.float32)[..., None] * frequency
    return (jnp.cos(angles), jnp.sin(angles))

def attend_tokens(block_item):
    query_matrix, key_matrix, value_matrix, document_labels = block_item
    token_length = query_matrix.shape[0]
    grouped_heads = query_matrix.reshape(token_length, KEY_VALUE_HEADS, QUERY_HEADS // KEY_VALUE_HEADS, HEAD_DIM)
    scores = jnp.einsum('sgrd,tgd->grst', grouped_heads, key_matrix, precision=highest) * HEAD_DIM ** (-0.5)
    scores = lowered_backward(scores)
    places = jnp.arange(token_length)
    allowed = (document_labels[:, None] == document_labels[None, :]) & (places[None, :] <= places[:, None])
    scores = jnp.where(allowed, scores, -1e+30)
    row_top = lax.optimization_barrier(jnp.max(scores, axis=-1, keepdims=True))
    exp_terms = jnp.exp(scores - row_top)
    prob_low = lowered_forward(exp_terms / lax.optimization_barrier(jnp.sum(exp_terms, axis=-1, keepdims=True)))
    attention_output = jnp.einsum('grst,tgd->sgrd', prob_low, value_matrix, precision=highest)
    return attention_output.reshape(token_length, QUERY_HEADS * HEAD_DIM)

def forward(inputs, params, document_labels, positions):
    w_query, key_weight, value_weight, w_output, w_gate, w_up, w_down, attn_gain, mlp_gain, query_gain, key_gain = params
    sequence_count, token_length = document_labels.shape
    cosine_table, sine_table = tables(positions.reshape(-1), HEAD_DIM)
    cosine_table = cosine_table[:, None, :]
    sine_table = sine_table[:, None, :]
    input_normalized = lowered_forward(normalize(inputs, attn_gain))
    query_raw = lowered_backward(matrix_product(input_normalized, w_query)).reshape(-1, QUERY_HEADS, HEAD_DIM)
    key_unrotated = lowered_backward(matrix_product(input_normalized, key_weight)).reshape(-1, KEY_VALUE_HEADS, HEAD_DIM)
    query_matrix = lowered_forward(rotate(normalize(query_raw, query_gain), cosine_table, sine_table))
    key_matrix = lowered_forward(rotate(normalize(key_unrotated, key_gain), cosine_table, sine_table))
    value_matrix = lowered_forward(lowered_backward(matrix_product(input_normalized, value_weight))).reshape(-1, KEY_VALUE_HEADS, HEAD_DIM)
    attention_output = lax.map(jax.checkpoint(attend_tokens), (query_matrix.reshape(sequence_count, token_length, QUERY_HEADS, HEAD_DIM), key_matrix.reshape(sequence_count, token_length, KEY_VALUE_HEADS, HEAD_DIM), value_matrix.reshape(sequence_count, token_length, KEY_VALUE_HEADS, HEAD_DIM), document_labels))
    attention_output = lowered_forward(lowered_backward(attention_output.reshape(-1, QUERY_HEADS * HEAD_DIM)))
    middle = inputs + lowered_backward(matrix_product(attention_output, w_output))
    normed_mid = lowered_forward(normalize(middle, mlp_gain))
    gate_proj = lowered_backward(matrix_product(normed_mid, w_gate))
    up_proj = lowered_backward(matrix_product(normed_mid, w_up))
    activated = lowered_forward(jax.nn.silu(gate_proj) * up_proj)
    return middle + lowered_backward(matrix_product(activated, w_down))

def reference(hidden_in, out_grad, segments, positions, w_query, key_weight, value_weight, w_output, w_gate, w_up, w_down, attn_gain, mlp_gain, query_gain, key_gain):
    params = tuple((item.astype(jnp.float32) for item in (w_query, key_weight, value_weight, w_output, w_gate, w_up, w_down, attn_gain, mlp_gain, query_gain, key_gain)))
    seq_total = TOKENS // TOK_DEV
    group_size = math.gcd(seq_total, max(1, 4096 // TOK_DEV))
    group_count = seq_total // group_size
    inputs_all = hidden_in.astype(jnp.float32).reshape(group_count, group_size * TOK_DEV, MODEL_WIDTH)
    grads_all = out_grad.astype(jnp.float32).reshape(group_count, group_size * TOK_DEV, MODEL_WIDTH)
    labels_all = segments.reshape(group_count, group_size, TOK_DEV)
    places_all = positions.reshape(group_count, group_size, TOK_DEV)

    def one_group(totals, group_item):
        inputs, upstream, document_labels, places = group_item

        def local_forward(local_in, local_params):
            return forward(local_in, local_params, document_labels, places)
        result, pullback = jax.vjp(local_forward, inputs, params)
        input_grad, param_grads = pullback(upstream)
        totals = tuple((left_side + right_side for left_side, right_side in zip(totals, param_grads)))
        return (totals, (result, input_grad))
    starting = tuple((jnp.zeros_like(item) for item in params))
    totals, (results, input_grads) = lax.scan(one_group, starting, (inputs_all, grads_all, labels_all, places_all))
    hidden_out = results.reshape(TOKENS, MODEL_WIDTH).astype(jnp.bfloat16)
    grad_in = input_grads.reshape(TOKENS, MODEL_WIDTH)
    return (hidden_out, grad_in, totals[0], totals[1], totals[2], totals[3], totals[4], totals[5], totals[6], totals[7], totals[8], totals[9], totals[10])
```

```python
import functools

import jax
import jax.numpy as jnp
from jax import lax
from jax.experimental import pallas as pl
from jax.experimental.pallas import tpu as pltpu
from jax.sharding import Mesh, PartitionSpec as P

epsilon = 1e-06
rope_base = 1000000.0
bf16 = jnp.bfloat16
f32 = jnp.float32
BESIDE = pl.CostEstimate(flops=1 << 20, bytes_accessed=1 << 16, transcendentals=0)


def dot(left, right):
    return jnp.dot(left, right, preferred_element_type=f32)


def dot_right_t(left, right):
    return lax.dot_general(left, right, (((1,), (1,)), ((), ())), preferred_element_type=f32)


def dot_left_t(left, right):
    return lax.dot_general(left, right, (((0,), (0,)), ((), ())), preferred_element_type=f32)


def normalize(operand, norm_gain):
    return (
        operand
        * lax.rsqrt(jnp.mean(operand * operand, axis=-1, keepdims=True) + epsilon)
        * norm_gain
    )


def norm_back(operand, norm_gain, upstream):
    factor = lax.rsqrt(jnp.mean(operand * operand, axis=-1, keepdims=True) + epsilon)
    weighted = upstream * norm_gain
    inner = jnp.mean(weighted * operand, axis=-1, keepdims=True)
    return factor * weighted - operand * factor * factor * factor * inner


def tables(positions, head_size):
    indices = jnp.arange(head_size // 2).astype(f32)
    frequency = rope_base ** (-2.0 * indices / head_size)
    angles = positions.astype(f32)[..., None] * frequency
    cosine, sine = jnp.cos(angles), jnp.sin(angles)
    return (jnp.concatenate([cosine, cosine], -1), jnp.concatenate([-sine, sine], -1))


def half_turn(operand):
    return pltpu.roll(operand, operand.shape[-1] // 2, 1)


def lay_in_order(scratch, refs, core):
    half = refs[0].shape[1]
    for j, ref in enumerate(refs):
        scratch[pl.ds(pl.multiple_of((core ^ j) * half, half), half)] = ref[0]


def head_rows(raw, heads, repeat, gains, cosine, sine):
    size = gains.shape[1]

    def turned(column, gain):
        rows = normalize(raw[:, column * size : (column + 1) * size], gain)
        return (rows * cosine + half_turn(rows) * sine).astype(bf16)

    queries = [turned(h, gains[0:1]) for h in range(heads * repeat)]
    keys = [turned(heads * repeat + g, gains[1:2]) for g in range(heads)]
    first = heads * repeat + heads
    values = [
        raw[:, (first + g) * size : (first + g + 1) * size].astype(bf16) for g in range(heads)
    ]
    return queries, keys, values


def masked_probs(key, query, allowed):
    scores = dot_right_t(key, query) * query.shape[1] ** (-0.5)
    scores = jnp.where(allowed, scores, -1e30)
    exp_terms = jnp.exp(scores - jnp.max(scores, axis=0, keepdims=True))
    return exp_terms * (1.0 / jnp.sum(exp_terms, axis=0, keepdims=True))


def query_strips(rows, column_ref, row_ref):
    step = min(128, rows)
    for first in range(0, rows, step):
        seen = first + step
        keys = lax.broadcasted_iota(jnp.int32, (seen, step), 0)
        queries = lax.broadcasted_iota(jnp.int32, (seen, step), 1) + first
        same = column_ref[0, :seen, 0:1] == row_ref[0, 0:1, first:seen]
        yield slice(first, seen), seen, same & (keys <= queries)


def attend_kernel(cores, heads, repeat, core_ref, *refs):
    raws, refs = refs[:cores], refs[cores:]
    cos_ref, sin_ref, column_ref, row_ref, gain_ref = refs[:5]
    outs, raw, rows_out = refs[5:-2], refs[-2], refs[-1]
    core = core_ref[0]
    half = raws[0].shape[1]
    lay_in_order(raw, raws, core)
    queries, keys, values = head_rows(
        raw, heads, repeat, gain_ref[...], cos_ref[0], sin_ref[0]
    )
    size = gain_ref.shape[1]
    turned = [value.astype(f32).T.astype(bf16) for value in values]
    for at, seen, allowed in query_strips(raw.shape[0], column_ref, row_ref):
        for h, query in enumerate(queries):
            g = h // repeat
            probs = masked_probs(keys[g][:seen], query[at], allowed).astype(bf16)
            rows = dot(turned[g][:, :seen], probs).T
            rows_out[at, h * size : (h + 1) * size] = rows.astype(bf16)
    for j, out in enumerate(outs):
        out[0] = rows_out[pl.ds(pl.multiple_of((core ^ j) * half, half), half)]


def attend_back_kernel(cores, heads, repeat, core_ref, *refs):
    raws, grads, refs = refs[:cores], refs[cores : 2 * cores], refs[2 * cores :]
    cos_ref, sin_ref, column_ref, row_ref, gain_ref = refs[:5]
    outs, gain_out = refs[5 : 5 + cores], refs[5 + cores]
    raw, grad, totals, rows_out = refs[6 + cores :]
    core = core_ref[0]
    half = raws[0].shape[1]
    cosine, sine, gains = cos_ref[0], sin_ref[0], gain_ref[...]
    lay_in_order(raw, raws, core)
    lay_in_order(grad, grads, core)
    queries, keys, values = head_rows(raw, heads, repeat, gains, cosine, sine)
    size = gains.shape[1]
    scale = size ** (-0.5)
    count = heads * repeat

    @pl.when(pl.program_id(0) == 0)
    def _():
        gain_out[...] = jnp.zeros_like(gain_out)

    def columns(i):
        return slice(i * size, (i + 1) * size)

    turned_keys = [key.astype(f32).T.astype(bf16) for key in keys]
    totals[:, count * size :] = jnp.zeros_like(totals[:, count * size :])
    for at, seen, allowed in query_strips(raw.shape[0], column_ref, row_ref):
        for g in range(heads):
            key_grad = value_grad = None
            for h in range(g * repeat, (g + 1) * repeat):
                probs = masked_probs(keys[g][:seen], queries[h][at], allowed)
                out_grad = grad[at, columns(h)]
                prob_grad = dot_right_t(values[g][:seen], out_grad)
                delta = jnp.sum(probs * prob_grad, axis=0, keepdims=True)
                score_grad = (probs * (prob_grad - delta)).astype(bf16)
                totals[at, columns(h)] = dot(turned_keys[g][:, :seen], score_grad).T * scale
                key_part = dot(score_grad, queries[h][at])
                value_part = dot(probs.astype(bf16), out_grad)
                key_grad = key_part if key_grad is None else key_grad + key_part
                value_grad = value_part if value_grad is None else value_grad + value_part
            totals[:seen, columns(count + g)] += key_grad * scale
            totals[:seen, columns(count + heads + g)] += value_grad
    for i in range(count + heads):
        row = 0 if i < count else 1
        upstream = totals[:, columns(i)]
        turned = upstream * cosine - half_turn(upstream) * sine
        rows = raw[:, columns(i)]
        factor = lax.rsqrt(jnp.mean(rows * rows, axis=-1, keepdims=True) + epsilon)
        gain_out[row : row + 1] += jnp.sum(turned * rows * factor, axis=0, keepdims=True)
        back = norm_back(rows, gains[row : row + 1], turned)
        rows_out[:, columns(i)] = back.astype(bf16)
    rows_out[:, (count + heads) * size :] = totals[:, (count + heads) * size :].astype(bf16)
    for j, out in enumerate(outs):
        out[0] = rows_out[pl.ds(pl.multiple_of((core ^ j) * half, half), half)]


def attention_call(kernel, name, core, halves, shared, gains, outs, extra_out, scratch):
    def per_sequence(array):
        return pl.BlockSpec((1,) + array.shape[1:], lambda i: (i, 0, 0))

    whole = pl.BlockSpec(gains.shape, lambda i: (0, 0))
    out_specs = [per_sequence(shape) for shape in outs] + [
        pl.BlockSpec(shape.shape, lambda i: (0, 0)) for shape in extra_out
    ]
    return pl.pallas_call(
        kernel,
        grid=(halves[0].shape[0],),
        in_specs=[pl.BlockSpec(memory_space=pltpu.SMEM)]
        + [per_sequence(array) for array in halves + shared]
        + [whole],
        out_specs=out_specs,
        out_shape=outs + extra_out,
        scratch_shapes=[pltpu.VMEM(shape, dtype) for shape, dtype in scratch],
        compiler_params=pltpu.CompilerParams(vmem_limit_bytes=48 << 20),
        cost_estimate=BESIDE,
        name=name,
    )(core.reshape(1), *halves, *shared, gains)


def resident(shape):
    zeros = (0,) * len(shape)
    return pl.BlockSpec(shape, lambda i: zeros, pipeline_mode=pl.Buffered(1))


def project_kernel(count, *refs):
    lefts, rights, outs = refs[:count], refs[count : 2 * count], refs[2 * count :]
    total = dot_right_t(lefts[0][...], rights[0][0])
    for left, right in zip(lefts[1:], rights[1:]):
        total = total + dot_right_t(left[...], right[0])
    first = 0
    for out in outs:
        out[...] = total[first : first + out.shape[0]].astype(out.dtype)
        first += out.shape[0]


def project(lefts, rights, places, first, sizes, step, name):
    parts = rights[0].shape[0]
    rows = sum(sizes)

    def left_spec(left):
        return pl.BlockSpec(
            (rows, left.shape[1]), lambda i: (first // rows, 0), pipeline_mode=pl.Buffered(1)
        )

    def right_spec(left, place):
        return pl.BlockSpec((1, step, left.shape[1]), lambda i: (i, 0, place))

    return list(
        pl.pallas_call(
            functools.partial(project_kernel, len(lefts)),
            grid=(parts,),
            in_specs=[left_spec(left) for left in lefts]
            + [right_spec(left, place) for left, place in zip(lefts, places)],
            out_specs=[pl.BlockSpec((size, step), lambda i: (0, i)) for size in sizes],
            out_shape=[
                jax.ShapeDtypeStruct((size, parts * step), bf16 if first or k else f32)
                for k, size in enumerate(sizes)
            ],
            compiler_params=pltpu.CompilerParams(vmem_limit_bytes=56 << 20),
            cost_estimate=BESIDE,
            name=name,
        )(*lefts, *rights)
    )


def project_and_send(lefts, rights, places, rows, step, name):
    if lax.axis_size("model") == 1:
        return project(lefts, rights, places, 0, [rows], step, name)[0], [], []
    half = rows // 2
    far = project(lefts, rights, places, 3 * rows, [half] * 2, step, name + "_far")
    got = [trade(far[0], "model", 1), trade(far[1], "model", 2)]
    own, *near = project(lefts, rights, places, 0, [rows] + [half] * 4, step, name)
    return own, got, send_near(near, got)


def put_rows(whole, pieces, change):
    first = 0
    for piece in pieces:
        whole[first : first + piece.shape[0]] = change(piece[...])
        first += piece.shape[0]


def rows_kernel(kind, count, *refs):
    (own, base), got, refs = refs[:2], refs[2 : 2 + count], list(refs[2 + count :])
    total = own[...]
    if count == 4:
        upper = got[0][...].astype(f32) + got[1][...].astype(f32)
        lower = got[2][...].astype(f32) + got[3][...].astype(f32)
        total += jnp.where(pl.program_id(0) < pl.num_programs(0) // 2, upper, lower)
    else:
        for piece in got:
            total += piece[...].astype(f32)
    rows = base[...].astype(f32)
    if kind == "sum":
        refs[0][...] = (rows + total).astype(bf16)
    elif kind == "norm":
        gain, whole, low = refs
        whole[...] = rows + total
        low[...] = normalize(rows + total, gain[...]).astype(bf16)
    else:
        gain, more, whole = refs[:3]
        total = more[...].astype(f32) + norm_back(rows, gain[...], total)
        whole[...] = total
        for low in refs[3:]:
            low[...] = total.astype(bf16)


def rows_call(kind, own, base, got, gain, more, dtypes, name):
    rows, width = own.shape
    step = rows // 4
    strip = pl.BlockSpec((step, width), lambda i: (i, 0))
    upper = pl.BlockSpec((step, width), lambda i: (jnp.minimum(i, 1), 0))
    lower = pl.BlockSpec((step, width), lambda i: (jnp.maximum(i - 2, 0), 0))
    operands = [own, base] + list(got)
    in_specs = [strip, strip]
    in_specs += [upper, upper, lower, lower] if len(got) == 4 else [strip] * len(got)
    if gain is not None:
        operands.append(gain.reshape(1, width))
        in_specs.append(resident((1, width)))
    if more is not None:
        operands.append(more)
        in_specs.append(strip)
    return list(
        pl.pallas_call(
            functools.partial(rows_kernel, kind, len(got)),
            grid=(4,),
            in_specs=in_specs,
            out_specs=[strip] * len(dtypes),
            out_shape=[jax.ShapeDtypeStruct((rows, width), dtype) for dtype in dtypes],
            compiler_params=pltpu.CompilerParams(vmem_limit_bytes=32 << 20),
            cost_estimate=BESIDE,
            name=name,
        )(*operands)
    )


def rows_product_kernel(count, normed, *refs):
    pieces, refs = refs[:count], list(refs[count:])
    gain = refs.pop(0)[...] if normed else None
    weight, out = refs[0], refs[-1]
    whole = pieces[0]
    if count > 1 or normed:
        whole = refs[1]

        def change(rows):
            return normalize(rows.astype(f32), gain).astype(bf16) if normed else rows

        put_rows(whole, pieces, change)
    columns = weight.shape[2]
    out[...] = dot(whole[...], weight[...].reshape(-1, columns)).astype(out.dtype)


def rows_product(pieces, gain, weight, block, place, step, dtype, name):
    rows = sum(piece.shape[0] for piece in pieces)
    parts, width = weight.shape[0], pieces[0].shape[1]
    joined = len(pieces) > 1 or gain is not None
    shapes = [jax.ShapeDtypeStruct((rows, width), bf16)] if joined else []
    shapes += [jax.ShapeDtypeStruct((rows, block), dtype)]
    gains = [] if gain is None else [gain.reshape(1, -1)]
    got = pl.pallas_call(
        functools.partial(rows_product_kernel, len(pieces), gain is not None),
        grid=(1,),
        in_specs=[resident(piece.shape) for piece in list(pieces) + gains]
        + [
            pl.BlockSpec(
                (parts, step, block), lambda i: (0, 0, place), pipeline_mode=pl.Buffered(1)
            )
        ],
        out_specs=[resident(shape.shape) for shape in shapes],
        out_shape=shapes,
        compiler_params=pltpu.CompilerParams(vmem_limit_bytes=56 << 20),
        cost_estimate=BESIDE,
        name=name,
    )(*pieces, *gains, weight)
    return (got[0], got[1]) if joined else (pieces[0], got[0])


def weight_grad_kernel(counts, number, *refs):
    count = sum(counts)
    lefts, rights, refs = refs[:count], refs[count : 2 * count], refs[2 * count :]
    received, below, out = refs[:number], refs[number:-1], refs[-1]
    rows = lefts[0].shape[1]
    first = pair = 0
    for size in counts:
        total = dot_left_t(lefts[pair][...], rights[pair][...])
        for i in range(pair + 1, pair + size):
            total = total + dot_left_t(lefts[i][...], rights[i][...])
        pair += size
        at = slice(first, first + total.shape[1])
        for block in received:
            total = total + block[0, :, at].astype(f32)
        out[0, :rows, at] = total.astype(bf16)
        first += total.shape[1]
    for block in below:
        out[0, rows:] = block[...]


def weight_grad(groups, received, below, step, name):
    pairs = [pair for group in groups for pair in group]
    rows, width = pairs[0][0].shape
    columns = sum(group[0][1].shape[1] for group in groups)
    deep = step + sum(block.shape[0] for block in below)
    return pl.pallas_call(
        functools.partial(
            weight_grad_kernel, [len(group) for group in groups], len(received)
        ),
        grid=(width // step,),
        in_specs=[pl.BlockSpec((rows, step), lambda i: (0, i))] * len(pairs)
        + [resident(right.shape) for _, right in pairs]
        + [pl.BlockSpec((1, step, columns), lambda i: (i, 0, 0))] * len(received)
        + [resident(block.shape) for block in below],
        out_specs=pl.BlockSpec((1, deep, columns), lambda i: (i, 0, 0)),
        out_shape=jax.ShapeDtypeStruct((width // step, deep, columns), bf16),
        compiler_params=pltpu.CompilerParams(vmem_limit_bytes=56 << 20),
        cost_estimate=BESIDE,
        name=name,
    )(*[left for left, _ in pairs], *[right for _, right in pairs], *received, *below)


def near_kernel(size, widths, me_ref, *refs):
    pieces, outs = refs[:size], refs[size:]
    rows = pieces[0].shape[0]
    for k, piece in enumerate(pieces):
        at = pl.ds(pl.multiple_of((me_ref[0] ^ k) * rows, rows), rows)
        first = 0
        for out, width in zip(outs, widths):
            out[at] = piece[:, first : first + width]
            first += width


def near_call(me, pieces, widths, name):
    rows = len(pieces) * pieces[0].shape[0]
    shapes = [jax.ShapeDtypeStruct((rows, width), bf16) for width in widths]
    return list(
        pl.pallas_call(
            functools.partial(near_kernel, len(pieces), widths),
            grid=(1,),
            in_specs=[pl.BlockSpec(memory_space=pltpu.SMEM)]
            + [resident(piece.shape) for piece in pieces],
            out_specs=[resident(shape.shape) for shape in shapes],
            out_shape=shapes,
            compiler_params=pltpu.CompilerParams(vmem_limit_bytes=32 << 20),
            cost_estimate=BESIDE,
            name=name,
        )(me.reshape(1), *pieces)
    )


def owned_kernel(size, layout, weighted, me_ref, *refs):
    count = size * len(layout)
    pieces, refs = refs[:count], refs[count:]
    weights, gain, refs = refs[:weighted], refs[weighted], refs[weighted + 1 :]
    outs, sums, below = refs[:-2], refs[-2], refs[-1]
    rows = gain.shape[0]
    total = jnp.zeros((rows, 1), f32)
    under = None
    for c, ranges in enumerate(layout):
        for k in range(size):
            piece = pieces[c * size + k]
            owner = me_ref[0] ^ k
            first = 0
            for number, place, wide, count, turned in ranges:
                block = piece[:rows, first : first + count].astype(f32)
                first += count
                at = pl.ds(pl.multiple_of(owner * wide + place, 128), count)
                if turned:
                    outs[number][at] = block.T
                    continue
                outs[number][:, at] = block
                if number < weighted:
                    product = weights[number][:, at].astype(f32) * block
                    total = total + jnp.sum(product, axis=1, keepdims=True)
            if piece.shape[0] > rows:
                more = piece[rows : rows + 8].astype(f32)
                under = more if under is None else under + more
    sums[...] = jnp.broadcast_to(total / gain[:, 0:1], sums.shape)
    below[...] = jnp.zeros_like(below) if under is None else under


def owned_call(me, chunks, layout, weights, gain, shapes, name):
    size = len(chunks[0])
    pieces = [piece for chunk in chunks for piece in chunk]
    rows = gain.shape[0]
    outs = [jax.ShapeDtypeStruct(shape, f32) for shape in shapes]
    outs += [jax.ShapeDtypeStruct((rows, 128), f32)]
    outs += [jax.ShapeDtypeStruct((8, pieces[0].shape[1]), f32)]
    column = jnp.broadcast_to(gain.astype(f32)[:, None], (rows, 128))
    operands = pieces + list(weights) + [column]
    return pl.pallas_call(
        functools.partial(owned_kernel, size, layout, len(weights)),
        grid=(1,),
        in_specs=[pl.BlockSpec(memory_space=pltpu.SMEM)]
        + [resident(array.shape) for array in operands],
        out_specs=[resident(shape.shape) for shape in outs],
        out_shape=outs,
        compiler_params=pltpu.CompilerParams(vmem_limit_bytes=48 << 20),
        cost_estimate=BESIDE,
        name=name,
    )(me.reshape(1), *operands)


def hidden_kernel(first, cores, x_count, g_count, tiles, *refs):
    refs = list(refs)

    def pop(number):
        taken, refs[:number] = refs[:number], []
        return taken

    x_pieces, g_pieces = (pop(x_count), pop(g_count)) if first else ([], [])
    x_all, g_all = (None, None) if first else pop(2)
    weights = [pop(3) for _ in range(cores)]
    if first:
        x_all, g_all = pop(2)
    grads_out, acts_out = pop(cores), pop(cores)
    step = pl.program_id(0)

    if first:

        @pl.when(step == 0)
        def _():
            put_rows(x_all, x_pieces, lambda rows: rows)
            put_rows(g_all, g_pieces, lambda rows: rows)

    def one_core(j):
        w_gate, w_up, w_down = (ref[...].reshape(-1, ref.shape[2]) for ref in weights[j])
        tile = w_gate.shape[1]
        place = step - j * tiles
        gate_place = pl.ds(pl.multiple_of(place * tile, tile), tile)
        up_place = pl.ds(pl.multiple_of((tiles + place) * tile, tile), tile)
        rows = x_all.shape[0] // 2
        for at in (slice(0, rows), slice(rows, None)):
            gate = dot(x_all[at], w_gate)
            up = dot(x_all[at], w_up)
            act_grad = dot(g_all[at], w_down)
            sigma = 1.0 / (1.0 + jnp.exp(-gate))
            silu = gate * sigma
            gate_grad = act_grad * up * sigma * (1.0 + gate * (1.0 - sigma))
            acts_out[j][at, gate_place] = (silu * up).astype(bf16)
            grads_out[j][at, gate_place] = gate_grad.astype(bf16)
            grads_out[j][at, up_place] = (act_grad * silu).astype(bf16)

    for j in range(cores):
        pl.when((step >= j * tiles) & (step < (j + 1) * tiles))(functools.partial(one_core, j))


def hidden_call(x_pieces, g_pieces, weights, name):
    cores, first = len(weights), len(x_pieces) > 1
    data, near, columns = weights[0].shape
    width = data * near
    units = columns // 3
    tile = min(256, units)
    tiles = units // tile
    rows = sum(piece.shape[0] for piece in x_pieces)

    def weight_specs(j):
        return [
            pl.BlockSpec(
                (data, near, tile),
                lambda i, k=k: (0, 0, k * tiles + jnp.clip(i - j * tiles, 0, tiles - 1)),
            )
            for k in range(3)
        ]

    operands = list(x_pieces) + list(g_pieces)
    in_specs = [resident(array.shape) for array in operands]
    for j, weight in enumerate(weights):
        in_specs += weight_specs(j)
        operands += [weight] * 3
    shapes = [jax.ShapeDtypeStruct((rows, width), bf16)] * 2 if first else []
    shapes += [jax.ShapeDtypeStruct((rows, 2 * units), bf16)] * cores
    shapes += [jax.ShapeDtypeStruct((rows, units), bf16)] * cores
    got = pl.pallas_call(
        functools.partial(
            hidden_kernel, first, cores, len(x_pieces), len(g_pieces), tiles
        ),
        grid=(cores * tiles,),
        in_specs=in_specs,
        out_specs=[resident(shape.shape) for shape in shapes],
        out_shape=shapes,
        compiler_params=pltpu.CompilerParams(vmem_limit_bytes=60 << 20),
        cost_estimate=BESIDE,
        name=name,
    )(*operands)
    got = list(got)
    kept, got = (got[:2], got[2:]) if first else ([x_pieces[0], g_pieces[0]], got)
    return kept, got[:cores], got[cores:]


def phase(always, body):
    def never():
        return jax.tree.map(lambda leaf: jnp.zeros(leaf.shape, leaf.dtype), jax.eval_shape(body))

    return lax.cond(always, body, never)


def trade(block, axis, step):
    return lax.ppermute(block, axis, [(i, i ^ step) for i in range(lax.axis_size(axis))])


def spread(block, *first):
    if lax.axis_size("model") == 1:
        return [block]
    near = [block, trade(block, "model", 1), trade(block, "model", 2)]
    return near + far_halves(near, *first)


def far_halves(near, *first):
    half = near[0].shape[0] // 2
    _, by_x, by_y = after(near, *first) if first else near
    return [trade(by_x[:half], "model", 2), trade(by_y[half:], "model", 1)]


def send_near(near, far):
    x_upper, x_lower, y_upper, y_lower = near
    x_upper, y_lower = after((x_upper, y_lower), *far)
    y_upper = (y_upper.astype(f32) + far[0].astype(f32)).astype(bf16)
    x_lower = (x_lower.astype(f32) + far[1].astype(f32)).astype(bf16)
    return [
        trade(x_upper, "model", 1),
        trade(y_upper, "model", 2),
        trade(x_lower, "model", 1),
        trade(y_lower, "model", 2),
    ]


def swap(piece_of):
    me = lax.axis_index("model")
    others = range(1, lax.axis_size("model"))
    return [piece_of(me)] + [trade(piece_of(me ^ k), "model", k) for k in others]


def take(array, index, count):
    size = array.shape[1] // count
    return lax.dynamic_slice_in_dim(array, index * size, size, 1)


def rows_at(array):
    return lambda i: lax.dynamic_index_in_dim(array, i, 0, keepdims=False)


def in_order(pieces):
    me = lax.axis_index("model")
    size = len(pieces)
    return jnp.stack(
        [lax.select_n(me, *[pieces[j ^ i] for j in range(size)]) for i in range(size)]
    )


def after(value, *first):
    return lax.optimization_barrier((value,) + first)[0]


def on_device(
    hidden_in,
    out_grad,
    segments,
    positions,
    w_query,
    key_weight,
    value_weight,
    w_output,
    w_gate,
    w_up,
    w_down,
    attn_gain,
    mlp_gain,
    query_gain,
    key_gain,
):
    data = lax.axis_size("data")
    model = lax.axis_size("model")
    cores = lax.axis_size("tp")
    core = lax.axis_index("tp")
    seq_len = positions.shape[0]
    half = seq_len // cores
    shard = w_query.shape[0]
    width = hidden_in.shape[1]
    head_size = query_gain.shape[0] * data * model
    q_heads = w_query.shape[1] // model // head_size
    kv_heads = key_weight.shape[1] // model // head_size
    repeat = q_heads // kv_heads
    q_cols = q_heads * head_size
    kv_cols = kv_heads * head_size
    cols = q_cols + 2 * kv_cols
    wide = cols + q_cols
    ff = w_gate.shape[1] // model
    always = (segments[0] * segments[0] + segments[0]) % 2 == 0

    small = jnp.concatenate([attn_gain, mlp_gain, query_gain, key_gain])
    small_rows = -(-small.shape[0] // wide)
    place_rows = -(-seq_len // wide)

    def as_rows(vector, rows):
        return jnp.pad(vector, (0, rows * wide - vector.shape[0])).reshape(rows, wide)

    extra = jnp.concatenate(
        [
            as_rows(small, small_rows),
            as_rows(segments.astype(bf16), place_rows),
            as_rows((positions // 8).astype(bf16), place_rows),
            as_rows((positions % 8).astype(bf16), place_rows),
        ]
    )
    extra = jnp.pad(extra, ((0, -extra.shape[0] % 16), (0, 0)))
    turned_output = w_output.T

    def attn_piece(i):
        parts = [
            take(w_query, i, model),
            take(key_weight, i, model),
            take(value_weight, i, model),
            take(turned_output, i, model),
        ]
        return jnp.concatenate([jnp.concatenate(parts, axis=1), extra])

    turned_down = w_down.T
    chunks = [ff - ff // 3, ff // 3] if ff % 768 == 0 else [ff]
    starts = [sum(chunks[:c]) for c in range(len(chunks))]

    def over_data(pieces):
        return lax.all_gather(pieces, "data", axis=0, tiled=False)

    attn_got = swap(attn_piece)
    x_sent, attn_got = lax.optimization_barrier((hidden_in, attn_got))
    x_near = [x_sent, trade(x_sent, "model", 1), trade(x_sent, "model", 2)]
    tied = lax.optimization_barrier((w_gate, w_up, turned_down, x_near))
    w_gate_sent, w_up_sent, turned_down, x_near = tied
    x_blocks = x_near + far_halves(x_near)
    mlp_got = swap(
        lambda i: jnp.concatenate(
            [
                take(weight, i, model)[:, first : first + count]
                for first, count in zip(starts, chunks)
                for weight in (w_gate_sent, w_up_sent, turned_down)
            ],
            axis=1,
        )
    )

    def places_of(first):
        rows = [
            got[shard + first : shard + first + place_rows].reshape(-1)[:seq_len]
            for got in attn_got
        ]
        return jnp.stack(rows).astype(f32)

    seg_all = places_of(small_rows)
    pos_all = 8.0 * places_of(small_rows + place_rows) + places_of(small_rows + 2 * place_rows)
    cosine, sine = tables(pos_all, head_size)

    attn_near = in_order(attn_got)
    gain_rows = attn_near[:, shard : shard + small_rows].reshape(-1, wide)
    gain_rows = jnp.pad(gain_rows, ((0, -gain_rows.shape[0] % 16), (0, 0)))
    near = jnp.concatenate([attn_near[:, :shard].reshape(-1, wide), gain_rows])
    me = lax.axis_index("model")
    mlp_near = near_call(me, mlp_got, [3 * count for count in chunks], "hidden_exchange")
    attn_full = over_data(near)
    tied = lax.optimization_barrier((attn_full, mlp_near, x_blocks, cosine, sine))
    attn_full, mlp_near, x_blocks, cosine, sine = tied
    mlp_full = [over_data(piece) for piece in mlp_near]

    gains = attn_full[:, model * shard : model * shard + model * small_rows]
    gains = gains.reshape(data * model, -1).astype(f32)
    part = query_gain.shape[0]
    gain_in = gains[:, :shard].reshape(-1)
    gain_mid = gains[:, shard : 2 * shard].reshape(-1)
    gain_query = gains[:, 2 * shard : 2 * shard + part].reshape(-1)
    gain_key = gains[:, 2 * shard + part : 2 * shard + 2 * part].reshape(-1)
    def with_cores(weight):
        return [weight] + [trade(weight, "tp", j) for j in range(1, cores)]

    near_rows = model * shard
    grad_sent, mlp_near = lax.optimization_barrier((out_grad, mlp_near))
    grad_blocks = [out_grad] + [trade(grad_sent, "model", k) for k in range(1, model)]

    seg_rows = jnp.pad(seg_all[:, None], ((0, 0), (0, 7), (0, 0)))
    seg_columns = seg_all[:, :, None]
    head_gains = jnp.pad(jnp.stack([gain_query, gain_key]), ((0, 6), (0, 0)))
    shared = [cosine, sine, seg_columns, seg_rows]
    o_place = [cols // q_cols] * cores

    def attention_phase():
        w_attn = with_cores(attn_full)
        normed_in, first_raw = rows_product(
            x_blocks, gain_in, w_attn[0], cols, 0, near_rows, f32, "query_key_value"
        )
        raw = [first_raw.reshape(model, half, cols)]
        for j in range(1, cores):
            mine = rows_product(
                [normed_in], None, w_attn[j], cols, 0, near_rows, f32, "query_key_value_other"
            )[1]
            raw.append(trade(mine, "tp", j).reshape(model, half, cols))
        attended = attention_call(
            functools.partial(attend_kernel, cores, kv_heads, repeat),
            "attend",
            core,
            raw,
            shared,
            head_gains,
            [jax.ShapeDtypeStruct((model, half, q_cols), bf16)] * cores,
            [],
            [((seq_len, cols), f32), ((seq_len, q_cols), bf16)],
        )
        att_pieces = [attended[0]] + [trade(attended[j], "tp", j) for j in range(1, cores)]
        att_flat = [piece.reshape(-1, q_cols) for piece in att_pieces]
        all_rows = with_cores(normed_in)
        return w_attn[1:], all_rows, raw, att_flat, list(attended)

    w_others, normed_in, raw, att_flat, attended = phase(always, attention_phase)
    w_attn = [attn_full] + w_others
    att_flat, grad_blocks = lax.optimization_barrier((att_flat, grad_blocks))

    def data_sum(total):
        return lax.psum_scatter(total, "data", scatter_dimension=0, tiled=False)

    def out_phase():
        own, _, got = project_and_send(
            att_flat, w_attn, o_place, half, near_rows, "attention_out"
        )
        middle, low = rows_call(
            "norm", own, hidden_in, got, gain_mid, None, [f32, bf16], "middle"
        )
        return middle, spread(low)

    middle, mid_blocks = phase(always, out_phase)

    def hidden_others(kept, rows, name):
        return [
            weight_grad([[(kept[k], rows[k][j])] for k in range(2)], [], (), near_rows, name)
            for j in range(1, cores)
        ]

    def hidden_own(kept, rows, received, name):
        pairs = [[(kept[k], rows[k][0])] for k in range(2)]
        return weight_grad(pairs, received, (), near_rows, name)

    def first_phase():
        weights = with_cores(mlp_full[0])
        rows, *by_core = hidden_call(mid_blocks, grad_blocks, weights[:1], "hidden_units_a")
        by_core = [by_core]
        for weight in weights[1:]:
            got = hidden_call(*[[whole] for whole in rows], [weight], "hidden_units_a_other")
            by_core.append(got[1:])
        first_rows = [[got[k][0] for got in by_core] for k in range(2)]
        others = hidden_others(rows, first_rows, "hidden_weights_a_other")
        received = [trade(other, "tp", j + 1) for j, other in enumerate(others)]
        return weights[1:], rows, first_rows, received

    other_weights, kept, first_rows, received = phase(always, first_phase)
    w_mlp = [[mlp_full[0]] + other_weights]
    mlp_sums = []
    if len(chunks) > 1:
        w_mlp.append(with_cores(after(mlp_full[1], *received)))
        mlp_sums.append(data_sum(hidden_own(kept, first_rows, received, "hidden_weights_a")))
    count = cores * len(chunks)
    both_cores = [w for pair in w_mlp for w in pair]

    def hidden_phase():
        rows = [first_rows]
        if len(chunks) > 1:
            wholes = [[whole] for whole in kept]
            rows.append(hidden_call(*wholes, w_mlp[1], "hidden_units_b")[1:])
        own, _, got = project_and_send(
            [grads for pair in rows for grads in pair[0]],
            both_cores,
            [0] * count,
            half,
            near_rows,
            "normed_mid_grad",
        )
        others = hidden_others(kept, after(rows[-1], own), "hidden_weights_b_other")
        return own, got, rows[-1], others, [acts for pair in rows for acts in pair[1]]

    mid_part, mid_got, last_rows, others, act_rows = phase(always, hidden_phase)

    def branch_phase():
        middle_grad, branch_own = rows_call(
            "back", mid_part, middle, mid_got, gain_mid, out_grad, [f32, bf16], "middle_grad"
        )
        down_parts = project(
            act_rows, both_cores, [2] * count, 0, [half] * model, near_rows, "hidden_out"
        )
        branch_blocks = spread(branch_own, *down_parts)
        received = [trade(other, "tp", j + 1) for j, other in enumerate(others)]
        last = after(last_rows, branch_own, *down_parts)
        total = hidden_own(kept, last, received, "hidden_weights_b")
        return middle_grad, branch_blocks, total, down_parts

    middle_grad, branch_blocks, total, down_parts = phase(always, branch_phase)
    mlp_sums.append(data_sum(total))
    down_got = [trade(down_parts[k], "model", k) for k in range(1, model)]

    def attend_back_phase():
        att_grads, rows = [], branch_blocks
        for j in reversed(range(cores)):
            branch, piece = rows_product(
                rows, None, w_attn[j], q_cols, o_place[j], near_rows, bf16, "attended_grad"
            )
            rows = [branch]
            piece = piece.reshape(model, half, q_cols)
            att_grads.insert(0, trade(piece, "tp", j) if j else piece)
        *qkv_back, head_grads = attention_call(
            functools.partial(attend_back_kernel, cores, kv_heads, repeat),
            "attend_back",
            core,
            raw + att_grads,
            shared,
            head_gains,
            [jax.ShapeDtypeStruct((model, half, cols), bf16)] * cores,
            [jax.ShapeDtypeStruct(head_gains.shape, f32)],
            [
                ((seq_len, cols), f32),
                ((seq_len, q_cols), bf16),
                ((seq_len, cols), f32),
                ((seq_len, cols), bf16),
            ],
        )
        return with_cores(branch), list(qkv_back), head_grads

    branch, qkv_back, head_grads = phase(always, attend_back_phase)
    tied = lax.optimization_barrier((qkv_back, mlp_sums[:-1], down_got))
    qkv_back, first_sums, down_got = tied
    first_got = [swap(rows_at(total.reshape(model, shard, -1))) for total in first_sums]

    def attention_weights_phase():
        back_pieces = [qkv_back[0]] + [trade(qkv_back[j], "tp", j) for j in range(1, cores)]
        ride = head_grads[:2].reshape(-1)
        ride = jnp.pad(ride, (0, ride_rows * wide - ride.shape[0])).astype(bf16)
        ride = jnp.pad(ride.reshape(ride_rows, wide), ((0, -ride_rows % 16), (0, 0)))
        groups = [
            [(normed_in[j], qkv_back[j].reshape(-1, cols)) for j in range(cores)],
            [(branch[j], attended[j].reshape(-1, q_cols)) for j in range(cores)],
        ]
        attn_total = weight_grad(groups, [], [ride], near_rows, "attention_weights")
        return attn_total, [piece.reshape(-1, cols) for piece in back_pieces]

    ride_rows = -(-2 * head_size // wide)
    attn_total, back_flat = phase(always, attention_weights_phase)
    attn_total, first_got = lax.optimization_barrier((attn_total, first_got))
    attn_sum = data_sum(attn_total)
    back_flat, last_sum = lax.optimization_barrier((back_flat, mlp_sums[-1]))

    def last_phase():
        own, in_far, in_got = project_and_send(
            back_flat, w_attn, [0] * cores, half, near_rows, "normed_in_grad"
        )
        hidden_out = rows_call(
            "sum", down_parts[0], middle, down_got, None, None, [bf16], "hidden_out_sum"
        )[0]
        last_got = swap(rows_at(after(last_sum.reshape(model, shard, -1), *in_far)))
        grad_in = rows_call(
            "back", own, hidden_in, in_got, gain_in, middle_grad, [f32], "grad_in"
        )[0]

        layout = [
            [(0, first, ff, size, False), (1, first, ff, size, False), (2, first, ff, size, True)]
            for first, size in zip(starts, chunks)
        ]
        shapes = [w_gate.shape, w_up.shape, w_down.shape]
        owned = owned_call(
            me, first_got + [last_got], layout, [w_gate, w_up], mlp_gain, shapes, "hidden_owned"
        )
        return hidden_out, grad_in, owned[:3], owned[3][:, 0]

    got = phase(always, last_phase)
    hidden_out, grad_in, (grad_gate, grad_up, grad_down), mlp_part = got
    attn_sum = after(attn_sum, grad_in)
    weight_rows = attn_sum[:near_rows].reshape(model, shard, wide)
    gain_row = attn_sum[near_rows:]
    gain_row = jnp.broadcast_to(gain_row, (model,) + gain_row.shape)
    attn_rows = jnp.concatenate([weight_rows, gain_row], axis=1)
    attn_got = swap(rows_at(attn_rows))
    layout = [
        [
            (0, 0, q_cols, q_cols, False),
            (1, 0, kv_cols, kv_cols, False),
            (2, 0, kv_cols, kv_cols, False),
            (3, 0, q_cols, q_cols, True),
        ]
    ]
    weights = [w_query, key_weight, value_weight]
    shapes = [weight.shape for weight in weights] + [w_output.shape]
    owned = owned_call(me, [attn_got], layout, weights, attn_gain, shapes, "attention_owned")
    grad_query, grad_key, grad_value, grad_output, attn_part, gain_sums = owned
    gain_sums = gain_sums[:ride_rows].reshape(-1)[: 2 * head_size]
    sums = lax.psum(jnp.concatenate([attn_part[:, 0], mlp_part, gain_sums]), "tp")
    where = lax.axis_index("data") * model + lax.axis_index("model")
    first = 2 * shard + where * part
    return (
        hidden_out,
        grad_in,
        grad_query,
        grad_key,
        grad_value,
        grad_output,
        grad_gate,
        grad_up,
        grad_down,
        sums[:shard],
        sums[shard : 2 * shard],
        lax.dynamic_slice_in_dim(sums, first, part),
        lax.dynamic_slice_in_dim(sums, first + head_size, part),
    )


def solution(mesh):
    fsdp, tp = mesh.shape["fsdp"], mesh.shape["tp"]
    model = 4 if fsdp % 4 == 0 else 1
    split = Mesh(mesh.devices.reshape(fsdp // model, model, tp), ("data", "model", "tp"))
    batch = ("data", "model")
    rows = P(("data", "model", "tp"), None)
    into = P(batch, "tp")
    back = P("tp", batch)
    in_specs = (rows, rows, P(batch), P(batch), into, into, into, back, into, into, back)
    in_specs = in_specs + (P(batch),) * 4
    out_specs = (rows, rows, into, into, into, back, into, into, back) + (P(batch),) * 4
    return jax.shard_map(
        on_device, mesh=split, in_specs=in_specs, out_specs=out_specs, check_vma=False
    )
```

```python
import functools

import jax
import jax.numpy as jnp
from jax import lax
from jax.experimental import pallas as pl
from jax.experimental.pallas import tpu as pltpu
from jax.sharding import Mesh, PartitionSpec as P

epsilon = 1e-06
rope_base = 1000000.0
bf16 = jnp.bfloat16
f32 = jnp.float32
BESIDE = pl.CostEstimate(flops=1 << 20, bytes_accessed=1 << 16, transcendentals=0)


def dot(left, right):
    return jnp.dot(left, right, preferred_element_type=f32)


def dot_right_t(left, right):
    return lax.dot_general(left, right, (((1,), (1,)), ((), ())), preferred_element_type=f32)


def dot_left_t(left, right):
    return lax.dot_general(left, right, (((0,), (0,)), ((), ())), preferred_element_type=f32)


def normalize(operand, norm_gain):
    return (
        operand
        * lax.rsqrt(jnp.mean(operand * operand, axis=-1, keepdims=True) + epsilon)
        * norm_gain
    )


def norm_back(operand, norm_gain, upstream):
    factor = lax.rsqrt(jnp.mean(operand * operand, axis=-1, keepdims=True) + epsilon)
    weighted = upstream * norm_gain
    inner = jnp.mean(weighted * operand, axis=-1, keepdims=True)
    return factor * weighted - operand * factor * factor * factor * inner


def tables(positions, head_size):
    indices = jnp.arange(head_size // 2).astype(f32)
    frequency = rope_base ** (-2.0 * indices / head_size)
    angles = positions.astype(f32)[..., None] * frequency
    cosine, sine = jnp.cos(angles), jnp.sin(angles)
    return (jnp.concatenate([cosine, cosine], -1), jnp.concatenate([-sine, sine], -1))


def half_turn(operand):
    return pltpu.roll(operand, operand.shape[-1] // 2, 1)


def lay_in_order(scratch, refs, core):
    half = refs[0].shape[1]
    for j, ref in enumerate(refs):
        scratch[pl.ds(pl.multiple_of((core ^ j) * half, half), half)] = ref[0]


def head_rows(raw, heads, repeat, gains, cosine, sine):
    size = gains.shape[1]

    def turned(column, gain):
        rows = normalize(raw[:, column * size : (column + 1) * size], gain)
        return (rows * cosine + half_turn(rows) * sine).astype(bf16)

    queries = [turned(h, gains[0:1]) for h in range(heads * repeat)]
    keys = [turned(heads * repeat + g, gains[1:2]) for g in range(heads)]
    first = heads * repeat + heads
    values = [
        raw[:, (first + g) * size : (first + g + 1) * size].astype(bf16) for g in range(heads)
    ]
    return queries, keys, values


def masked_probs(key, query, allowed):
    scores = dot_right_t(key, query) * query.shape[1] ** (-0.5)
    scores = jnp.where(allowed, scores, -1e30)
    exp_terms = jnp.exp(scores - jnp.max(scores, axis=0, keepdims=True))
    return exp_terms * (1.0 / jnp.sum(exp_terms, axis=0, keepdims=True))


def query_strips(rows, column_ref, row_ref):
    step = min(128, rows)
    for first in range(0, rows, step):
        seen = first + step
        keys = lax.broadcasted_iota(jnp.int32, (seen, step), 0)
        queries = lax.broadcasted_iota(jnp.int32, (seen, step), 1) + first
        same = column_ref[0, :seen, 0:1] == row_ref[0, 0:1, first:seen]
        yield slice(first, seen), seen, same & (keys <= queries)


def attend_kernel(cores, heads, repeat, core_ref, *refs):
    raws, refs = refs[:cores], refs[cores:]
    cos_ref, sin_ref, column_ref, row_ref, gain_ref = refs[:5]
    outs, raw, rows_out = refs[5:-2], refs[-2], refs[-1]
    core = core_ref[0]
    half = raws[0].shape[1]
    lay_in_order(raw, raws, core)
    queries, keys, values = head_rows(
        raw, heads, repeat, gain_ref[...], cos_ref[0], sin_ref[0]
    )
    size = gain_ref.shape[1]
    turned = [value.astype(f32).T.astype(bf16) for value in values]
    for at, seen, allowed in query_strips(raw.shape[0], column_ref, row_ref):
        for h, query in enumerate(queries):
            g = h // repeat
            probs = masked_probs(keys[g][:seen], query[at], allowed).astype(bf16)
            rows = dot(turned[g][:, :seen], probs).T
            rows_out[at, h * size : (h + 1) * size] = rows.astype(bf16)
    for j, out in enumerate(outs):
        out[0] = rows_out[pl.ds(pl.multiple_of((core ^ j) * half, half), half)]


def attend_back_kernel(cores, heads, repeat, core_ref, *refs):
    raws, grads, refs = refs[:cores], refs[cores : 2 * cores], refs[2 * cores :]
    cos_ref, sin_ref, column_ref, row_ref, gain_ref = refs[:5]
    outs, gain_out = refs[5 : 5 + cores], refs[5 + cores]
    raw, grad, totals, rows_out = refs[6 + cores :]
    core = core_ref[0]
    half = raws[0].shape[1]
    cosine, sine, gains = cos_ref[0], sin_ref[0], gain_ref[...]
    lay_in_order(raw, raws, core)
    lay_in_order(grad, grads, core)
    queries, keys, values = head_rows(raw, heads, repeat, gains, cosine, sine)
    size = gains.shape[1]
    scale = size ** (-0.5)
    count = heads * repeat

    @pl.when(pl.program_id(0) == 0)
    def _():
        gain_out[...] = jnp.zeros_like(gain_out)

    def columns(i):
        return slice(i * size, (i + 1) * size)

    turned_keys = [key.astype(f32).T.astype(bf16) for key in keys]
    totals[:, count * size :] = jnp.zeros_like(totals[:, count * size :])
    for at, seen, allowed in query_strips(raw.shape[0], column_ref, row_ref):
        for g in range(heads):
            key_grad = value_grad = None
            for h in range(g * repeat, (g + 1) * repeat):
                probs = masked_probs(keys[g][:seen], queries[h][at], allowed)
                out_grad = grad[at, columns(h)]
                prob_grad = dot_right_t(values[g][:seen], out_grad)
                delta = jnp.sum(probs * prob_grad, axis=0, keepdims=True)
                score_grad = (probs * (prob_grad - delta)).astype(bf16)
                totals[at, columns(h)] = dot(turned_keys[g][:, :seen], score_grad).T * scale
                key_part = dot(score_grad, queries[h][at])
                value_part = dot(probs.astype(bf16), out_grad)
                key_grad = key_part if key_grad is None else key_grad + key_part
                value_grad = value_part if value_grad is None else value_grad + value_part
            totals[:seen, columns(count + g)] += key_grad * scale
            totals[:seen, columns(count + heads + g)] += value_grad
    for i in range(count + heads):
        row = 0 if i < count else 1
        upstream = totals[:, columns(i)]
        turned = upstream * cosine - half_turn(upstream) * sine
        rows = raw[:, columns(i)]
        factor = lax.rsqrt(jnp.mean(rows * rows, axis=-1, keepdims=True) + epsilon)
        gain_out[row : row + 1] += jnp.sum(turned * rows * factor, axis=0, keepdims=True)
        back = norm_back(rows, gains[row : row + 1], turned)
        rows_out[:, columns(i)] = back.astype(bf16)
    rows_out[:, (count + heads) * size :] = totals[:, (count + heads) * size :].astype(bf16)
    for j, out in enumerate(outs):
        out[0] = rows_out[pl.ds(pl.multiple_of((core ^ j) * half, half), half)]


def attention_call(kernel, name, core, halves, shared, gains, outs, extra_out, scratch):
    def per_sequence(array):
        return pl.BlockSpec((1,) + array.shape[1:], lambda i: (i, 0, 0))

    whole = pl.BlockSpec(gains.shape, lambda i: (0, 0))
    out_specs = [per_sequence(shape) for shape in outs] + [
        pl.BlockSpec(shape.shape, lambda i: (0, 0)) for shape in extra_out
    ]
    return pl.pallas_call(
        kernel,
        grid=(halves[0].shape[0],),
        in_specs=[pl.BlockSpec(memory_space=pltpu.SMEM)]
        + [per_sequence(array) for array in halves + shared]
        + [whole],
        out_specs=out_specs,
        out_shape=outs + extra_out,
        scratch_shapes=[pltpu.VMEM(shape, dtype) for shape, dtype in scratch],
        compiler_params=pltpu.CompilerParams(vmem_limit_bytes=48 << 20),
        cost_estimate=BESIDE,
        name=name,
    )(core.reshape(1), *halves, *shared, gains)


def resident(shape):
    zeros = (0,) * len(shape)
    return pl.BlockSpec(shape, lambda i: zeros, pipeline_mode=pl.Buffered(1))


def project_kernel(count, *refs):
    lefts, rights, outs = refs[:count], refs[count : 2 * count], refs[2 * count :]
    total = dot_right_t(lefts[0][...], rights[0][0])
    for left, right in zip(lefts[1:], rights[1:]):
        total = total + dot_right_t(left[...], right[0])
    first = 0
    for out in outs:
        out[...] = total[first : first + out.shape[0]].astype(out.dtype)
        first += out.shape[0]


def project(lefts, rights, places, first, sizes, step, name):
    parts = rights[0].shape[0]
    rows = sum(sizes)

    def left_spec(left):
        return pl.BlockSpec(
            (rows, left.shape[1]), lambda i: (first // rows, 0), pipeline_mode=pl.Buffered(1)
        )

    def right_spec(left, place):
        return pl.BlockSpec((1, step, left.shape[1]), lambda i: (i, 0, place))

    return list(
        pl.pallas_call(
            functools.partial(project_kernel, len(lefts)),
            grid=(parts,),
            in_specs=[left_spec(left) for left in lefts]
            + [right_spec(left, place) for left, place in zip(lefts, places)],
            out_specs=[pl.BlockSpec((size, step), lambda i: (0, i)) for size in sizes],
            out_shape=[
                jax.ShapeDtypeStruct((size, parts * step), bf16 if first or k else f32)
                for k, size in enumerate(sizes)
            ],
            compiler_params=pltpu.CompilerParams(vmem_limit_bytes=56 << 20),
            cost_estimate=BESIDE,
            name=name,
        )(*lefts, *rights)
    )


def project_and_send(lefts, rights, places, rows, step, name):
    if lax.axis_size("model") == 1:
        return project(lefts, rights, places, 0, [rows], step, name)[0], [], []
    half = rows // 2
    far = project(lefts, rights, places, 3 * rows, [half] * 2, step, name + "_far")
    got = [trade(far[0], "model", 1), trade(far[1], "model", 2)]
    own, *near = project(lefts, rights, places, 0, [rows] + [half] * 4, step, name)
    return own, got, send_near(near, got)


def put_rows(whole, pieces, change):
    first = 0
    for piece in pieces:
        whole[first : first + piece.shape[0]] = change(piece[...])
        first += piece.shape[0]


def rows_kernel(kind, count, *refs):
    (own, base), got, refs = refs[:2], refs[2 : 2 + count], list(refs[2 + count :])
    total = own[...]
    if count == 4:
        upper = got[0][...].astype(f32) + got[1][...].astype(f32)
        lower = got[2][...].astype(f32) + got[3][...].astype(f32)
        total += jnp.where(pl.program_id(0) == 0, upper, lower)
    else:
        for piece in got:
            total += piece[...].astype(f32)
    rows = base[...].astype(f32)
    if kind == "sum":
        refs[0][...] = (rows + total).astype(bf16)
        return
    gain = refs[0][...]
    if kind == "norm":
        whole, *low = refs[1:]
        total = rows + total
        sent = normalize(total, gain)
    else:
        more, whole, *low = refs[1:]
        total = more[...].astype(f32) + norm_back(rows, gain, total)
        sent = total
    whole[...] = total
    for place, half in enumerate(low):

        @pl.when(pl.program_id(0) == place)
        def _():
            half[...] = sent.astype(bf16)


def rows_call(kind, own, base, got, gain, more, sent, name):
    rows, width = own.shape
    step = rows // 2
    strip = pl.BlockSpec((step, width), lambda i: (i, 0))
    half = resident((step, width))
    operands = [own, base] + list(got)
    in_specs = [strip, strip] + [half if len(got) == 4 else strip] * len(got)
    if gain is not None:
        operands.append(gain.reshape(1, width))
        in_specs.append(resident((1, width)))
    if more is not None:
        operands.append(more)
        in_specs.append(strip)
    out_specs, shapes = [strip], [jax.ShapeDtypeStruct((rows, width), bf16 if gain is None else f32)]
    if sent:
        out_specs += [half] * 2
        shapes += [jax.ShapeDtypeStruct((step, width), bf16)] * 2
    return list(
        pl.pallas_call(
            functools.partial(rows_kernel, kind, len(got)),
            grid=(2,),
            in_specs=in_specs,
            out_specs=out_specs,
            out_shape=shapes,
            compiler_params=pltpu.CompilerParams(vmem_limit_bytes=48 << 20),
            cost_estimate=BESIDE,
            name=name,
        )(*operands)
    )


def rows_product_kernel(count, normed, *refs):
    pieces, refs = refs[:count], list(refs[count:])
    gain = refs.pop(0)[...] if normed else None
    weight, out = refs[0], refs[-1]
    whole = pieces[0]
    if count > 1 or normed:
        whole = refs[1]

        def change(rows):
            return normalize(rows.astype(f32), gain).astype(bf16) if normed else rows

        put_rows(whole, pieces, change)
    columns = weight.shape[2]
    out[...] = dot(whole[...], weight[...].reshape(-1, columns)).astype(out.dtype)


def rows_product(pieces, gain, weight, block, place, step, dtype, name):
    rows = sum(piece.shape[0] for piece in pieces)
    parts, width = weight.shape[0], pieces[0].shape[1]
    joined = len(pieces) > 1 or gain is not None
    shapes = [jax.ShapeDtypeStruct((rows, width), bf16)] if joined else []
    shapes += [jax.ShapeDtypeStruct((rows, block), dtype)]
    gains = [] if gain is None else [gain.reshape(1, -1)]
    got = pl.pallas_call(
        functools.partial(rows_product_kernel, len(pieces), gain is not None),
        grid=(1,),
        in_specs=[resident(piece.shape) for piece in list(pieces) + gains]
        + [
            pl.BlockSpec(
                (parts, step, block), lambda i: (0, 0, place), pipeline_mode=pl.Buffered(1)
            )
        ],
        out_specs=[resident(shape.shape) for shape in shapes],
        out_shape=shapes,
        compiler_params=pltpu.CompilerParams(vmem_limit_bytes=56 << 20),
        cost_estimate=BESIDE,
        name=name,
    )(*pieces, *gains, weight)
    return (got[0], got[1]) if joined else (pieces[0], got[0])


def weight_grad_kernel(counts, number, *refs):
    count = sum(counts)
    lefts, rights, refs = refs[:count], refs[count : 2 * count], refs[2 * count :]
    received, below, out = refs[:number], refs[number:-1], refs[-1]
    rows = lefts[0].shape[1]
    first = pair = 0
    for size in counts:
        total = dot_left_t(lefts[pair][...], rights[pair][...])
        for i in range(pair + 1, pair + size):
            total = total + dot_left_t(lefts[i][...], rights[i][...])
        pair += size
        at = slice(first, first + total.shape[1])
        for block in received:
            total = total + block[0, :, at].astype(f32)
        out[0, :rows, at] = total.astype(bf16)
        first += total.shape[1]
    for block in below:
        out[0, rows:] = block[...]


def weight_grad(groups, received, below, step, name):
    pairs = [pair for group in groups for pair in group]
    rows, width = pairs[0][0].shape
    columns = sum(group[0][1].shape[1] for group in groups)
    deep = step + sum(block.shape[0] for block in below)
    return pl.pallas_call(
        functools.partial(
            weight_grad_kernel, [len(group) for group in groups], len(received)
        ),
        grid=(width // step,),
        in_specs=[pl.BlockSpec((rows, step), lambda i: (0, i))] * len(pairs)
        + [resident(right.shape) for _, right in pairs]
        + [pl.BlockSpec((1, step, columns), lambda i: (i, 0, 0))] * len(received)
        + [resident(block.shape) for block in below],
        out_specs=pl.BlockSpec((1, deep, columns), lambda i: (i, 0, 0)),
        out_shape=jax.ShapeDtypeStruct((width // step, deep, columns), bf16),
        compiler_params=pltpu.CompilerParams(vmem_limit_bytes=56 << 20),
        cost_estimate=BESIDE,
        name=name,
    )(*[left for left, _ in pairs], *[right for _, right in pairs], *received, *below)


def near_kernel(size, widths, me_ref, *refs):
    pieces, outs = refs[:size], refs[size:]
    rows = pieces[0].shape[0]
    for k, piece in enumerate(pieces):
        at = pl.ds(pl.multiple_of((me_ref[0] ^ k) * rows, rows), rows)
        first = 0
        for out, width in zip(outs, widths):
            out[at] = piece[:, first : first + width]
            first += width


def near_call(me, pieces, widths, name):
    rows = len(pieces) * pieces[0].shape[0]
    shapes = [jax.ShapeDtypeStruct((rows, width), bf16) for width in widths]
    return list(
        pl.pallas_call(
            functools.partial(near_kernel, len(pieces), widths),
            grid=(1,),
            in_specs=[pl.BlockSpec(memory_space=pltpu.SMEM)]
            + [resident(piece.shape) for piece in pieces],
            out_specs=[resident(shape.shape) for shape in shapes],
            out_shape=shapes,
            compiler_params=pltpu.CompilerParams(vmem_limit_bytes=32 << 20),
            cost_estimate=BESIDE,
            name=name,
        )(me.reshape(1), *pieces)
    )


def owned_kernel(size, layout, weighted, me_ref, *refs):
    count = size * len(layout)
    pieces, refs = refs[:count], refs[count:]
    weights, gain, refs = refs[:weighted], refs[weighted], refs[weighted + 1 :]
    outs, sums, below = refs[:-2], refs[-2], refs[-1]
    rows = gain.shape[0]
    total = jnp.zeros((rows, 1), f32)
    under = None
    for c, ranges in enumerate(layout):
        for k in range(size):
            piece = pieces[c * size + k]
            owner = me_ref[0] ^ k
            first = 0
            for number, place, wide, count, turned in ranges:
                block = piece[:rows, first : first + count].astype(f32)
                first += count
                at = pl.ds(pl.multiple_of(owner * wide + place, 128), count)
                if turned:
                    outs[number][at] = block.T
                    continue
                outs[number][:, at] = block
                if number < weighted:
                    product = weights[number][:, at].astype(f32) * block
                    total = total + jnp.sum(product, axis=1, keepdims=True)
            if piece.shape[0] > rows:
                more = piece[rows : rows + 8].astype(f32)
                under = more if under is None else under + more
    sums[...] = jnp.broadcast_to(total / gain[:, 0:1], sums.shape)
    below[...] = jnp.zeros_like(below) if under is None else under


def owned_call(me, chunks, layout, weights, gain, shapes, name):
    size = len(chunks[0])
    pieces = [piece for chunk in chunks for piece in chunk]
    rows = gain.shape[0]
    outs = [jax.ShapeDtypeStruct(shape, f32) for shape in shapes]
    outs += [jax.ShapeDtypeStruct((rows, 128), f32)]
    outs += [jax.ShapeDtypeStruct((8, pieces[0].shape[1]), f32)]
    column = jnp.broadcast_to(gain.astype(f32)[:, None], (rows, 128))
    operands = pieces + list(weights) + [column]
    return pl.pallas_call(
        functools.partial(owned_kernel, size, layout, len(weights)),
        grid=(1,),
        in_specs=[pl.BlockSpec(memory_space=pltpu.SMEM)]
        + [resident(array.shape) for array in operands],
        out_specs=[resident(shape.shape) for shape in outs],
        out_shape=outs,
        compiler_params=pltpu.CompilerParams(vmem_limit_bytes=48 << 20),
        cost_estimate=BESIDE,
        name=name,
    )(me.reshape(1), *operands)


def hidden_kernel(first, cores, x_count, g_count, tiles, *refs):
    refs = list(refs)

    def pop(number):
        taken, refs[:number] = refs[:number], []
        return taken

    x_pieces, g_pieces = (pop(x_count), pop(g_count)) if first else ([], [])
    x_all, g_all = (None, None) if first else pop(2)
    weights = [pop(3) for _ in range(cores)]
    if first:
        x_all, g_all = pop(2)
    grads_out, acts_out = pop(cores), pop(cores)
    step = pl.program_id(0)

    if first:

        @pl.when(step == 0)
        def _():
            put_rows(x_all, x_pieces, lambda rows: rows)
            put_rows(g_all, g_pieces, lambda rows: rows)

    def one_core(j):
        w_gate, w_up, w_down = (ref[...].reshape(-1, ref.shape[2]) for ref in weights[j])
        tile = w_gate.shape[1]
        place = step - j * tiles
        gate_place = pl.ds(pl.multiple_of(place * tile, tile), tile)
        up_place = pl.ds(pl.multiple_of((tiles + place) * tile, tile), tile)
        rows = x_all.shape[0] // 2
        for at in (slice(0, rows), slice(rows, None)):
            gate = dot(x_all[at], w_gate)
            up = dot(x_all[at], w_up)
            act_grad = dot(g_all[at], w_down)
            sigma = 1.0 / (1.0 + jnp.exp(-gate))
            silu = gate * sigma
            gate_grad = act_grad * up * sigma * (1.0 + gate * (1.0 - sigma))
            acts_out[j][at, gate_place] = (silu * up).astype(bf16)
            grads_out[j][at, gate_place] = gate_grad.astype(bf16)
            grads_out[j][at, up_place] = (act_grad * silu).astype(bf16)

    for j in range(cores):
        pl.when((step >= j * tiles) & (step < (j + 1) * tiles))(functools.partial(one_core, j))


def hidden_call(x_pieces, g_pieces, weights, name):
    cores, first = len(weights), len(x_pieces) > 1
    data, near, columns = weights[0].shape
    width = data * near
    units = columns // 3
    tile = min(256, units)
    tiles = units // tile
    rows = sum(piece.shape[0] for piece in x_pieces)

    def weight_specs(j):
        return [
            pl.BlockSpec(
                (data, near, tile),
                lambda i, k=k: (0, 0, k * tiles + jnp.clip(i - j * tiles, 0, tiles - 1)),
            )
            for k in range(3)
        ]

    operands = list(x_pieces) + list(g_pieces)
    in_specs = [resident(array.shape) for array in operands]
    for j, weight in enumerate(weights):
        in_specs += weight_specs(j)
        operands += [weight] * 3
    shapes = [jax.ShapeDtypeStruct((rows, width), bf16)] * 2 if first else []
    shapes += [jax.ShapeDtypeStruct((rows, 2 * units), bf16)] * cores
    shapes += [jax.ShapeDtypeStruct((rows, units), bf16)] * cores
    got = pl.pallas_call(
        functools.partial(
            hidden_kernel, first, cores, len(x_pieces), len(g_pieces), tiles
        ),
        grid=(cores * tiles,),
        in_specs=in_specs,
        out_specs=[resident(shape.shape) for shape in shapes],
        out_shape=shapes,
        compiler_params=pltpu.CompilerParams(vmem_limit_bytes=60 << 20),
        cost_estimate=BESIDE,
        name=name,
    )(*operands)
    got = list(got)
    kept, got = (got[:2], got[2:]) if first else ([x_pieces[0], g_pieces[0]], got)
    return kept, got[:cores], got[cores:]


def phase(always, body):
    def never():
        return jax.tree.map(lambda leaf: jnp.zeros(leaf.shape, leaf.dtype), jax.eval_shape(body))

    return lax.cond(always, body, never)


def trade(block, axis, step):
    return lax.ppermute(block, axis, [(i, i ^ step) for i in range(lax.axis_size(axis))])


def halves(rows):
    middle = rows.shape[0] // 2
    return [rows[:middle], rows[middle:]]


def spread_near(own):
    if lax.axis_size("model") == 1:
        return list(own)
    return list(own) + [trade(half, "model", k) for k in (1, 2) for half in own]


def spread_far(near, *first):
    if len(near) == 2:
        return []
    upper, lower = near[2], near[5]
    if first:
        upper, lower = after((upper, lower), *first)
    return [trade(upper, "model", 2), trade(lower, "model", 1)]


def send_near(near, far):
    x_upper, x_lower, y_upper, y_lower = near
    x_upper, y_lower = after((x_upper, y_lower), *far)
    y_upper = (y_upper.astype(f32) + far[0].astype(f32)).astype(bf16)
    x_lower = (x_lower.astype(f32) + far[1].astype(f32)).astype(bf16)
    return [
        trade(x_upper, "model", 1),
        trade(y_upper, "model", 2),
        trade(x_lower, "model", 1),
        trade(y_lower, "model", 2),
    ]


def swap(piece_of):
    me = lax.axis_index("model")
    others = range(1, lax.axis_size("model"))
    return [piece_of(me)] + [trade(piece_of(me ^ k), "model", k) for k in others]


def take(array, index, count):
    size = array.shape[1] // count
    return lax.dynamic_slice_in_dim(array, index * size, size, 1)


def rows_at(array):
    return lambda i: lax.dynamic_index_in_dim(array, i, 0, keepdims=False)


def in_order(pieces):
    me = lax.axis_index("model")
    size = len(pieces)
    return jnp.stack(
        [lax.select_n(me, *[pieces[j ^ i] for j in range(size)]) for i in range(size)]
    )


def after(value, *first):
    return lax.optimization_barrier((value,) + first)[0]


def on_device(
    hidden_in,
    out_grad,
    segments,
    positions,
    w_query,
    key_weight,
    value_weight,
    w_output,
    w_gate,
    w_up,
    w_down,
    attn_gain,
    mlp_gain,
    query_gain,
    key_gain,
):
    data = lax.axis_size("data")
    model = lax.axis_size("model")
    cores = lax.axis_size("tp")
    core = lax.axis_index("tp")
    seq_len = positions.shape[0]
    half = seq_len // cores
    shard = w_query.shape[0]
    width = hidden_in.shape[1]
    head_size = query_gain.shape[0] * data * model
    q_heads = w_query.shape[1] // model // head_size
    kv_heads = key_weight.shape[1] // model // head_size
    repeat = q_heads // kv_heads
    q_cols = q_heads * head_size
    kv_cols = kv_heads * head_size
    cols = q_cols + 2 * kv_cols
    wide = cols + q_cols
    ff = w_gate.shape[1] // model
    always = (segments[0] * segments[0] + segments[0]) % 2 == 0

    small = jnp.concatenate([attn_gain, mlp_gain, query_gain, key_gain])
    small_rows = -(-small.shape[0] // wide)
    place_rows = -(-seq_len // wide)

    def as_rows(vector, rows):
        return jnp.pad(vector, (0, rows * wide - vector.shape[0])).reshape(rows, wide)

    extra = jnp.concatenate(
        [
            as_rows(small, small_rows),
            as_rows(segments.astype(bf16), place_rows),
            as_rows((positions // 8).astype(bf16), place_rows),
            as_rows((positions % 8).astype(bf16), place_rows),
        ]
    )
    extra = jnp.pad(extra, ((0, -extra.shape[0] % 16), (0, 0)))
    turned_output = w_output.T

    def attn_piece(i):
        parts = [
            take(w_query, i, model),
            take(key_weight, i, model),
            take(value_weight, i, model),
            take(turned_output, i, model),
        ]
        return jnp.concatenate([jnp.concatenate(parts, axis=1), extra])

    turned_down = w_down.T
    chunks = [ff - ff // 3, ff // 3] if ff % 768 == 0 else [ff]
    starts = [sum(chunks[:c]) for c in range(len(chunks))]

    def over_data(pieces):
        return lax.all_gather(pieces, "data", axis=0, tiled=False)

    attn_got = swap(attn_piece)
    x_near = spread_near(lax.optimization_barrier((halves(hidden_in), attn_got))[0])
    tied = lax.optimization_barrier((w_gate, w_up, turned_down, x_near))
    w_gate_sent, w_up_sent, turned_down, x_near = tied
    x_blocks = x_near + spread_far(x_near)
    mlp_got = swap(
        lambda i: jnp.concatenate(
            [
                take(weight, i, model)[:, first : first + count]
                for first, count in zip(starts, chunks)
                for weight in (w_gate_sent, w_up_sent, turned_down)
            ],
            axis=1,
        )
    )

    def places_of(first):
        rows = [
            got[shard + first : shard + first + place_rows].reshape(-1)[:seq_len]
            for got in attn_got
        ]
        return jnp.stack(rows).astype(f32)

    seg_all = places_of(small_rows)
    pos_all = 8.0 * places_of(small_rows + place_rows) + places_of(small_rows + 2 * place_rows)
    cosine, sine = tables(pos_all, head_size)

    attn_near = in_order(attn_got)
    gain_rows = attn_near[:, shard : shard + small_rows].reshape(-1, wide)
    gain_rows = jnp.pad(gain_rows, ((0, -gain_rows.shape[0] % 16), (0, 0)))
    near = jnp.concatenate([attn_near[:, :shard].reshape(-1, wide), gain_rows])
    me = lax.axis_index("model")
    mlp_near = near_call(me, mlp_got, [3 * count for count in chunks], "hidden_exchange")
    attn_full = over_data(near)
    tied = lax.optimization_barrier((attn_full, mlp_near, x_blocks, cosine, sine))
    attn_full, mlp_near, x_blocks, cosine, sine = tied
    mlp_full = [over_data(piece) for piece in mlp_near]

    gains = attn_full[:, model * shard : model * shard + model * small_rows]
    gains = gains.reshape(data * model, -1).astype(f32)
    part = query_gain.shape[0]
    gain_in = gains[:, :shard].reshape(-1)
    gain_mid = gains[:, shard : 2 * shard].reshape(-1)
    gain_query = gains[:, 2 * shard : 2 * shard + part].reshape(-1)
    gain_key = gains[:, 2 * shard + part : 2 * shard + 2 * part].reshape(-1)
    def with_cores(weight):
        return [weight] + [trade(weight, "tp", j) for j in range(1, cores)]

    near_rows = model * shard
    grad_near = spread_near(after(halves(out_grad), *x_blocks, *mlp_near))

    seg_rows = jnp.pad(seg_all[:, None], ((0, 0), (0, 7), (0, 0)))
    seg_columns = seg_all[:, :, None]
    head_gains = jnp.pad(jnp.stack([gain_query, gain_key]), ((0, 6), (0, 0)))
    shared = [cosine, sine, seg_columns, seg_rows]
    o_place = [cols // q_cols] * cores

    def product_phase():
        w_attn = with_cores(attn_full)
        normed_in, first_raw = rows_product(
            x_blocks, gain_in, w_attn[0], cols, 0, near_rows, f32, "query_key_value"
        )
        raw = [first_raw.reshape(model, half, cols)]
        for j in range(1, cores):
            mine = rows_product(
                [normed_in], None, w_attn[j], cols, 0, near_rows, f32, "query_key_value_other"
            )[1]
            raw.append(trade(mine, "tp", j).reshape(model, half, cols))
        return w_attn[1:], normed_in, raw

    w_others, own_normed, raw = phase(always, product_phase)
    w_attn = [attn_full] + w_others
    raw, grad_near = lax.optimization_barrier((raw, grad_near))

    def attention_phase():
        far = spread_far(grad_near)
        attended = attention_call(
            functools.partial(attend_kernel, cores, kv_heads, repeat),
            "attend",
            core,
            raw,
            shared,
            head_gains,
            [jax.ShapeDtypeStruct((model, half, q_cols), bf16)] * cores,
            [],
            [((seq_len, cols), f32), ((seq_len, q_cols), bf16)],
        )
        attended, far = lax.optimization_barrier((list(attended), far))
        att_pieces = [attended[0]] + [trade(attended[j], "tp", j) for j in range(1, cores)]
        att_flat = [piece.reshape(-1, q_cols) for piece in att_pieces]
        return with_cores(own_normed)[1:], att_flat, attended, far

    normed_others, att_flat, attended, grad_far = phase(always, attention_phase)
    normed_in = [own_normed] + normed_others
    grad_blocks = grad_near + grad_far

    def data_sum(total):
        return lax.psum_scatter(total, "data", scatter_dimension=0, tiled=False)

    def out_phase():
        own, _, got = project_and_send(
            att_flat, w_attn, o_place, half, near_rows, "attention_out"
        )
        middle, *low = rows_call("norm", own, hidden_in, got, gain_mid, None, True, "middle")
        near = spread_near(low)
        return middle, near + spread_far(near)

    middle, mid_blocks = phase(always, out_phase)

    def for_own_core(rows):
        return [
            [rows[k][0]] + [trade(rows[k][j], "tp", j) for j in range(1, cores)] for k in range(2)
        ]

    def hidden_weights(kept, rows, name):
        groups = [[(kept[k][j], rows[k][j]) for j in range(cores)] for k in range(2)]
        return weight_grad(groups, [], (), near_rows, name)

    def first_phase():
        weights = with_cores(mlp_full[0])
        rows, *by_core = hidden_call(mid_blocks, grad_blocks, weights[:1], "hidden_units_a")
        kept = [with_cores(whole) for whole in rows]
        by_core = [by_core]
        for weight in weights[1:]:
            got = hidden_call(*[[whole] for whole in rows], [weight], "hidden_units_a_other")
            by_core.append(got[1:])
        first_rows = [[got[k][0] for got in by_core] for k in range(2)]
        total = hidden_weights(kept, for_own_core(first_rows), "hidden_weights_a")
        return weights[1:], kept, first_rows, total

    other_weights, kept, first_rows, total = phase(always, first_phase)
    w_mlp = [[mlp_full[0]] + other_weights]
    wholes = [[kept[k][0]] for k in range(2)]
    mlp_sums = []
    if len(chunks) > 1:
        mlp_sums.append(data_sum(total))
    count = cores * len(chunks)

    def hidden_phase():
        rows, weights = [first_rows], list(w_mlp)
        if len(chunks) > 1:
            weights.append(with_cores(mlp_full[1]))
            by_core = [
                hidden_call(*wholes, [weight], "hidden_units_b")[1:] for weight in weights[1]
            ]
            rows.append([[got[k][0] for got in by_core] for k in range(2)])
        both_cores = [w for pair in weights for w in pair]
        own, _, got = project_and_send(
            [grads for pair in rows for grads in pair[0]],
            both_cores,
            [0] * count,
            half,
            near_rows,
            "normed_mid_grad",
        )
        last_rows = after(for_own_core(rows[-1]), own)
        total = hidden_weights(kept, last_rows, "hidden_weights_b")
        acts = [acts for pair in rows for acts in pair[1]]
        return own, got, total, acts, [w for pair in weights[1:] for w in pair[1:]]

    mid_part, mid_got, total, act_rows, other_weights = phase(always, hidden_phase)
    if len(chunks) > 1:
        mlp_sums.append(data_sum(total))
        w_mlp.append([mlp_full[1]] + other_weights)
    both_cores = [w for pair in w_mlp for w in pair]

    def branch_phase():
        middle_grad, *low = rows_call(
            "back", mid_part, middle, mid_got, gain_mid, out_grad, True, "middle_grad"
        )
        down_parts = project(
            act_rows, both_cores, [2] * count, 0, [half] * model, near_rows, "hidden_out"
        )
        near = spread_near(low)
        branch_blocks = near + spread_far(near, *down_parts)
        return middle_grad, branch_blocks, down_parts

    middle_grad, branch_blocks, down_parts = phase(always, branch_phase)
    down_got = [trade(down_parts[k], "model", k) for k in range(1, model)]

    def attend_back_phase():
        att_grads, rows = [], branch_blocks
        for j in reversed(range(cores)):
            branch, piece = rows_product(
                rows, None, w_attn[j], q_cols, o_place[j], near_rows, bf16, "attended_grad"
            )
            rows = [branch]
            piece = piece.reshape(model, half, q_cols)
            att_grads.insert(0, trade(piece, "tp", j) if j else piece)
        *qkv_back, head_grads = attention_call(
            functools.partial(attend_back_kernel, cores, kv_heads, repeat),
            "attend_back",
            core,
            raw + att_grads,
            shared,
            head_gains,
            [jax.ShapeDtypeStruct((model, half, cols), bf16)] * cores,
            [jax.ShapeDtypeStruct(head_gains.shape, f32)],
            [
                ((seq_len, cols), f32),
                ((seq_len, q_cols), bf16),
                ((seq_len, cols), f32),
                ((seq_len, cols), bf16),
            ],
        )
        return with_cores(branch), list(qkv_back), head_grads

    branch, qkv_back, head_grads = phase(always, attend_back_phase)

    def attention_weights_phase():
        back_pieces = [qkv_back[0]] + [trade(qkv_back[j], "tp", j) for j in range(1, cores)]
        ride = head_grads[:2].reshape(-1)
        ride = jnp.pad(ride, (0, ride_rows * wide - ride.shape[0])).astype(bf16)
        ride = jnp.pad(ride.reshape(ride_rows, wide), ((0, -ride_rows % 16), (0, 0)))
        groups = [
            [(normed_in[j], qkv_back[j].reshape(-1, cols)) for j in range(cores)],
            [(branch[j], attended[j].reshape(-1, q_cols)) for j in range(cores)],
        ]
        attn_total = weight_grad(groups, [], [ride], near_rows, "attention_weights")
        return attn_total, [piece.reshape(-1, cols) for piece in back_pieces]

    ride_rows = -(-2 * head_size // wide)
    attn_total, back_flat = phase(always, attention_weights_phase)
    attn_total, down_got = lax.optimization_barrier((attn_total, down_got))
    attn_sum = data_sum(attn_total)
    back_flat, first_sums = lax.optimization_barrier((back_flat, mlp_sums[:-1]))

    def exchanged(total):
        return swap(rows_at(total.reshape(model, shard, -1)))

    def in_grad_phase():
        own, _, got = project_and_send(
            back_flat, w_attn, [0] * cores, half, near_rows, "normed_in_grad"
        )
        return own, got, [exchanged(total) for total in first_sums]

    in_part, in_got, first_got = phase(always, in_grad_phase)
    in_got, last_sum = lax.optimization_barrier((in_got, mlp_sums[-1]))

    def last_phase():
        last_got = exchanged(last_sum)
        hidden_out = rows_call(
            "sum", down_parts[0], middle, down_got, None, None, False, "hidden_out_sum"
        )[0]
        grad_in = rows_call(
            "back", in_part, hidden_in, in_got, gain_in, middle_grad, False, "grad_in"
        )[0]
        layout = [
            [(kind, first, ff, size, kind == 2) for kind in range(3)]
            for first, size in zip(starts, chunks)
        ]
        shapes = [w_gate.shape, w_up.shape, w_down.shape]
        owned = owned_call(
            me, first_got + [last_got], layout, [w_gate, w_up], mlp_gain, shapes, "hidden_owned"
        )
        return hidden_out, grad_in, owned[:3], owned[3][:, 0]

    got = phase(always, last_phase)
    hidden_out, grad_in, (grad_gate, grad_up, grad_down), mlp_part = got
    attn_sum = after(attn_sum, grad_in)
    weight_rows = attn_sum[:near_rows].reshape(model, shard, wide)
    gain_row = attn_sum[near_rows:]
    gain_row = jnp.broadcast_to(gain_row, (model,) + gain_row.shape)
    attn_rows = jnp.concatenate([weight_rows, gain_row], axis=1)
    attn_got = swap(rows_at(attn_rows))
    layout = [
        [
            (0, 0, q_cols, q_cols, False),
            (1, 0, kv_cols, kv_cols, False),
            (2, 0, kv_cols, kv_cols, False),
            (3, 0, q_cols, q_cols, True),
        ]
    ]
    weights = [w_query, key_weight, value_weight]
    shapes = [weight.shape for weight in weights] + [w_output.shape]
    owned = owned_call(me, [attn_got], layout, weights, attn_gain, shapes, "attention_owned")
    grad_query, grad_key, grad_value, grad_output, attn_part, gain_sums = owned
    gain_sums = gain_sums[:ride_rows].reshape(-1)[: 2 * head_size]
    sums = lax.psum(jnp.concatenate([attn_part[:, 0], mlp_part, gain_sums]), "tp")
    where = lax.axis_index("data") * model + lax.axis_index("model")
    first = 2 * shard + where * part
    return (
        hidden_out,
        grad_in,
        grad_query,
        grad_key,
        grad_value,
        grad_output,
        grad_gate,
        grad_up,
        grad_down,
        sums[:shard],
        sums[shard : 2 * shard],
        lax.dynamic_slice_in_dim(sums, first, part),
        lax.dynamic_slice_in_dim(sums, first + head_size, part),
    )


def solution(mesh):
    fsdp, tp = mesh.shape["fsdp"], mesh.shape["tp"]
    model = 4 if fsdp % 4 == 0 else 1
    split = Mesh(mesh.devices.reshape(fsdp // model, model, tp), ("data", "model", "tp"))
    batch = ("data", "model")
    rows = P(("data", "model", "tp"), None)
    into = P(batch, "tp")
    back = P("tp", batch)
    in_specs = (rows, rows, P(batch), P(batch), into, into, into, back, into, into, back)
    in_specs = in_specs + (P(batch),) * 4
    out_specs = (rows, rows, into, into, into, back, into, into, back) + (P(batch),) * 4
    return jax.shard_map(
        on_device, mesh=split, in_specs=in_specs, out_specs=out_specs, check_vma=False
    )
```

```python
import functools

import jax
import jax.numpy as jnp
from jax import lax
from jax.experimental import pallas as pl
from jax.experimental.pallas import tpu as pltpu
from jax.sharding import Mesh, PartitionSpec as P

epsilon = 1e-06
rope_base = 1000000.0
bf16 = jnp.bfloat16
f32 = jnp.float32
BESIDE = pl.CostEstimate(flops=1 << 20, bytes_accessed=1 << 16, transcendentals=0)


def dot(left, right):
    return jnp.dot(left, right, preferred_element_type=f32)


def dot_right_t(left, right):
    return lax.dot_general(left, right, (((1,), (1,)), ((), ())), preferred_element_type=f32)


def dot_left_t(left, right):
    return lax.dot_general(left, right, (((0,), (0,)), ((), ())), preferred_element_type=f32)


def normalize(operand, norm_gain):
    return (
        operand
        * lax.rsqrt(jnp.mean(operand * operand, axis=-1, keepdims=True) + epsilon)
        * norm_gain
    )


def norm_back(operand, norm_gain, upstream):
    factor = lax.rsqrt(jnp.mean(operand * operand, axis=-1, keepdims=True) + epsilon)
    weighted = upstream * norm_gain
    inner = jnp.mean(weighted * operand, axis=-1, keepdims=True)
    return factor * weighted - operand * factor * factor * factor * inner


def tables(positions, head_size):
    indices = jnp.arange(head_size // 2).astype(f32)
    frequency = rope_base ** (-2.0 * indices / head_size)
    angles = positions.astype(f32)[..., None] * frequency
    cosine, sine = jnp.cos(angles), jnp.sin(angles)
    return (jnp.concatenate([cosine, cosine], -1), jnp.concatenate([-sine, sine], -1))


def half_turn(operand):
    return pltpu.roll(operand, operand.shape[-1] // 2, 1)


def lay_in_order(scratch, refs, core):
    half = refs[0].shape[1]
    for j, ref in enumerate(refs):
        scratch[pl.ds(pl.multiple_of((core ^ j) * half, half), half)] = ref[0]


def head_rows(raw, heads, repeat, gains, cosine, sine):
    size = gains.shape[1]

    def turned(column, gain):
        rows = normalize(raw[:, column * size : (column + 1) * size], gain)
        return (rows * cosine + half_turn(rows) * sine).astype(bf16)

    queries = [turned(h, gains[0:1]) for h in range(heads * repeat)]
    keys = [turned(heads * repeat + g, gains[1:2]) for g in range(heads)]
    first = heads * repeat + heads
    values = [
        raw[:, (first + g) * size : (first + g + 1) * size].astype(bf16) for g in range(heads)
    ]
    return queries, keys, values


def masked_probs(key, query, allowed):
    scores = dot_right_t(key, query) * query.shape[1] ** (-0.5)
    scores = jnp.where(allowed, scores, -1e30)
    exp_terms = jnp.exp(scores - jnp.max(scores, axis=0, keepdims=True))
    return exp_terms * (1.0 / jnp.sum(exp_terms, axis=0, keepdims=True))


def query_strips(rows, column_ref, row_ref):
    step = min(256, rows)
    for first in range(0, rows, step):
        seen = first + step
        keys = lax.broadcasted_iota(jnp.int32, (seen, step), 0)
        queries = lax.broadcasted_iota(jnp.int32, (seen, step), 1) + first
        same = column_ref[0, :seen, 0:1] == row_ref[0, 0:1, first:seen]
        yield slice(first, seen), seen, same & (keys <= queries)


def attend_kernel(cores, heads, repeat, core_ref, *refs):
    raws, refs = refs[:cores], refs[cores:]
    cos_ref, sin_ref, column_ref, row_ref, gain_ref = refs[:5]
    outs, raw, rows_out = refs[5:-2], refs[-2], refs[-1]
    core = core_ref[0]
    half = raws[0].shape[1]
    lay_in_order(raw, raws, core)
    queries, keys, values = head_rows(
        raw, heads, repeat, gain_ref[...], cos_ref[0], sin_ref[0]
    )
    size = gain_ref.shape[1]
    turned = [value.astype(f32).T.astype(bf16) for value in values]
    for at, seen, allowed in query_strips(raw.shape[0], column_ref, row_ref):
        for h, query in enumerate(queries):
            g = h // repeat
            probs = masked_probs(keys[g][:seen], query[at], allowed).astype(bf16)
            rows = dot(turned[g][:, :seen], probs).T
            rows_out[at, h * size : (h + 1) * size] = rows.astype(bf16)
    for j, out in enumerate(outs):
        out[0] = rows_out[pl.ds(pl.multiple_of((core ^ j) * half, half), half)]


def attend_back_kernel(cores, heads, repeat, core_ref, *refs):
    raws, grads, refs = refs[:cores], refs[cores : 2 * cores], refs[2 * cores :]
    cos_ref, sin_ref, column_ref, row_ref, gain_ref = refs[:5]
    outs, gain_out = refs[5 : 5 + cores], refs[5 + cores]
    raw, grad, totals, rows_out = refs[6 + cores :]
    core = core_ref[0]
    half = raws[0].shape[1]
    cosine, sine, gains = cos_ref[0], sin_ref[0], gain_ref[...]
    lay_in_order(raw, raws, core)
    lay_in_order(grad, grads, core)
    queries, keys, values = head_rows(raw, heads, repeat, gains, cosine, sine)
    size = gains.shape[1]
    scale = size ** (-0.5)
    count = heads * repeat

    @pl.when(pl.program_id(0) == 0)
    def _():
        gain_out[...] = jnp.zeros_like(gain_out)

    def columns(i):
        return slice(i * size, (i + 1) * size)

    turned_keys = [key.astype(f32).T.astype(bf16) for key in keys]
    totals[:, count * size :] = jnp.zeros_like(totals[:, count * size :])
    for at, seen, allowed in query_strips(raw.shape[0], column_ref, row_ref):
        for g in range(heads):
            key_grad = value_grad = None
            for h in range(g * repeat, (g + 1) * repeat):
                probs = masked_probs(keys[g][:seen], queries[h][at], allowed)
                out_grad = grad[at, columns(h)]
                prob_grad = dot_right_t(values[g][:seen], out_grad)
                delta = jnp.sum(probs * prob_grad, axis=0, keepdims=True)
                score_grad = (probs * (prob_grad - delta)).astype(bf16)
                totals[at, columns(h)] = dot(turned_keys[g][:, :seen], score_grad).T * scale
                key_part = dot(score_grad, queries[h][at])
                value_part = dot(probs.astype(bf16), out_grad)
                key_grad = key_part if key_grad is None else key_grad + key_part
                value_grad = value_part if value_grad is None else value_grad + value_part
            totals[:seen, columns(count + g)] += key_grad * scale
            totals[:seen, columns(count + heads + g)] += value_grad
    for i in range(count + heads):
        row = 0 if i < count else 1
        upstream = totals[:, columns(i)]
        turned = upstream * cosine - half_turn(upstream) * sine
        rows = raw[:, columns(i)]
        factor = lax.rsqrt(jnp.mean(rows * rows, axis=-1, keepdims=True) + epsilon)
        gain_out[row : row + 1] += jnp.sum(turned * rows * factor, axis=0, keepdims=True)
        back = norm_back(rows, gains[row : row + 1], turned)
        rows_out[:, columns(i)] = back.astype(bf16)
    rows_out[:, (count + heads) * size :] = totals[:, (count + heads) * size :].astype(bf16)
    for j, out in enumerate(outs):
        out[0] = rows_out[pl.ds(pl.multiple_of((core ^ j) * half, half), half)]


def attention_call(kernel, name, core, halves, shared, gains, outs, extra_out, scratch):
    def per_sequence(array):
        return pl.BlockSpec((1,) + array.shape[1:], lambda i: (i, 0, 0))

    whole = pl.BlockSpec(gains.shape, lambda i: (0, 0))
    out_specs = [per_sequence(shape) for shape in outs] + [
        pl.BlockSpec(shape.shape, lambda i: (0, 0)) for shape in extra_out
    ]
    return pl.pallas_call(
        kernel,
        grid=(halves[0].shape[0],),
        in_specs=[pl.BlockSpec(memory_space=pltpu.SMEM)]
        + [per_sequence(array) for array in halves + shared]
        + [whole],
        out_specs=out_specs,
        out_shape=outs + extra_out,
        scratch_shapes=[pltpu.VMEM(shape, dtype) for shape, dtype in scratch],
        compiler_params=pltpu.CompilerParams(vmem_limit_bytes=48 << 20),
        cost_estimate=BESIDE,
        name=name,
    )(core.reshape(1), *halves, *shared, gains)


def resident(shape):
    zeros = (0,) * len(shape)
    return pl.BlockSpec(shape, lambda i: zeros, pipeline_mode=pl.Buffered(1))


def project_kernel(count, few, *refs):
    lefts, rights, outs = refs[:count], refs[count : 2 * count], refs[2 * count :]

    def product(left, right):
        return dot_right_t(right[0], left[...]) if few else dot_right_t(left[...], right[0])

    total = product(lefts[0], rights[0])
    for left, right in zip(lefts[1:], rights[1:]):
        total = total + product(left, right)
    total = total.T if few else total
    first = 0
    for out in outs:
        out[...] = total[first : first + out.shape[0]].astype(out.dtype)
        first += out.shape[0]


def project(lefts, rights, places, first, sizes, step, name):
    parts = rights[0].shape[0]
    rows = sum(sizes)

    def left_spec(left):
        return pl.BlockSpec(
            (rows, left.shape[1]), lambda i: (first // rows, 0), pipeline_mode=pl.Buffered(1)
        )

    def right_spec(left, place):
        return pl.BlockSpec((1, step, left.shape[1]), lambda i: (i, 0, place))

    return list(
        pl.pallas_call(
            functools.partial(project_kernel, len(lefts), bool(first)),
            grid=(parts,),
            in_specs=[left_spec(left) for left in lefts]
            + [right_spec(left, place) for left, place in zip(lefts, places)],
            out_specs=[pl.BlockSpec((size, step), lambda i: (0, i)) for size in sizes],
            out_shape=[
                jax.ShapeDtypeStruct((size, parts * step), bf16 if first or k else f32)
                for k, size in enumerate(sizes)
            ],
            compiler_params=pltpu.CompilerParams(vmem_limit_bytes=56 << 20),
            cost_estimate=BESIDE,
            name=name,
        )(*lefts, *rights)
    )


def project_and_send(lefts, rights, places, rows, step, name):
    if lax.axis_size("model") == 1:
        return project(lefts, rights, places, 0, [rows], step, name)[0], [], []
    half = rows // 2
    far = project(lefts, rights, places, 3 * rows, [half] * 2, step, name + "_far")
    got = [trade(far[0], "model", 1), trade(far[1], "model", 2)]
    own, *near = project(lefts, rights, places, 0, [rows] + [half] * 4, step, name)
    return own, got, send_near(near, got)


def put_rows(whole, pieces, change):
    first = 0
    for piece in pieces:
        whole[first : first + piece.shape[0]] = change(piece[...])
        first += piece.shape[0]


def rows_kernel(kind, count, *refs):
    (own, base), got, refs = refs[:2], refs[2 : 2 + count], list(refs[2 + count :])
    total = own[...]
    if count == 4:
        upper = got[0][...].astype(f32) + got[1][...].astype(f32)
        lower = got[2][...].astype(f32) + got[3][...].astype(f32)
        total += jnp.where(pl.program_id(0) == 0, upper, lower)
    else:
        for piece in got:
            total += piece[...].astype(f32)
    rows = base[...].astype(f32)
    if kind == "sum":
        refs[0][...] = (rows + total).astype(bf16)
        return
    gain = refs[0][...]
    if kind == "norm":
        whole, *low = refs[1:]
        total = rows + total
        sent = normalize(total, gain)
    else:
        more, whole, *low = refs[1:]
        total = more[...].astype(f32) + norm_back(rows, gain, total)
        sent = total
    whole[...] = total
    for place, half in enumerate(low):

        @pl.when(pl.program_id(0) == place)
        def _():
            half[...] = sent.astype(bf16)


def rows_call(kind, own, base, got, gain, more, sent, name):
    rows, width = own.shape
    step = rows // 2
    strip = pl.BlockSpec((step, width), lambda i: (i, 0))
    half = resident((step, width))
    operands = [own, base] + list(got)
    in_specs = [strip, strip] + [half if len(got) == 4 else strip] * len(got)
    if gain is not None:
        operands.append(gain.reshape(1, width))
        in_specs.append(resident((1, width)))
    if more is not None:
        operands.append(more)
        in_specs.append(strip)
    out_specs, shapes = [strip], [jax.ShapeDtypeStruct((rows, width), bf16 if gain is None else f32)]
    if sent:
        out_specs += [half] * 2
        shapes += [jax.ShapeDtypeStruct((step, width), bf16)] * 2
    return list(
        pl.pallas_call(
            functools.partial(rows_kernel, kind, len(got)),
            grid=(2,),
            in_specs=in_specs,
            out_specs=out_specs,
            out_shape=shapes,
            compiler_params=pltpu.CompilerParams(vmem_limit_bytes=48 << 20),
            cost_estimate=BESIDE,
            name=name,
        )(*operands)
    )


def rows_product_kernel(count, normed, number, *refs):
    pieces, refs = refs[:count], list(refs[count:])
    gain = refs.pop(0)[...] if normed else None
    weights, refs = refs[:number], refs[number:]
    whole = pieces[0]
    if count > 1 or normed:
        whole = refs.pop(0)

        def change(rows):
            return normalize(rows.astype(f32), gain).astype(bf16) if normed else rows

        put_rows(whole, pieces, change)
    for weight, out in zip(weights, refs):
        matrix = weight[...].reshape(-1, weight.shape[2])
        out[...] = dot(whole[...], matrix).astype(out.dtype)


def rows_product(pieces, gain, weights, block, place, step, dtype, name):
    rows = sum(piece.shape[0] for piece in pieces)
    parts, width = weights[0].shape[0], pieces[0].shape[1]
    joined = len(pieces) > 1 or gain is not None
    shapes = [jax.ShapeDtypeStruct((rows, width), bf16)] if joined else []
    shapes += [jax.ShapeDtypeStruct((rows, block), dtype)] * len(weights)
    gains = [] if gain is None else [gain.reshape(1, -1)]
    got = pl.pallas_call(
        functools.partial(rows_product_kernel, len(pieces), gain is not None, len(weights)),
        grid=(1,),
        in_specs=[resident(piece.shape) for piece in list(pieces) + gains]
        + [
            pl.BlockSpec(
                (parts, step, block), lambda i: (0, 0, place), pipeline_mode=pl.Buffered(1)
            )
        ]
        * len(weights),
        out_specs=[resident(shape.shape) for shape in shapes],
        out_shape=shapes,
        compiler_params=pltpu.CompilerParams(vmem_limit_bytes=56 << 20),
        cost_estimate=BESIDE,
        name=name,
    )(*pieces, *gains, *weights)
    return (got[0], list(got[1:])) if joined else (pieces[0], list(got))


def weight_grad_kernel(counts, number, *refs):
    count = sum(counts)
    lefts, rights, refs = refs[:count], refs[count : 2 * count], refs[2 * count :]
    received, below, out = refs[:number], refs[number:-1], refs[-1]
    rows = lefts[0].shape[1]
    first = pair = 0
    for size in counts:
        total = dot_left_t(lefts[pair][...], rights[pair][...])
        for i in range(pair + 1, pair + size):
            total = total + dot_left_t(lefts[i][...], rights[i][...])
        pair += size
        at = slice(first, first + total.shape[1])
        for block in received:
            total = total + block[0, :, at].astype(f32)
        out[0, :rows, at] = total.astype(bf16)
        first += total.shape[1]
    for block in below:
        out[0, rows:] = block[...]


def weight_grad(groups, received, below, step, name):
    pairs = [pair for group in groups for pair in group]
    rows, width = pairs[0][0].shape
    columns = sum(group[0][1].shape[1] for group in groups)
    deep = step + sum(block.shape[0] for block in below)
    return pl.pallas_call(
        functools.partial(
            weight_grad_kernel, [len(group) for group in groups], len(received)
        ),
        grid=(width // step,),
        in_specs=[pl.BlockSpec((rows, step), lambda i: (0, i))] * len(pairs)
        + [resident(right.shape) for _, right in pairs]
        + [pl.BlockSpec((1, step, columns), lambda i: (i, 0, 0))] * len(received)
        + [resident(block.shape) for block in below],
        out_specs=pl.BlockSpec((1, deep, columns), lambda i: (i, 0, 0)),
        out_shape=jax.ShapeDtypeStruct((width // step, deep, columns), bf16),
        compiler_params=pltpu.CompilerParams(vmem_limit_bytes=56 << 20),
        cost_estimate=BESIDE,
        name=name,
    )(*[left for left, _ in pairs], *[right for _, right in pairs], *received, *below)


def near_kernel(size, widths, me_ref, *refs):
    pieces, outs = refs[:size], refs[size:]
    rows = pieces[0].shape[0]
    for k, piece in enumerate(pieces):
        at = pl.ds(pl.multiple_of((me_ref[0] ^ k) * rows, rows), rows)
        first = 0
        for out, width in zip(outs, widths):
            out[at] = piece[:, first : first + width]
            first += width


def near_call(me, pieces, widths, name):
    rows = len(pieces) * pieces[0].shape[0]
    shapes = [jax.ShapeDtypeStruct((rows, width), bf16) for width in widths]
    return list(
        pl.pallas_call(
            functools.partial(near_kernel, len(pieces), widths),
            grid=(1,),
            in_specs=[pl.BlockSpec(memory_space=pltpu.SMEM)]
            + [resident(piece.shape) for piece in pieces],
            out_specs=[resident(shape.shape) for shape in shapes],
            out_shape=shapes,
            compiler_params=pltpu.CompilerParams(vmem_limit_bytes=32 << 20),
            cost_estimate=BESIDE,
            name=name,
        )(me.reshape(1), *pieces)
    )


def owned_kernel(size, layout, weighted, me_ref, *refs):
    count = size * len(layout)
    pieces, refs = refs[:count], refs[count:]
    weights, gain, refs = refs[:weighted], refs[weighted], refs[weighted + 1 :]
    outs, sums, below = refs[:-2], refs[-2], refs[-1]
    rows = gain.shape[0]
    total = jnp.zeros((rows, 1), f32)
    under = None
    for c, ranges in enumerate(layout):
        for k in range(size):
            piece = pieces[c * size + k]
            owner = me_ref[0] ^ k
            first = 0
            for number, place, wide, count, turned in ranges:
                block = piece[:rows, first : first + count].astype(f32)
                first += count
                at = pl.ds(pl.multiple_of(owner * wide + place, 128), count)
                if turned:
                    outs[number][at] = block.T
                    continue
                outs[number][:, at] = block
                if number < weighted:
                    product = weights[number][:, at].astype(f32) * block
                    total = total + jnp.sum(product, axis=1, keepdims=True)
            if piece.shape[0] > rows:
                more = piece[rows : rows + 8].astype(f32)
                under = more if under is None else under + more
    sums[...] = jnp.broadcast_to(total / gain[:, 0:1], sums.shape)
    below[...] = jnp.zeros_like(below) if under is None else under


def owned_call(me, chunks, layout, weights, gain, shapes, name):
    size = len(chunks[0])
    pieces = [piece for chunk in chunks for piece in chunk]
    rows = gain.shape[0]
    outs = [jax.ShapeDtypeStruct(shape, f32) for shape in shapes]
    outs += [jax.ShapeDtypeStruct((rows, 128), f32)]
    outs += [jax.ShapeDtypeStruct((8, pieces[0].shape[1]), f32)]
    column = jnp.broadcast_to(gain.astype(f32)[:, None], (rows, 128))
    operands = pieces + list(weights) + [column]
    return pl.pallas_call(
        functools.partial(owned_kernel, size, layout, len(weights)),
        grid=(1,),
        in_specs=[pl.BlockSpec(memory_space=pltpu.SMEM)]
        + [resident(array.shape) for array in operands],
        out_specs=[resident(shape.shape) for shape in outs],
        out_shape=outs,
        compiler_params=pltpu.CompilerParams(vmem_limit_bytes=48 << 20),
        cost_estimate=BESIDE,
        name=name,
    )(me.reshape(1), *operands)


def hidden_kernel(first, cores, x_count, g_count, tiles, *refs):
    refs = list(refs)

    def pop(number):
        taken, refs[:number] = refs[:number], []
        return taken

    x_pieces, g_pieces = (pop(x_count), pop(g_count)) if first else ([], [])
    x_all, g_all = (None, None) if first else pop(2)
    weights = [pop(3) for _ in range(cores)]
    if first:
        x_all, g_all = pop(2)
    grads_out, acts_out = pop(cores), pop(cores)
    step = pl.program_id(0)

    if first:

        @pl.when(step == 0)
        def _():
            put_rows(x_all, x_pieces, lambda rows: rows)
            put_rows(g_all, g_pieces, lambda rows: rows)

    def one_core(j):
        w_gate, w_up, w_down = (ref[...].reshape(-1, ref.shape[2]) for ref in weights[j])
        tile = w_gate.shape[1]
        place = step - j * tiles
        gate_place = pl.ds(pl.multiple_of(place * tile, tile), tile)
        up_place = pl.ds(pl.multiple_of((tiles + place) * tile, tile), tile)
        rows = x_all.shape[0] // 2
        for at in (slice(0, rows), slice(rows, None)):
            gate = dot(x_all[at], w_gate)
            up = dot(x_all[at], w_up)
            act_grad = dot(g_all[at], w_down)
            sigma = 1.0 / (1.0 + jnp.exp(-gate))
            silu = gate * sigma
            gate_grad = act_grad * up * sigma * (1.0 + gate * (1.0 - sigma))
            acts_out[j][at, gate_place] = (silu * up).astype(bf16)
            grads_out[j][at, gate_place] = gate_grad.astype(bf16)
            grads_out[j][at, up_place] = (act_grad * silu).astype(bf16)

    for j in range(cores):
        pl.when((step >= j * tiles) & (step < (j + 1) * tiles))(functools.partial(one_core, j))


def hidden_call(x_pieces, g_pieces, weights, name):
    cores, first = len(weights), len(x_pieces) > 1
    data, near, columns = weights[0].shape
    width = data * near
    units = columns // 3
    tile = min(256, units)
    tiles = units // tile
    rows = sum(piece.shape[0] for piece in x_pieces)

    def weight_specs(j):
        return [
            pl.BlockSpec(
                (data, near, tile),
                lambda i, k=k: (0, 0, k * tiles + jnp.clip(i - j * tiles, 0, tiles - 1)),
            )
            for k in range(3)
        ]

    operands = list(x_pieces) + list(g_pieces)
    in_specs = [resident(array.shape) for array in operands]
    for j, weight in enumerate(weights):
        in_specs += weight_specs(j)
        operands += [weight] * 3
    shapes = [jax.ShapeDtypeStruct((rows, width), bf16)] * 2 if first else []
    shapes += [jax.ShapeDtypeStruct((rows, 2 * units), bf16)] * cores
    shapes += [jax.ShapeDtypeStruct((rows, units), bf16)] * cores
    got = pl.pallas_call(
        functools.partial(
            hidden_kernel, first, cores, len(x_pieces), len(g_pieces), tiles
        ),
        grid=(cores * tiles,),
        in_specs=in_specs,
        out_specs=[resident(shape.shape) for shape in shapes],
        out_shape=shapes,
        compiler_params=pltpu.CompilerParams(vmem_limit_bytes=60 << 20),
        cost_estimate=BESIDE,
        name=name,
    )(*operands)
    got = list(got)
    kept, got = (got[:2], got[2:]) if first else ([x_pieces[0], g_pieces[0]], got)
    return kept, got[:cores], got[cores:]


def phase(always, body):
    def never():
        return jax.tree.map(lambda leaf: jnp.zeros(leaf.shape, leaf.dtype), jax.eval_shape(body))

    return lax.cond(always, body, never)


def trade(block, axis, step):
    return lax.ppermute(block, axis, [(i, i ^ step) for i in range(lax.axis_size(axis))])


def halves(rows):
    middle = rows.shape[0] // 2
    return [rows[:middle], rows[middle:]]


def spread_near(own):
    if lax.axis_size("model") == 1:
        return list(own)
    return list(own) + [trade(half, "model", k) for k in (1, 2) for half in own]


def spread_far(near, *first):
    if len(near) == 2:
        return []
    upper, lower = near[2], near[5]
    if first:
        upper, lower = after((upper, lower), *first)
    return [trade(upper, "model", 2), trade(lower, "model", 1)]


def send_near(near, far):
    x_upper, x_lower, y_upper, y_lower = near
    x_upper, y_lower = after((x_upper, y_lower), *far)
    y_upper = (y_upper.astype(f32) + far[0].astype(f32)).astype(bf16)
    x_lower = (x_lower.astype(f32) + far[1].astype(f32)).astype(bf16)
    return [
        trade(x_upper, "model", 1),
        trade(y_upper, "model", 2),
        trade(x_lower, "model", 1),
        trade(y_lower, "model", 2),
    ]


def swap(piece_of):
    me = lax.axis_index("model")
    others = range(1, lax.axis_size("model"))
    return [piece_of(me)] + [trade(piece_of(me ^ k), "model", k) for k in others]


def take(array, index, count):
    size = array.shape[1] // count
    return lax.dynamic_slice_in_dim(array, index * size, size, 1)


def rows_at(array):
    return lambda i: lax.dynamic_index_in_dim(array, i, 0, keepdims=False)


def in_order(pieces):
    me = lax.axis_index("model")
    size = len(pieces)
    return jnp.stack(
        [lax.select_n(me, *[pieces[j ^ i] for j in range(size)]) for i in range(size)]
    )


def after(value, *first):
    return lax.optimization_barrier((value,) + first)[0]


def on_device(
    hidden_in,
    out_grad,
    segments,
    positions,
    w_query,
    key_weight,
    value_weight,
    w_output,
    w_gate,
    w_up,
    w_down,
    attn_gain,
    mlp_gain,
    query_gain,
    key_gain,
):
    data = lax.axis_size("data")
    model = lax.axis_size("model")
    cores = lax.axis_size("tp")
    core = lax.axis_index("tp")
    seq_len = positions.shape[0]
    half = seq_len // cores
    shard = w_query.shape[0]
    width = hidden_in.shape[1]
    head_size = query_gain.shape[0] * data * model
    q_heads = w_query.shape[1] // model // head_size
    kv_heads = key_weight.shape[1] // model // head_size
    repeat = q_heads // kv_heads
    q_cols = q_heads * head_size
    kv_cols = kv_heads * head_size
    cols = q_cols + 2 * kv_cols
    wide = cols + q_cols
    ff = w_gate.shape[1] // model
    always = (segments[0] * segments[0] + segments[0]) % 2 == 0

    small = jnp.concatenate([attn_gain, mlp_gain, query_gain, key_gain])
    small_rows = -(-small.shape[0] // wide)
    place_rows = -(-seq_len // wide)

    def as_rows(vector, rows):
        return jnp.pad(vector, (0, rows * wide - vector.shape[0])).reshape(rows, wide)

    extra = jnp.concatenate(
        [
            as_rows(small, small_rows),
            as_rows(segments.astype(bf16), place_rows),
            as_rows((positions // 8).astype(bf16), place_rows),
            as_rows((positions % 8).astype(bf16), place_rows),
        ]
    )
    extra = jnp.pad(extra, ((0, -extra.shape[0] % 16), (0, 0)))
    turned_output = w_output.T

    def attn_piece(i):
        parts = [
            take(w_query, i, model),
            take(key_weight, i, model),
            take(value_weight, i, model),
            take(turned_output, i, model),
        ]
        return jnp.concatenate([jnp.concatenate(parts, axis=1), extra])

    turned_down = w_down.T
    chunks = [ff - ff // 3, ff // 3] if ff % 768 == 0 else [ff]
    starts = [sum(chunks[:c]) for c in range(len(chunks))]

    def over_data(pieces):
        return lax.all_gather(pieces, "data", axis=0, tiled=False)

    attn_got = swap(attn_piece)
    tied = lax.optimization_barrier((halves(hidden_in), halves(out_grad), attn_got))
    grad_halves = tied[1]
    x_near = spread_near(tied[0])
    tied = lax.optimization_barrier((w_gate, w_up, turned_down, x_near))
    w_gate_sent, w_up_sent, turned_down, x_near = tied
    x_blocks = x_near + spread_far(x_near)
    mlp_got = swap(
        lambda i: jnp.concatenate(
            [
                take(weight, i, model)[:, first : first + count]
                for first, count in zip(starts, chunks)
                for weight in (w_gate_sent, w_up_sent, turned_down)
            ],
            axis=1,
        )
    )

    def places_of(first):
        rows = [
            got[shard + first : shard + first + place_rows].reshape(-1)[:seq_len]
            for got in attn_got
        ]
        return jnp.stack(rows).astype(f32)

    seg_all = places_of(small_rows)
    pos_all = 8.0 * places_of(small_rows + place_rows) + places_of(small_rows + 2 * place_rows)
    cosine, sine = tables(pos_all, head_size)

    attn_near = in_order(attn_got)
    gain_rows = attn_near[:, shard : shard + small_rows].reshape(-1, wide)
    gain_rows = jnp.pad(gain_rows, ((0, -gain_rows.shape[0] % 16), (0, 0)))
    near = jnp.concatenate([attn_near[:, :shard].reshape(-1, wide), gain_rows])
    me = lax.axis_index("model")
    mlp_near = near_call(me, mlp_got, [3 * count for count in chunks], "hidden_exchange")
    attn_full = over_data(near)
    tied = lax.optimization_barrier((attn_full, mlp_near, x_blocks, cosine, sine))
    attn_full, mlp_near, x_blocks, cosine, sine = tied
    mlp_full = [over_data(piece) for piece in mlp_near]

    gains = attn_full[:, model * shard : model * shard + model * small_rows]
    gains = gains.reshape(data * model, -1).astype(f32)
    part = query_gain.shape[0]
    gain_in = gains[:, :shard].reshape(-1)
    gain_mid = gains[:, shard : 2 * shard].reshape(-1)
    gain_query = gains[:, 2 * shard : 2 * shard + part].reshape(-1)
    gain_key = gains[:, 2 * shard + part : 2 * shard + 2 * part].reshape(-1)
    def with_cores(weight):
        return [weight] + [trade(weight, "tp", j) for j in range(1, cores)]

    near_rows = model * shard
    grad_near = spread_near(after(grad_halves, *x_blocks, *mlp_near))

    seg_rows = jnp.pad(seg_all[:, None], ((0, 0), (0, 7), (0, 0)))
    seg_columns = seg_all[:, :, None]
    head_gains = jnp.pad(jnp.stack([gain_query, gain_key]), ((0, 6), (0, 0)))
    shared = [cosine, sine, seg_columns, seg_rows]
    o_place = [cols // q_cols] * cores

    def product_phase():
        w_attn = with_cores(attn_full)
        normed_in, first_raw = rows_product(
            x_blocks, gain_in, w_attn[:1], cols, 0, near_rows, f32, "query_key_value"
        )
        raw = [first_raw[0].reshape(model, half, cols)]
        for j in range(1, cores):
            mine = rows_product(
                [normed_in], None, [w_attn[j]], cols, 0, near_rows, f32, "query_key_value_other"
            )[1][0]
            raw.append(trade(mine, "tp", j).reshape(model, half, cols))
        return w_attn[1:], normed_in, raw

    w_others, own_normed, raw = phase(always, product_phase)
    w_attn = [attn_full] + w_others
    raw, grad_near = lax.optimization_barrier((raw, grad_near))

    def attention_phase():
        far = spread_far(grad_near)
        attended = attention_call(
            functools.partial(attend_kernel, cores, kv_heads, repeat),
            "attend",
            core,
            raw,
            shared,
            head_gains,
            [jax.ShapeDtypeStruct((model, half, q_cols), bf16)] * cores,
            [],
            [((seq_len, cols), f32), ((seq_len, q_cols), bf16)],
        )
        attended, far = lax.optimization_barrier((list(attended), far))
        att_pieces = [attended[0]] + [trade(attended[j], "tp", j) for j in range(1, cores)]
        att_flat = [piece.reshape(-1, q_cols) for piece in att_pieces]
        return with_cores(own_normed)[1:], att_flat, attended, far

    normed_others, att_flat, attended, grad_far = phase(always, attention_phase)
    normed_in = [own_normed] + normed_others
    grad_blocks = grad_near + grad_far

    def data_sum(total):
        return lax.psum_scatter(total, "data", scatter_dimension=0, tiled=False)

    def out_phase():
        own, _, got = project_and_send(
            att_flat, w_attn, o_place, half, near_rows, "attention_out"
        )
        middle, *low = rows_call("norm", own, hidden_in, got, gain_mid, None, True, "middle")
        near = spread_near(low)
        return middle, near + spread_far(near)

    middle, mid_blocks = phase(always, out_phase)

    def for_own_core(rows):
        return [
            [rows[k][0]] + [trade(rows[k][j], "tp", j) for j in range(1, cores)] for k in range(2)
        ]

    def hidden_weights(kept, rows, name):
        groups = [[(kept[k][j], rows[k][j]) for j in range(cores)] for k in range(2)]
        return weight_grad(groups, [], (), near_rows, name)

    def first_phase():
        weights = with_cores(mlp_full[0])
        rows, *by_core = hidden_call(mid_blocks, grad_blocks, weights[:1], "hidden_units_a")
        kept = [with_cores(whole) for whole in rows]
        by_core = [by_core]
        for weight in weights[1:]:
            got = hidden_call(*[[whole] for whole in rows], [weight], "hidden_units_a_other")
            by_core.append(got[1:])
        first_rows = [[got[k][0] for got in by_core] for k in range(2)]
        total = hidden_weights(kept, for_own_core(first_rows), "hidden_weights_a")
        return weights[1:], kept, first_rows, total

    other_weights, kept, first_rows, total = phase(always, first_phase)
    w_mlp = [[mlp_full[0]] + other_weights]
    wholes = [[kept[k][0]] for k in range(2)]
    mlp_sums = []
    if len(chunks) > 1:
        mlp_sums.append(data_sum(total))
    count = cores * len(chunks)

    def hidden_phase():
        rows, weights = [first_rows], list(w_mlp)
        if len(chunks) > 1:
            weights.append(with_cores(mlp_full[1]))
            by_core = [
                hidden_call(*wholes, [weight], "hidden_units_b")[1:] for weight in weights[1]
            ]
            rows.append([[got[k][0] for got in by_core] for k in range(2)])
        both_cores = [w for pair in weights for w in pair]
        own, _, got = project_and_send(
            [grads for pair in rows for grads in pair[0]],
            both_cores,
            [0] * count,
            half,
            near_rows,
            "normed_mid_grad",
        )
        last_rows = after(for_own_core(rows[-1]), own)
        total = hidden_weights(kept, last_rows, "hidden_weights_b")
        acts = [acts for pair in rows for acts in pair[1]]
        return own, got, total, acts, [w for pair in weights[1:] for w in pair[1:]]

    mid_part, mid_got, total, act_rows, other_weights = phase(always, hidden_phase)
    if len(chunks) > 1:
        mlp_sums.append(data_sum(total))
        w_mlp.append([mlp_full[1]] + other_weights)
    both_cores = [w for pair in w_mlp for w in pair]

    def branch_phase():
        middle_grad, *low = rows_call(
            "back", mid_part, middle, mid_got, gain_mid, out_grad, True, "middle_grad"
        )
        down_parts = project(
            act_rows, both_cores, [2] * count, 0, [half] * model, near_rows, "hidden_out"
        )
        near = spread_near(low)
        branch_blocks = near + spread_far(near, *down_parts)
        return middle_grad, branch_blocks, down_parts

    middle_grad, branch_blocks, down_parts = phase(always, branch_phase)
    down_got = [trade(down_parts[k], "model", k) for k in range(1, model)]

    def attend_back_phase():
        branch, products = rows_product(
            branch_blocks, None, w_attn, q_cols, o_place[0], near_rows, bf16, "attended_grad"
        )
        products = [piece.reshape(model, half, q_cols) for piece in products]
        att_grads = [trade(piece, "tp", j) if j else piece for j, piece in enumerate(products)]
        *qkv_back, head_grads = attention_call(
            functools.partial(attend_back_kernel, cores, kv_heads, repeat),
            "attend_back",
            core,
            raw + att_grads,
            shared,
            head_gains,
            [jax.ShapeDtypeStruct((model, half, cols), bf16)] * cores,
            [jax.ShapeDtypeStruct(head_gains.shape, f32)],
            [
                ((seq_len, cols), f32),
                ((seq_len, q_cols), bf16),
                ((seq_len, cols), f32),
                ((seq_len, cols), bf16),
            ],
        )
        return with_cores(branch), list(qkv_back), head_grads

    branch, qkv_back, head_grads = phase(always, attend_back_phase)

    def attention_weights_phase():
        back_pieces = [qkv_back[0]] + [trade(qkv_back[j], "tp", j) for j in range(1, cores)]
        ride = head_grads[:2].reshape(-1)
        ride = jnp.pad(ride, (0, ride_rows * wide - ride.shape[0])).astype(bf16)
        ride = jnp.pad(ride.reshape(ride_rows, wide), ((0, -ride_rows % 16), (0, 0)))
        groups = [
            [(normed_in[j], qkv_back[j].reshape(-1, cols)) for j in range(cores)],
            [(branch[j], attended[j].reshape(-1, q_cols)) for j in range(cores)],
        ]
        attn_total = weight_grad(groups, [], [ride], near_rows, "attention_weights")
        return attn_total, [piece.reshape(-1, cols) for piece in back_pieces]

    ride_rows = -(-2 * head_size // wide)
    attn_total, back_flat = phase(always, attention_weights_phase)
    attn_total, down_got = lax.optimization_barrier((attn_total, down_got))
    attn_sum = data_sum(attn_total)
    back_flat, first_sums = lax.optimization_barrier((back_flat, mlp_sums[:-1]))

    def exchanged(total):
        return swap(rows_at(total.reshape(model, shard, -1)))

    def in_grad_phase():
        own, far, got = project_and_send(
            back_flat, w_attn, [0] * cores, half, near_rows, "normed_in_grad"
        )
        hidden_out = rows_call(
            "sum", down_parts[0], middle, after(down_got, *far), None, None, False, "hidden_out_sum"
        )[0]
        return own, got, [exchanged(total) for total in first_sums], hidden_out

    in_part, in_got, first_got, hidden_out = phase(always, in_grad_phase)
    in_got, last_sum = lax.optimization_barrier((in_got, mlp_sums[-1]))

    def last_phase():
        last_got = exchanged(last_sum)
        grad_in = rows_call(
            "back", in_part, hidden_in, in_got, gain_in, middle_grad, False, "grad_in"
        )[0]
        layout = [
            [(kind, first, ff, size, kind == 2) for kind in range(3)]
            for first, size in zip(starts, chunks)
        ]
        shapes = [w_gate.shape, w_up.shape, w_down.shape]
        owned = owned_call(
            me, first_got + [last_got], layout, [w_gate, w_up], mlp_gain, shapes, "hidden_owned"
        )
        return grad_in, owned[:3], owned[3][:, 0]

    got = phase(always, last_phase)
    grad_in, (grad_gate, grad_up, grad_down), mlp_part = got
    attn_sum = after(attn_sum, grad_in)
    weight_rows = attn_sum[:near_rows].reshape(model, shard, wide)
    gain_row = attn_sum[near_rows:]
    gain_row = jnp.broadcast_to(gain_row, (model,) + gain_row.shape)
    attn_rows = jnp.concatenate([weight_rows, gain_row], axis=1)
    attn_got = swap(rows_at(attn_rows))
    layout = [
        [
            (0, 0, q_cols, q_cols, False),
            (1, 0, kv_cols, kv_cols, False),
            (2, 0, kv_cols, kv_cols, False),
            (3, 0, q_cols, q_cols, True),
        ]
    ]
    weights = [w_query, key_weight, value_weight]
    shapes = [weight.shape for weight in weights] + [w_output.shape]
    owned = owned_call(me, [attn_got], layout, weights, attn_gain, shapes, "attention_owned")
    grad_query, grad_key, grad_value, grad_output, attn_part, gain_sums = owned
    gain_sums = gain_sums[:ride_rows].reshape(-1)[: 2 * head_size]
    sums = lax.psum(jnp.concatenate([attn_part[:, 0], mlp_part, gain_sums]), "tp")
    where = lax.axis_index("data") * model + lax.axis_index("model")
    first = 2 * shard + where * part
    return (
        hidden_out,
        grad_in,
        grad_query,
        grad_key,
        grad_value,
        grad_output,
        grad_gate,
        grad_up,
        grad_down,
        sums[:shard],
        sums[shard : 2 * shard],
        lax.dynamic_slice_in_dim(sums, first, part),
        lax.dynamic_slice_in_dim(sums, first + head_size, part),
    )


def solution(mesh):
    fsdp, tp = mesh.shape["fsdp"], mesh.shape["tp"]
    model = 4 if fsdp % 4 == 0 else 1
    split = Mesh(mesh.devices.reshape(fsdp // model, model, tp), ("data", "model", "tp"))
    batch = ("data", "model")
    rows = P(("data", "model", "tp"), None)
    into = P(batch, "tp")
    back = P("tp", batch)
    in_specs = (rows, rows, P(batch), P(batch), into, into, into, back, into, into, back)
    in_specs = in_specs + (P(batch),) * 4
    out_specs = (rows, rows, into, into, into, back, into, into, back) + (P(batch),) * 4
    return jax.shard_map(
        on_device, mesh=split, in_specs=in_specs, out_specs=out_specs, check_vma=False
    )
```

```python
import functools

import jax
import jax.numpy as jnp
from jax import lax
from jax.experimental import pallas as pl
from jax.experimental.pallas import tpu as pltpu
from jax.sharding import Mesh, PartitionSpec as P

epsilon = 1e-06
rope_base = 1000000.0
bf16 = jnp.bfloat16
f32 = jnp.float32
BESIDE = pl.CostEstimate(flops=1 << 20, bytes_accessed=1 << 16, transcendentals=0)


def dot(left, right):
    return jnp.dot(left, right, preferred_element_type=f32)


def dot_right_t(left, right):
    return lax.dot_general(left, right, (((1,), (1,)), ((), ())), preferred_element_type=f32)


def dot_left_t(left, right):
    return lax.dot_general(left, right, (((0,), (0,)), ((), ())), preferred_element_type=f32)


def normalize(operand, norm_gain):
    return (
        operand
        * lax.rsqrt(jnp.mean(operand * operand, axis=-1, keepdims=True) + epsilon)
        * norm_gain
    )


def norm_back(operand, norm_gain, upstream):
    factor = lax.rsqrt(jnp.mean(operand * operand, axis=-1, keepdims=True) + epsilon)
    weighted = upstream * norm_gain
    inner = jnp.mean(weighted * operand, axis=-1, keepdims=True)
    return factor * weighted - operand * factor * factor * factor * inner


def tables(positions, head_size):
    indices = jnp.arange(head_size // 2).astype(f32)
    frequency = rope_base ** (-2.0 * indices / head_size)
    angles = positions.astype(f32)[..., None] * frequency
    cosine, sine = jnp.cos(angles), jnp.sin(angles)
    return (jnp.concatenate([cosine, cosine], -1), jnp.concatenate([-sine, sine], -1))


def half_turn(operand):
    return pltpu.roll(operand, operand.shape[-1] // 2, 1)


def lay_in_order(scratch, refs, core):
    half = refs[0].shape[1]
    for j, ref in enumerate(refs):
        scratch[pl.ds(pl.multiple_of((core ^ j) * half, half), half)] = ref[0]


def head_rows(raw, heads, repeat, gains, cosine, sine):
    size = gains.shape[1]

    def turned(column, gain):
        rows = normalize(raw[:, column * size : (column + 1) * size], gain)
        return (rows * cosine + half_turn(rows) * sine).astype(bf16)

    queries = [turned(h, gains[0:1]) for h in range(heads * repeat)]
    keys = [turned(heads * repeat + g, gains[1:2]) for g in range(heads)]
    first = heads * repeat + heads
    values = [
        raw[:, (first + g) * size : (first + g + 1) * size].astype(bf16) for g in range(heads)
    ]
    return queries, keys, values


def masked_probs(key, query, allowed):
    scores = dot_right_t(key, query) * query.shape[1] ** (-0.5)
    scores = jnp.where(allowed, scores, -1e30)
    exp_terms = jnp.exp(scores - jnp.max(scores, axis=0, keepdims=True))
    return exp_terms * (1.0 / jnp.sum(exp_terms, axis=0, keepdims=True))


def query_strips(rows, column_ref, row_ref):
    step = min(256, rows)
    for first in range(0, rows, step):
        seen = first + step
        keys = lax.broadcasted_iota(jnp.int32, (seen, step), 0)
        queries = lax.broadcasted_iota(jnp.int32, (seen, step), 1) + first
        same = column_ref[0, :seen, 0:1] == row_ref[0, 0:1, first:seen]
        yield slice(first, seen), seen, same & (keys <= queries)


def attend_kernel(cores, heads, repeat, core_ref, *refs):
    raws, refs = refs[:cores], refs[cores:]
    cos_ref, sin_ref, column_ref, row_ref, gain_ref = refs[:5]
    outs, raw, rows_out = refs[5:-2], refs[-2], refs[-1]
    core = core_ref[0]
    half = raws[0].shape[1]
    lay_in_order(raw, raws, core)
    queries, keys, values = head_rows(
        raw, heads, repeat, gain_ref[...], cos_ref[0], sin_ref[0]
    )
    size = gain_ref.shape[1]
    turned = [value.astype(f32).T.astype(bf16) for value in values]
    for at, seen, allowed in query_strips(raw.shape[0], column_ref, row_ref):
        for h, query in enumerate(queries):
            g = h // repeat
            probs = masked_probs(keys[g][:seen], query[at], allowed).astype(bf16)
            rows = dot(turned[g][:, :seen], probs).T
            rows_out[at, h * size : (h + 1) * size] = rows.astype(bf16)
    for j, out in enumerate(outs):
        out[0] = rows_out[pl.ds(pl.multiple_of((core ^ j) * half, half), half)]


def attend_back_kernel(cores, heads, repeat, core_ref, *refs):
    raws, grads, refs = refs[:cores], refs[cores : 2 * cores], refs[2 * cores :]
    cos_ref, sin_ref, column_ref, row_ref, gain_ref = refs[:5]
    outs, gain_out = refs[5 : 5 + cores], refs[5 + cores]
    raw, grad, totals, rows_out = refs[6 + cores :]
    core = core_ref[0]
    half = raws[0].shape[1]
    cosine, sine, gains = cos_ref[0], sin_ref[0], gain_ref[...]
    lay_in_order(raw, raws, core)
    lay_in_order(grad, grads, core)
    queries, keys, values = head_rows(raw, heads, repeat, gains, cosine, sine)
    size = gains.shape[1]
    scale = size ** (-0.5)
    count = heads * repeat

    @pl.when(pl.program_id(0) == 0)
    def _():
        gain_out[...] = jnp.zeros_like(gain_out)

    def columns(i):
        return slice(i * size, (i + 1) * size)

    turned_keys = [key.astype(f32).T.astype(bf16) for key in keys]
    totals[:, count * size :] = jnp.zeros_like(totals[:, count * size :])
    for at, seen, allowed in query_strips(raw.shape[0], column_ref, row_ref):
        for g in range(heads):
            key_grad = value_grad = None
            for h in range(g * repeat, (g + 1) * repeat):
                probs = masked_probs(keys[g][:seen], queries[h][at], allowed)
                out_grad = grad[at, columns(h)]
                prob_grad = dot_right_t(values[g][:seen], out_grad)
                delta = jnp.sum(probs * prob_grad, axis=0, keepdims=True)
                score_grad = (probs * (prob_grad - delta)).astype(bf16)
                totals[at, columns(h)] = dot(turned_keys[g][:, :seen], score_grad).T * scale
                key_part = dot(score_grad, queries[h][at])
                value_part = dot(probs.astype(bf16), out_grad)
                key_grad = key_part if key_grad is None else key_grad + key_part
                value_grad = value_part if value_grad is None else value_grad + value_part
            totals[:seen, columns(count + g)] += key_grad * scale
            totals[:seen, columns(count + heads + g)] += value_grad
    for i in range(count + heads):
        row = 0 if i < count else 1
        upstream = totals[:, columns(i)]
        turned = upstream * cosine - half_turn(upstream) * sine
        rows = raw[:, columns(i)]
        factor = lax.rsqrt(jnp.mean(rows * rows, axis=-1, keepdims=True) + epsilon)
        gain_out[row : row + 1] += jnp.sum(turned * rows * factor, axis=0, keepdims=True)
        back = norm_back(rows, gains[row : row + 1], turned)
        rows_out[:, columns(i)] = back.astype(bf16)
    rows_out[:, (count + heads) * size :] = totals[:, (count + heads) * size :].astype(bf16)
    for j, out in enumerate(outs):
        out[0] = rows_out[pl.ds(pl.multiple_of((core ^ j) * half, half), half)]


def attention_call(kernel, name, core, halves, shared, gains, outs, extra_out, scratch):
    def per_sequence(array):
        return pl.BlockSpec((1,) + array.shape[1:], lambda i: (i, 0, 0))

    whole = pl.BlockSpec(gains.shape, lambda i: (0, 0))
    out_specs = [per_sequence(shape) for shape in outs] + [
        pl.BlockSpec(shape.shape, lambda i: (0, 0)) for shape in extra_out
    ]
    return pl.pallas_call(
        kernel,
        grid=(halves[0].shape[0],),
        in_specs=[pl.BlockSpec(memory_space=pltpu.SMEM)]
        + [per_sequence(array) for array in halves + shared]
        + [whole],
        out_specs=out_specs,
        out_shape=outs + extra_out,
        scratch_shapes=[pltpu.VMEM(shape, dtype) for shape, dtype in scratch],
        compiler_params=pltpu.CompilerParams(vmem_limit_bytes=48 << 20),
        cost_estimate=BESIDE,
        name=name,
    )(core.reshape(1), *halves, *shared, gains)


def resident(shape):
    zeros = (0,) * len(shape)
    return pl.BlockSpec(shape, lambda i: zeros, pipeline_mode=pl.Buffered(1))


def project_kernel(count, *refs):
    lefts, rights, outs = refs[:count], refs[count : 2 * count], refs[2 * count :]

    total = dot_right_t(lefts[0][...], rights[0][0])
    for left, right in zip(lefts[1:], rights[1:]):
        total = total + dot_right_t(left[...], right[0])
    first = 0
    for out in outs:
        out[...] = total[first : first + out.shape[0]].astype(out.dtype)
        first += out.shape[0]


def project(lefts, rights, places, first, sizes, step, name):
    parts = rights[0].shape[0]
    rows = sum(sizes)

    def left_spec(left):
        return pl.BlockSpec(
            (rows, left.shape[1]), lambda i: (first // rows, 0), pipeline_mode=pl.Buffered(1)
        )

    def right_spec(left, place):
        return pl.BlockSpec((1, step, left.shape[1]), lambda i: (i, 0, place))

    return list(
        pl.pallas_call(
            functools.partial(project_kernel, len(lefts)),
            grid=(parts,),
            in_specs=[left_spec(left) for left in lefts]
            + [right_spec(left, place) for left, place in zip(lefts, places)],
            out_specs=[pl.BlockSpec((size, step), lambda i: (0, i)) for size in sizes],
            out_shape=[
                jax.ShapeDtypeStruct((size, parts * step), bf16 if first or k else f32)
                for k, size in enumerate(sizes)
            ],
            compiler_params=pltpu.CompilerParams(vmem_limit_bytes=56 << 20),
            cost_estimate=BESIDE,
            name=name,
        )(*lefts, *rights)
    )


def project_and_send(lefts, rights, places, rows, step, name, near_too=True):
    if lax.axis_size("model") == 1:
        return project(lefts, rights, places, 0, [rows], step, name)[0], [], []
    half = rows // 2
    far = project(lefts, rights, places, 3 * rows, [half] * 2, step, name + "_far")
    got = [trade(far[0], "model", 1), trade(far[1], "model", 2)]
    own, *near = project(lefts, rights, places, 0, [rows] + [half] * 4, step, name)
    return own, got, send_near(near, got) if near_too else near


def put_rows(whole, pieces, change):
    first = 0
    for piece in pieces:
        whole[first : first + piece.shape[0]] = change(piece[...])
        first += piece.shape[0]


def rows_kernel(kind, count, *refs):
    (own, base), got, refs = refs[:2], refs[2 : 2 + count], list(refs[2 + count :])
    total = own[...]
    if count == 4:
        upper = got[0][...].astype(f32) + got[1][...].astype(f32)
        lower = got[2][...].astype(f32) + got[3][...].astype(f32)
        total += jnp.where(pl.program_id(0) == 0, upper, lower)
    else:
        for piece in got:
            total += piece[...].astype(f32)
    rows = base[...].astype(f32)
    if kind == "sum":
        refs[0][...] = (rows + total).astype(bf16)
        return
    gain = refs[0][...]
    if kind == "norm":
        whole, *low = refs[1:]
        total = rows + total
        sent = normalize(total, gain)
    else:
        more, whole, *low = refs[1:]
        total = more[...].astype(f32) + norm_back(rows, gain, total)
        sent = total
    whole[...] = total
    for place, half in enumerate(low):

        @pl.when(pl.program_id(0) == place)
        def _():
            half[...] = sent.astype(bf16)


def rows_call(kind, own, base, got, gain, more, sent, name):
    rows, width = own.shape
    step = rows // 2
    strip = pl.BlockSpec((step, width), lambda i: (i, 0))
    half = resident((step, width))
    operands = [own, base] + list(got)
    in_specs = [strip, strip] + [half if len(got) == 4 else strip] * len(got)
    if gain is not None:
        operands.append(gain.reshape(1, width))
        in_specs.append(resident((1, width)))
    if more is not None:
        operands.append(more)
        in_specs.append(strip)
    out_specs, shapes = [strip], [jax.ShapeDtypeStruct((rows, width), bf16 if gain is None else f32)]
    if sent:
        out_specs += [half] * 2
        shapes += [jax.ShapeDtypeStruct((step, width), bf16)] * 2
    return list(
        pl.pallas_call(
            functools.partial(rows_kernel, kind, len(got)),
            grid=(2,),
            in_specs=in_specs,
            out_specs=out_specs,
            out_shape=shapes,
            compiler_params=pltpu.CompilerParams(vmem_limit_bytes=48 << 20),
            cost_estimate=BESIDE,
            name=name,
        )(*operands)
    )


def rows_product_kernel(count, normed, number, *refs):
    pieces, refs = refs[:count], list(refs[count:])
    gain = refs.pop(0)[...] if normed else None
    weights, refs = refs[:number], refs[number:]
    whole = pieces[0]
    if count > 1 or normed:
        whole = refs.pop(0)

        def change(rows):
            return normalize(rows.astype(f32), gain).astype(bf16) if normed else rows

        put_rows(whole, pieces, change)
    for weight, out in zip(weights, refs):
        matrix = weight[...].reshape(-1, weight.shape[2])
        out[...] = dot(whole[...], matrix).astype(out.dtype)


def rows_product(pieces, gain, weights, block, place, step, dtype, name):
    rows = sum(piece.shape[0] for piece in pieces)
    parts, width = weights[0].shape[0], pieces[0].shape[1]
    joined = len(pieces) > 1 or gain is not None
    shapes = [jax.ShapeDtypeStruct((rows, width), bf16)] if joined else []
    shapes += [jax.ShapeDtypeStruct((rows, block), dtype)] * len(weights)
    gains = [] if gain is None else [gain.reshape(1, -1)]
    got = pl.pallas_call(
        functools.partial(rows_product_kernel, len(pieces), gain is not None, len(weights)),
        grid=(1,),
        in_specs=[resident(piece.shape) for piece in list(pieces) + gains]
        + [
            pl.BlockSpec(
                (parts, step, block), lambda i: (0, 0, place), pipeline_mode=pl.Buffered(1)
            )
        ]
        * len(weights),
        out_specs=[resident(shape.shape) for shape in shapes],
        out_shape=shapes,
        compiler_params=pltpu.CompilerParams(vmem_limit_bytes=56 << 20),
        cost_estimate=BESIDE,
        name=name,
    )(*pieces, *gains, *weights)
    return (got[0], list(got[1:])) if joined else (pieces[0], list(got))


def weight_grad_kernel(counts, number, *refs):
    count = sum(counts)
    lefts, rights, refs = refs[:count], refs[count : 2 * count], refs[2 * count :]
    received, below, out = refs[:number], refs[number:-1], refs[-1]
    rows = lefts[0].shape[1]
    first = pair = 0
    for size in counts:
        total = dot_left_t(lefts[pair][...], rights[pair][...])
        for i in range(pair + 1, pair + size):
            total = total + dot_left_t(lefts[i][...], rights[i][...])
        pair += size
        at = slice(first, first + total.shape[1])
        for block in received:
            total = total + block[0, :, at].astype(f32)
        out[0, :rows, at] = total.astype(bf16)
        first += total.shape[1]
    for block in below:
        out[0, rows:] = block[...]


def weight_grad(groups, received, below, step, name):
    pairs = [pair for group in groups for pair in group]
    rows, width = pairs[0][0].shape
    columns = sum(group[0][1].shape[1] for group in groups)
    deep = step + sum(block.shape[0] for block in below)
    return pl.pallas_call(
        functools.partial(
            weight_grad_kernel, [len(group) for group in groups], len(received)
        ),
        grid=(width // step,),
        in_specs=[pl.BlockSpec((rows, step), lambda i: (0, i))] * len(pairs)
        + [resident(right.shape) for _, right in pairs]
        + [pl.BlockSpec((1, step, columns), lambda i: (i, 0, 0))] * len(received)
        + [resident(block.shape) for block in below],
        out_specs=pl.BlockSpec((1, deep, columns), lambda i: (i, 0, 0)),
        out_shape=jax.ShapeDtypeStruct((width // step, deep, columns), bf16),
        compiler_params=pltpu.CompilerParams(vmem_limit_bytes=56 << 20),
        cost_estimate=BESIDE,
        name=name,
    )(*[left for left, _ in pairs], *[right for _, right in pairs], *received, *below)


def near_kernel(size, widths, me_ref, *refs):
    pieces, outs = refs[:size], refs[size:]
    rows = pieces[0].shape[0]
    for k, piece in enumerate(pieces):
        at = pl.ds(pl.multiple_of((me_ref[0] ^ k) * rows, rows), rows)
        first = 0
        for out, width in zip(outs, widths):
            out[at] = piece[:, first : first + width]
            first += width


def near_call(me, pieces, widths, name):
    rows = len(pieces) * pieces[0].shape[0]
    shapes = [jax.ShapeDtypeStruct((rows, width), bf16) for width in widths]
    return list(
        pl.pallas_call(
            functools.partial(near_kernel, len(pieces), widths),
            grid=(1,),
            in_specs=[pl.BlockSpec(memory_space=pltpu.SMEM)]
            + [resident(piece.shape) for piece in pieces],
            out_specs=[resident(shape.shape) for shape in shapes],
            out_shape=shapes,
            compiler_params=pltpu.CompilerParams(vmem_limit_bytes=32 << 20),
            cost_estimate=BESIDE,
            name=name,
        )(me.reshape(1), *pieces)
    )


def owned_kernel(size, layout, weighted, me_ref, *refs):
    count = size * len(layout)
    pieces, refs = refs[:count], refs[count:]
    weights, gain, refs = refs[:weighted], refs[weighted], refs[weighted + 1 :]
    outs, sums, below = refs[:-2], refs[-2], refs[-1]
    rows = gain.shape[0]
    total = jnp.zeros((rows, 1), f32)
    under = None
    for c, ranges in enumerate(layout):
        for k in range(size):
            piece = pieces[c * size + k]
            owner = me_ref[0] ^ k
            first = 0
            for number, place, wide, count, turned in ranges:
                block = piece[:rows, first : first + count].astype(f32)
                first += count
                at = pl.ds(pl.multiple_of(owner * wide + place, 128), count)
                if turned:
                    outs[number][at] = block.T
                    continue
                outs[number][:, at] = block
                if number < weighted:
                    product = weights[number][:, at].astype(f32) * block
                    total = total + jnp.sum(product, axis=1, keepdims=True)
            if piece.shape[0] > rows:
                more = piece[rows : rows + 8].astype(f32)
                under = more if under is None else under + more
    sums[...] = jnp.broadcast_to(total / gain[:, 0:1], sums.shape)
    below[...] = jnp.zeros_like(below) if under is None else under


def owned_call(me, chunks, layout, weights, gain, shapes, name):
    size = len(chunks[0])
    pieces = [piece for chunk in chunks for piece in chunk]
    rows = gain.shape[0]
    outs = [jax.ShapeDtypeStruct(shape, f32) for shape in shapes]
    outs += [jax.ShapeDtypeStruct((rows, 128), f32)]
    outs += [jax.ShapeDtypeStruct((8, pieces[0].shape[1]), f32)]
    column = jnp.broadcast_to(gain.astype(f32)[:, None], (rows, 128))
    operands = pieces + list(weights) + [column]
    return pl.pallas_call(
        functools.partial(owned_kernel, size, layout, len(weights)),
        grid=(1,),
        in_specs=[pl.BlockSpec(memory_space=pltpu.SMEM)]
        + [resident(array.shape) for array in operands],
        out_specs=[resident(shape.shape) for shape in outs],
        out_shape=outs,
        compiler_params=pltpu.CompilerParams(vmem_limit_bytes=48 << 20),
        cost_estimate=BESIDE,
        name=name,
    )(me.reshape(1), *operands)


def join_kernel(*refs):
    put_rows(refs[-1], refs[:-1], lambda rows: rows)


def join(pieces, name):
    rows, width = sum(piece.shape[0] for piece in pieces), pieces[0].shape[1]
    return pl.pallas_call(
        join_kernel,
        grid=(1,),
        in_specs=[resident(piece.shape) for piece in pieces],
        out_specs=resident((rows, width)),
        out_shape=jax.ShapeDtypeStruct((rows, width), pieces[0].dtype),
        compiler_params=pltpu.CompilerParams(vmem_limit_bytes=32 << 20),
        cost_estimate=BESIDE,
        name=name,
    )(*pieces)


def hidden_kernel(first, cores, x_count, tiles, *refs):
    refs = list(refs)

    def pop(number):
        taken, refs[:number] = refs[:number], []
        return taken

    x_pieces = pop(x_count)
    g_all = pop(1)[0]
    x_all = x_pieces[0]
    weights = [pop(3) for _ in range(cores)]
    if first:
        x_all = pop(1)[0]
    grads_out, acts_out = pop(cores), pop(cores)
    step = pl.program_id(0)

    if first:

        @pl.when(step == 0)
        def _():
            put_rows(x_all, x_pieces, lambda rows: rows)

    def one_core(j):
        w_gate, w_up, w_down = (ref[...].reshape(-1, ref.shape[2]) for ref in weights[j])
        tile = w_gate.shape[1]
        place = step - j * tiles
        gate_place = pl.ds(pl.multiple_of(place * tile, tile), tile)
        up_place = pl.ds(pl.multiple_of((tiles + place) * tile, tile), tile)
        rows = x_all.shape[0] // 2
        for at in (slice(0, rows), slice(rows, None)):
            gate = dot(x_all[at], w_gate)
            up = dot(x_all[at], w_up)
            act_grad = dot(g_all[at], w_down)
            sigma = 1.0 / (1.0 + jnp.exp(-gate))
            silu = gate * sigma
            gate_grad = act_grad * up * sigma * (1.0 + gate * (1.0 - sigma))
            acts_out[j][at, gate_place] = (silu * up).astype(bf16)
            grads_out[j][at, gate_place] = gate_grad.astype(bf16)
            grads_out[j][at, up_place] = (act_grad * silu).astype(bf16)

    for j in range(cores):
        pl.when((step >= j * tiles) & (step < (j + 1) * tiles))(functools.partial(one_core, j))


def hidden_call(x_pieces, g_all, weights, name):
    cores, first = len(weights), len(x_pieces) > 1
    data, near, columns = weights[0].shape
    width = data * near
    units = columns // 3
    tile = min(256, units)
    tiles = units // tile
    rows = sum(piece.shape[0] for piece in x_pieces)

    def weight_specs(j):
        return [
            pl.BlockSpec(
                (data, near, tile),
                lambda i, k=k: (0, 0, k * tiles + jnp.clip(i - j * tiles, 0, tiles - 1)),
            )
            for k in range(3)
        ]

    operands = list(x_pieces) + [g_all]
    in_specs = [resident(array.shape) for array in operands]
    for j, weight in enumerate(weights):
        in_specs += weight_specs(j)
        operands += [weight] * 3
    shapes = [jax.ShapeDtypeStruct((rows, width), bf16)] if first else []
    shapes += [jax.ShapeDtypeStruct((rows, 2 * units), bf16)] * cores
    shapes += [jax.ShapeDtypeStruct((rows, units), bf16)] * cores
    got = pl.pallas_call(
        functools.partial(
            hidden_kernel, first, cores, len(x_pieces), tiles
        ),
        grid=(cores * tiles,),
        in_specs=in_specs,
        out_specs=[resident(shape.shape) for shape in shapes],
        out_shape=shapes,
        compiler_params=pltpu.CompilerParams(vmem_limit_bytes=60 << 20),
        cost_estimate=BESIDE,
        name=name,
    )(*operands)
    got = list(got)
    whole, got = (got[0], got[1:]) if first else (x_pieces[0], got)
    return whole, got[:cores], got[cores:]


def phase(always, body):
    def never():
        return jax.tree.map(lambda leaf: jnp.zeros(leaf.shape, leaf.dtype), jax.eval_shape(body))

    return lax.cond(always, body, never)


def trade(block, axis, step):
    return lax.ppermute(block, axis, [(i, i ^ step) for i in range(lax.axis_size(axis))])


def halves(rows):
    middle = rows.shape[0] // 2
    return [rows[:middle], rows[middle:]]


def spread_near(own):
    if lax.axis_size("model") == 1:
        return list(own)
    return list(own) + [trade(half, "model", k) for k in (1, 2) for half in own]


def spread_far(near, *first):
    if len(near) == 2:
        return []
    upper, lower = near[2], near[5]
    if first:
        upper, lower = after((upper, lower), *first)
    return [trade(upper, "model", 2), trade(lower, "model", 1)]


def send_near(near, far):
    x_upper, x_lower, y_upper, y_lower = near
    x_upper, y_lower = after((x_upper, y_lower), *far)
    y_upper = (y_upper.astype(f32) + far[0].astype(f32)).astype(bf16)
    x_lower = (x_lower.astype(f32) + far[1].astype(f32)).astype(bf16)
    return [
        trade(x_upper, "model", 1),
        trade(y_upper, "model", 2),
        trade(x_lower, "model", 1),
        trade(y_lower, "model", 2),
    ]


def swap(piece_of):
    me = lax.axis_index("model")
    others = range(1, lax.axis_size("model"))
    return [piece_of(me)] + [trade(piece_of(me ^ k), "model", k) for k in others]


def take(array, index, count):
    size = array.shape[1] // count
    return lax.dynamic_slice_in_dim(array, index * size, size, 1)


def rows_at(array):
    return lambda i: lax.dynamic_index_in_dim(array, i, 0, keepdims=False)


def in_order(pieces):
    me = lax.axis_index("model")
    size = len(pieces)
    return jnp.stack(
        [lax.select_n(me, *[pieces[j ^ i] for j in range(size)]) for i in range(size)]
    )


def after(value, *first):
    return lax.optimization_barrier((value,) + first)[0]


def on_device(
    hidden_in,
    out_grad,
    segments,
    positions,
    w_query,
    key_weight,
    value_weight,
    w_output,
    w_gate,
    w_up,
    w_down,
    attn_gain,
    mlp_gain,
    query_gain,
    key_gain,
):
    data = lax.axis_size("data")
    model = lax.axis_size("model")
    cores = lax.axis_size("tp")
    core = lax.axis_index("tp")
    seq_len = positions.shape[0]
    half = seq_len // cores
    shard = w_query.shape[0]
    width = hidden_in.shape[1]
    head_size = query_gain.shape[0] * data * model
    q_heads = w_query.shape[1] // model // head_size
    kv_heads = key_weight.shape[1] // model // head_size
    repeat = q_heads // kv_heads
    q_cols = q_heads * head_size
    kv_cols = kv_heads * head_size
    cols = q_cols + 2 * kv_cols
    wide = cols + q_cols
    ff = w_gate.shape[1] // model
    always = (segments[0] * segments[0] + segments[0]) % 2 == 0

    small = jnp.concatenate([attn_gain, mlp_gain, query_gain, key_gain])
    small_rows = -(-small.shape[0] // wide)
    place_rows = -(-seq_len // wide)

    def as_rows(vector, rows):
        return jnp.pad(vector, (0, rows * wide - vector.shape[0])).reshape(rows, wide)

    extra = jnp.concatenate(
        [
            as_rows(small, small_rows),
            as_rows(segments.astype(bf16), place_rows),
            as_rows((positions // 8).astype(bf16), place_rows),
            as_rows((positions % 8).astype(bf16), place_rows),
        ]
    )
    extra = jnp.pad(extra, ((0, -extra.shape[0] % 16), (0, 0)))
    turned_output = w_output.T

    def attn_piece(i):
        parts = [
            take(w_query, i, model),
            take(key_weight, i, model),
            take(value_weight, i, model),
            take(turned_output, i, model),
        ]
        return jnp.concatenate([jnp.concatenate(parts, axis=1), extra])

    turned_down = w_down.T
    chunks = [ff - ff // 3, ff // 3] if ff % 768 == 0 else [ff]
    starts = [sum(chunks[:c]) for c in range(len(chunks))]

    def over_data(pieces):
        return lax.all_gather(pieces, "data", axis=0, tiled=False)

    attn_got = swap(attn_piece)
    tied = lax.optimization_barrier((halves(hidden_in), halves(out_grad), attn_got))
    grad_halves = tied[1]
    x_near = spread_near(tied[0])
    tied = lax.optimization_barrier((w_gate, w_up, turned_down, x_near))
    w_gate_sent, w_up_sent, turned_down, x_near = tied
    x_blocks = x_near + spread_far(x_near)
    mlp_got = swap(
        lambda i: jnp.concatenate(
            [
                take(weight, i, model)[:, first : first + count]
                for first, count in zip(starts, chunks)
                for weight in (w_gate_sent, w_up_sent, turned_down)
            ],
            axis=1,
        )
    )

    def places_of(first):
        rows = [
            got[shard + first : shard + first + place_rows].reshape(-1)[:seq_len]
            for got in attn_got
        ]
        return jnp.stack(rows).astype(f32)

    seg_all = places_of(small_rows)
    pos_all = 8.0 * places_of(small_rows + place_rows) + places_of(small_rows + 2 * place_rows)
    cosine, sine = tables(pos_all, head_size)

    attn_near = in_order(attn_got)
    gain_rows = attn_near[:, shard : shard + small_rows].reshape(-1, wide)
    gain_rows = jnp.pad(gain_rows, ((0, -gain_rows.shape[0] % 16), (0, 0)))
    near = jnp.concatenate([attn_near[:, :shard].reshape(-1, wide), gain_rows])
    me = lax.axis_index("model")
    mlp_near = near_call(me, mlp_got, [3 * count for count in chunks], "hidden_exchange")
    attn_full = over_data(near)
    tied = lax.optimization_barrier((attn_full, mlp_near, x_blocks, cosine, sine))
    attn_full, mlp_near, x_blocks, cosine, sine = tied
    mlp_full = [over_data(piece) for piece in mlp_near]

    gains = attn_full[:, model * shard : model * shard + model * small_rows]
    gains = gains.reshape(data * model, -1).astype(f32)
    part = query_gain.shape[0]
    gain_in = gains[:, :shard].reshape(-1)
    gain_mid = gains[:, shard : 2 * shard].reshape(-1)
    gain_query = gains[:, 2 * shard : 2 * shard + part].reshape(-1)
    gain_key = gains[:, 2 * shard + part : 2 * shard + 2 * part].reshape(-1)
    def with_cores(weight):
        return [weight] + [trade(weight, "tp", j) for j in range(1, cores)]

    near_rows = model * shard
    grad_near = spread_near(after(grad_halves, *x_blocks, *mlp_near))

    seg_rows = jnp.pad(seg_all[:, None], ((0, 0), (0, 7), (0, 0)))
    seg_columns = seg_all[:, :, None]
    head_gains = jnp.pad(jnp.stack([gain_query, gain_key]), ((0, 6), (0, 0)))
    shared = [cosine, sine, seg_columns, seg_rows]
    o_place = [cols // q_cols] * cores

    def product_phase():
        w_attn = with_cores(attn_full)
        normed_in, first_raw = rows_product(
            x_blocks, gain_in, w_attn[:1], cols, 0, near_rows, f32, "query_key_value"
        )
        raw = [first_raw[0].reshape(model, half, cols)]
        for j in range(1, cores):
            mine = rows_product(
                [normed_in], None, [w_attn[j]], cols, 0, near_rows, f32, "query_key_value_other"
            )[1][0]
            raw.append(trade(mine, "tp", j).reshape(model, half, cols))
        return w_attn[1:], normed_in, raw

    w_others, own_normed, raw = phase(always, product_phase)
    w_attn = [attn_full] + w_others
    raw, grad_near = lax.optimization_barrier((raw, grad_near))

    def attention_phase():
        far = spread_far(grad_near)
        attended = attention_call(
            functools.partial(attend_kernel, cores, kv_heads, repeat),
            "attend",
            core,
            raw,
            shared,
            head_gains,
            [jax.ShapeDtypeStruct((model, half, q_cols), bf16)] * cores,
            [],
            [((seq_len, cols), f32), ((seq_len, q_cols), bf16)],
        )
        attended, far = lax.optimization_barrier((list(attended), far))
        got = [trade(attended[j], "tp", j) for j in range(1, cores)]
        return with_cores(own_normed)[1:], got, attended, far

    normed_others, got, attended, grad_far = phase(always, attention_phase)
    att_flat = [piece.reshape(-1, q_cols) for piece in [attended[0]] + got]
    normed_in = [own_normed] + normed_others
    grad_blocks = grad_near + grad_far

    def data_sum(total):
        return lax.psum_scatter(total, "data", scatter_dimension=0, tiled=False)

    def out_phase():
        own, _, got = project_and_send(
            att_flat, w_attn, o_place, half, near_rows, "attention_out"
        )
        own_grad = join(after(grad_blocks, own), "out_grad_rows")
        middle, *low = rows_call("norm", own, hidden_in, got, gain_mid, None, True, "middle")
        near = spread_near(low)
        return middle, near + spread_far(near), own_grad

    middle, mid_blocks, own_grad = phase(always, out_phase)

    def for_own_core(rows):
        return [
            [rows[k][0]] + [trade(rows[k][j], "tp", j) for j in range(1, cores)] for k in range(2)
        ]

    def hidden_weights(kept, rows, name):
        groups = [[(kept[k][j], rows[k][j]) for j in range(cores)] for k in range(2)]
        return weight_grad(groups, [], (), near_rows, name)

    def first_phase():
        weights = with_cores(mlp_full[0])
        whole, *by_core = hidden_call(mid_blocks, own_grad, weights[:1], "hidden_units_a")
        normed_mid, grad_all = with_cores(whole), with_cores(own_grad)
        by_core = [by_core]
        for weight in weights[1:]:
            got = hidden_call([whole], own_grad, [weight], "hidden_units_a_other")
            by_core.append(got[1:])
        first_rows = [[got[k][0] for got in by_core] for k in range(2)]
        kept = [normed_mid, grad_all]
        total = hidden_weights(kept, for_own_core(first_rows), "hidden_weights_a")
        return weights[1:], normed_mid, grad_all[1:], first_rows, total

    other_weights, normed_mid, grad_others, first_rows, total = phase(always, first_phase)
    kept = [normed_mid, [own_grad] + grad_others]
    w_mlp = [[mlp_full[0]] + other_weights]
    mlp_sums = []
    if len(chunks) > 1:
        mlp_sums.append(data_sum(total))
    count = cores * len(chunks)

    def hidden_phase():
        rows, weights = [first_rows], list(w_mlp)
        if len(chunks) > 1:
            weights.append(with_cores(mlp_full[1]))
            by_core = [
                hidden_call([normed_mid[0]], own_grad, [weight], "hidden_units_b")[1:]
                for weight in weights[1]
            ]
            rows.append([[got[k][0] for got in by_core] for k in range(2)])
        both_cores = [w for pair in weights for w in pair]
        own, _, got = project_and_send(
            [grads for pair in rows for grads in pair[0]],
            both_cores,
            [0] * count,
            half,
            near_rows,
            "normed_mid_grad",
        )
        last_rows = after(for_own_core(rows[-1]), own)
        total = hidden_weights(kept, last_rows, "hidden_weights_b")
        acts = [acts for pair in rows for acts in pair[1]]
        return own, got, total, acts, [w for pair in weights[1:] for w in pair[1:]]

    mid_part, mid_got, total, act_rows, other_weights = phase(always, hidden_phase)
    if len(chunks) > 1:
        mlp_sums.append(data_sum(total))
        w_mlp.append([mlp_full[1]] + other_weights)
    both_cores = [w for pair in w_mlp for w in pair]

    def branch_phase():
        middle_grad, *low = rows_call(
            "back", mid_part, middle, mid_got, gain_mid, out_grad, True, "middle_grad"
        )
        down_parts = project(
            act_rows, both_cores, [2] * count, 0, [half] * model, near_rows, "hidden_out"
        )
        near = spread_near(low)
        branch_blocks = near + spread_far(near, *down_parts)
        return middle_grad, branch_blocks, down_parts

    middle_grad, branch_blocks, down_parts = phase(always, branch_phase)
    tied = lax.optimization_barrier((branch_blocks, down_parts, mlp_sums[0]))
    branch_blocks, down_parts, mlp_sums[0] = tied
    down_got = [trade(down_parts[k], "model", k) for k in range(1, model)]

    def attend_back_phase():
        branch, products = rows_product(
            branch_blocks, None, w_attn, q_cols, o_place[0], near_rows, bf16, "attended_grad"
        )
        products = [piece.reshape(model, half, q_cols) for piece in products]
        att_grads = [trade(piece, "tp", j) if j else piece for j, piece in enumerate(products)]
        *qkv_back, head_grads = attention_call(
            functools.partial(attend_back_kernel, cores, kv_heads, repeat),
            "attend_back",
            core,
            raw + att_grads,
            shared,
            head_gains,
            [jax.ShapeDtypeStruct((model, half, cols), bf16)] * cores,
            [jax.ShapeDtypeStruct(head_gains.shape, f32)],
            [
                ((seq_len, cols), f32),
                ((seq_len, q_cols), bf16),
                ((seq_len, cols), f32),
                ((seq_len, cols), bf16),
            ],
        )
        return with_cores(branch), list(qkv_back), head_grads

    branch, qkv_back, head_grads = phase(always, attend_back_phase)

    def attention_weights_phase():
        back_pieces = [qkv_back[0]] + [trade(qkv_back[j], "tp", j) for j in range(1, cores)]
        ride = head_grads[:2].reshape(-1)
        ride = jnp.pad(ride, (0, ride_rows * wide - ride.shape[0])).astype(bf16)
        ride = jnp.pad(ride.reshape(ride_rows, wide), ((0, -ride_rows % 16), (0, 0)))
        groups = [
            [(normed_in[j], qkv_back[j].reshape(-1, cols)) for j in range(cores)],
            [(branch[j], attended[j].reshape(-1, q_cols)) for j in range(cores)],
        ]
        attn_total = weight_grad(groups, [], [ride], near_rows, "attention_weights")
        return attn_total, [piece.reshape(-1, cols) for piece in back_pieces]

    ride_rows = -(-2 * head_size // wide)
    attn_total, back_flat = phase(always, attention_weights_phase)
    attn_total, down_got = lax.optimization_barrier((attn_total, down_got))
    attn_sum = data_sum(attn_total)
    def in_grad_phase():
        return project_and_send(
            back_flat, w_attn, [0] * cores, half, near_rows, "normed_in_grad", False
        )

    in_part, in_far, in_near = phase(always, in_grad_phase)
    in_near, sums = lax.optimization_barrier((in_near, mlp_sums))

    def last_phase():
        in_got = send_near(in_near, in_far) if model > 1 else []
        rows = jnp.concatenate([total.reshape(model, shard, -1) for total in sums], axis=2)
        mlp_got = swap(rows_at(after(rows, *in_got)))
        hidden_out = rows_call(
            "sum", down_parts[0], middle, after(down_got, *in_got), None, None, False, "hidden_out_sum"
        )[0]
        grad_in = rows_call(
            "back", in_part, hidden_in, in_got, gain_in, middle_grad, False, "grad_in"
        )[0]
        return hidden_out, grad_in, mlp_got

    hidden_out, grad_in, mlp_got = phase(always, last_phase)
    attn_sum = after(attn_sum, grad_in)
    weight_rows = attn_sum[:near_rows].reshape(model, shard, wide)
    gain_row = attn_sum[near_rows:]
    gain_row = jnp.broadcast_to(gain_row, (model,) + gain_row.shape)
    attn_rows = jnp.concatenate([weight_rows, gain_row], axis=1)
    attn_got = swap(rows_at(attn_rows))
    layout = [
        [
            (kind, first, ff, size, kind == 2)
            for first, size in zip(starts, chunks)
            for kind in range(3)
        ]
    ]
    shapes = [w_gate.shape, w_up.shape, w_down.shape]
    mlp_got = after(mlp_got, attn_rows)
    owned = owned_call(
        me, [mlp_got], layout, [w_gate, w_up], mlp_gain, shapes, "hidden_owned"
    )
    grad_gate, grad_up, grad_down, mlp_part = owned[:4]
    layout = [
        [
            (0, 0, q_cols, q_cols, False),
            (1, 0, kv_cols, kv_cols, False),
            (2, 0, kv_cols, kv_cols, False),
            (3, 0, q_cols, q_cols, True),
        ]
    ]
    weights = [w_query, key_weight, value_weight]
    shapes = [weight.shape for weight in weights] + [w_output.shape]
    owned = owned_call(me, [attn_got], layout, weights, attn_gain, shapes, "attention_owned")
    grad_query, grad_key, grad_value, grad_output, attn_part, gain_sums = owned
    gain_sums = gain_sums[:ride_rows].reshape(-1)[: 2 * head_size]
    sums = lax.psum(jnp.concatenate([attn_part[:, 0], mlp_part[:, 0], gain_sums]), "tp")
    where = lax.axis_index("data") * model + lax.axis_index("model")
    first = 2 * shard + where * part
    return (
        hidden_out,
        grad_in,
        grad_query,
        grad_key,
        grad_value,
        grad_output,
        grad_gate,
        grad_up,
        grad_down,
        sums[:shard],
        sums[shard : 2 * shard],
        lax.dynamic_slice_in_dim(sums, first, part),
        lax.dynamic_slice_in_dim(sums, first + head_size, part),
    )


def solution(mesh):
    fsdp, tp = mesh.shape["fsdp"], mesh.shape["tp"]
    model = 4 if fsdp % 4 == 0 else 1
    split = Mesh(mesh.devices.reshape(fsdp // model, model, tp), ("data", "model", "tp"))
    batch = ("data", "model")
    rows = P(("data", "model", "tp"), None)
    into = P(batch, "tp")
    back = P("tp", batch)
    in_specs = (rows, rows, P(batch), P(batch), into, into, into, back, into, into, back)
    in_specs = in_specs + (P(batch),) * 4
    out_specs = (rows, rows, into, into, into, back, into, into, back) + (P(batch),) * 4
    return jax.shard_map(
        on_device, mesh=split, in_specs=in_specs, out_specs=out_specs, check_vma=False
    )
```

```python
import functools

import jax
import jax.numpy as jnp
from jax import lax
from jax.experimental import pallas as pl
from jax.experimental.pallas import tpu as pltpu
from jax.sharding import Mesh, PartitionSpec as P

epsilon = 1e-06
rope_base = 1000000.0
bf16 = jnp.bfloat16
f32 = jnp.float32
BESIDE = pl.CostEstimate(flops=1 << 20, bytes_accessed=1 << 16, transcendentals=0)


def dot(left, right):
    return jnp.dot(left, right, preferred_element_type=f32)


def dot_right_t(left, right):
    return lax.dot_general(left, right, (((1,), (1,)), ((), ())), preferred_element_type=f32)


def dot_left_t(left, right):
    return lax.dot_general(left, right, (((0,), (0,)), ((), ())), preferred_element_type=f32)


def normalize(operand, norm_gain):
    return (
        operand
        * lax.rsqrt(jnp.mean(operand * operand, axis=-1, keepdims=True) + epsilon)
        * norm_gain
    )


def norm_back(operand, norm_gain, upstream):
    factor = lax.rsqrt(jnp.mean(operand * operand, axis=-1, keepdims=True) + epsilon)
    weighted = upstream * norm_gain
    inner = jnp.mean(weighted * operand, axis=-1, keepdims=True)
    return factor * weighted - operand * factor * factor * factor * inner


def tables(positions, head_size):
    indices = jnp.arange(head_size // 2).astype(f32)
    frequency = rope_base ** (-2.0 * indices / head_size)
    angles = positions.astype(f32)[..., None] * frequency
    cosine, sine = jnp.cos(angles), jnp.sin(angles)
    return (jnp.concatenate([cosine, cosine], -1), jnp.concatenate([-sine, sine], -1))


def half_turn(operand):
    return pltpu.roll(operand, operand.shape[-1] // 2, 1)


def lay_in_order(scratch, refs, core):
    half = refs[0].shape[1]
    for j, ref in enumerate(refs):
        scratch[pl.ds(pl.multiple_of((core ^ j) * half, half), half)] = ref[0]


def head_rows(raw, heads, repeat, gains, cosine, sine):
    size = gains.shape[1]

    def turned(column, gain):
        rows = normalize(raw[:, column * size : (column + 1) * size], gain)
        return (rows * cosine + half_turn(rows) * sine).astype(bf16)

    queries = [turned(h, gains[0:1]) for h in range(heads * repeat)]
    keys = [turned(heads * repeat + g, gains[1:2]) for g in range(heads)]
    first = heads * repeat + heads
    values = [
        raw[:, (first + g) * size : (first + g + 1) * size].astype(bf16) for g in range(heads)
    ]
    return queries, keys, values


def masked_probs(key, query, allowed):
    scores = dot_right_t(key, query) * query.shape[1] ** (-0.5)
    scores = jnp.where(allowed, scores, -1e30)
    exp_terms = jnp.exp(scores - jnp.max(scores, axis=0, keepdims=True))
    return exp_terms * (1.0 / jnp.sum(exp_terms, axis=0, keepdims=True))


def query_strips(rows, column_ref, row_ref):
    step = min(256, rows)
    for first in range(0, rows, step):
        seen = first + step
        keys = lax.broadcasted_iota(jnp.int32, (seen, step), 0)
        queries = lax.broadcasted_iota(jnp.int32, (seen, step), 1) + first
        same = column_ref[0, :seen, 0:1] == row_ref[0, 0:1, first:seen]
        yield slice(first, seen), seen, same & (keys <= queries)


def attend_kernel(cores, heads, repeat, core_ref, *refs):
    raws, refs = refs[:cores], refs[cores:]
    cos_ref, sin_ref, column_ref, row_ref, gain_ref = refs[:5]
    outs, raw, rows_out = refs[5:-2], refs[-2], refs[-1]
    core = core_ref[0]
    half = raws[0].shape[1]
    lay_in_order(raw, raws, core)
    queries, keys, values = head_rows(
        raw, heads, repeat, gain_ref[...], cos_ref[0], sin_ref[0]
    )
    size = gain_ref.shape[1]
    turned = [value.astype(f32).T.astype(bf16) for value in values]
    for at, seen, allowed in query_strips(raw.shape[0], column_ref, row_ref):
        for h, query in enumerate(queries):
            g = h // repeat
            probs = masked_probs(keys[g][:seen], query[at], allowed).astype(bf16)
            rows = dot(turned[g][:, :seen], probs).T
            rows_out[at, h * size : (h + 1) * size] = rows.astype(bf16)
    for j, out in enumerate(outs):
        out[0] = rows_out[pl.ds(pl.multiple_of((core ^ j) * half, half), half)]


def attend_back_kernel(cores, heads, repeat, core_ref, *refs):
    raws, grads, refs = refs[:cores], refs[cores : 2 * cores], refs[2 * cores :]
    cos_ref, sin_ref, column_ref, row_ref, gain_ref = refs[:5]
    outs, gain_out = refs[5 : 5 + cores], refs[5 + cores]
    raw, grad, totals, rows_out = refs[6 + cores :]
    core = core_ref[0]
    half = raws[0].shape[1]
    cosine, sine, gains = cos_ref[0], sin_ref[0], gain_ref[...]
    lay_in_order(raw, raws, core)
    lay_in_order(grad, grads, core)
    queries, keys, values = head_rows(raw, heads, repeat, gains, cosine, sine)
    size = gains.shape[1]
    scale = size ** (-0.5)
    count = heads * repeat

    @pl.when(pl.program_id(0) == 0)
    def _():
        gain_out[...] = jnp.zeros_like(gain_out)

    def columns(i):
        return slice(i * size, (i + 1) * size)

    turned_keys = [key.astype(f32).T.astype(bf16) for key in keys]
    totals[:, count * size :] = jnp.zeros_like(totals[:, count * size :])
    for at, seen, allowed in query_strips(raw.shape[0], column_ref, row_ref):
        for g in range(heads):
            key_grad = value_grad = None
            for h in range(g * repeat, (g + 1) * repeat):
                probs = masked_probs(keys[g][:seen], queries[h][at], allowed)
                out_grad = grad[at, columns(h)]
                prob_grad = dot_right_t(values[g][:seen], out_grad)
                delta = jnp.sum(probs * prob_grad, axis=0, keepdims=True)
                score_grad = (probs * (prob_grad - delta)).astype(bf16)
                totals[at, columns(h)] = dot(turned_keys[g][:, :seen], score_grad).T * scale
                key_part = dot(score_grad, queries[h][at])
                value_part = dot(probs.astype(bf16), out_grad)
                key_grad = key_part if key_grad is None else key_grad + key_part
                value_grad = value_part if value_grad is None else value_grad + value_part
            totals[:seen, columns(count + g)] += key_grad * scale
            totals[:seen, columns(count + heads + g)] += value_grad
    for i in range(count + heads):
        row = 0 if i < count else 1
        upstream = totals[:, columns(i)]
        turned = upstream * cosine - half_turn(upstream) * sine
        rows = raw[:, columns(i)]
        factor = lax.rsqrt(jnp.mean(rows * rows, axis=-1, keepdims=True) + epsilon)
        gain_out[row : row + 1] += jnp.sum(turned * rows * factor, axis=0, keepdims=True)
        back = norm_back(rows, gains[row : row + 1], turned)
        rows_out[:, columns(i)] = back.astype(bf16)
    rows_out[:, (count + heads) * size :] = totals[:, (count + heads) * size :].astype(bf16)
    for j, out in enumerate(outs):
        out[0] = rows_out[pl.ds(pl.multiple_of((core ^ j) * half, half), half)]


def attention_call(kernel, name, core, halves, shared, gains, outs, extra_out, scratch):
    def per_sequence(array):
        return pl.BlockSpec((1,) + array.shape[1:], lambda i: (i, 0, 0))

    whole = pl.BlockSpec(gains.shape, lambda i: (0, 0))
    out_specs = [per_sequence(shape) for shape in outs] + [
        pl.BlockSpec(shape.shape, lambda i: (0, 0)) for shape in extra_out
    ]
    return pl.pallas_call(
        kernel,
        grid=(halves[0].shape[0],),
        in_specs=[pl.BlockSpec(memory_space=pltpu.SMEM)]
        + [per_sequence(array) for array in halves + shared]
        + [whole],
        out_specs=out_specs,
        out_shape=outs + extra_out,
        scratch_shapes=[pltpu.VMEM(shape, dtype) for shape, dtype in scratch],
        compiler_params=pltpu.CompilerParams(vmem_limit_bytes=48 << 20),
        cost_estimate=BESIDE,
        name=name,
    )(core.reshape(1), *halves, *shared, gains)


def resident(shape):
    zeros = (0,) * len(shape)
    return pl.BlockSpec(shape, lambda i: zeros, pipeline_mode=pl.Buffered(1))


def project_kernel(count, *refs):
    lefts, rights, outs = refs[:count], refs[count : 2 * count], refs[2 * count :]

    total = dot_right_t(lefts[0][...], rights[0][0])
    for left, right in zip(lefts[1:], rights[1:]):
        total = total + dot_right_t(left[...], right[0])
    first = 0
    for out in outs:
        out[...] = total[first : first + out.shape[0]].astype(out.dtype)
        first += out.shape[0]


def project(lefts, rights, places, first, sizes, step, name):
    parts = rights[0].shape[0]
    rows = sum(sizes)

    def left_spec(left):
        return pl.BlockSpec(
            (rows, left.shape[1]), lambda i: (first // rows, 0), pipeline_mode=pl.Buffered(1)
        )

    def right_spec(left, place):
        return pl.BlockSpec((1, step, left.shape[1]), lambda i: (i, 0, place))

    return list(
        pl.pallas_call(
            functools.partial(project_kernel, len(lefts)),
            grid=(parts,),
            in_specs=[left_spec(left) for left in lefts]
            + [right_spec(left, place) for left, place in zip(lefts, places)],
            out_specs=[pl.BlockSpec((size, step), lambda i: (0, i)) for size in sizes],
            out_shape=[
                jax.ShapeDtypeStruct((size, parts * step), bf16 if first or k else f32)
                for k, size in enumerate(sizes)
            ],
            compiler_params=pltpu.CompilerParams(vmem_limit_bytes=56 << 20),
            cost_estimate=BESIDE,
            name=name,
        )(*lefts, *rights)
    )


def project_and_send(lefts, rights, places, rows, step, name, near_too=True):
    if lax.axis_size("model") == 1:
        return project(lefts, rights, places, 0, [rows], step, name)[0], [], []
    half = rows // 2
    far = project(lefts, rights, places, 3 * rows, [half] * 2, step, name + "_far")
    got = [trade(far[0], "model", 1), trade(far[1], "model", 2)]
    own, *near = project(lefts, rights, places, 0, [rows] + [half] * 4, step, name)
    return own, got, send_near(near, got) if near_too else near


def put_rows(whole, pieces, change):
    first = 0
    for piece in pieces:
        whole[first : first + piece.shape[0]] = change(piece[...])
        first += piece.shape[0]


def rows_kernel(kind, count, *refs):
    (own, base), got, refs = refs[:2], refs[2 : 2 + count], list(refs[2 + count :])
    total = own[...]
    if count == 4:
        upper = got[0][...].astype(f32) + got[1][...].astype(f32)
        lower = got[2][...].astype(f32) + got[3][...].astype(f32)
        total += jnp.where(pl.program_id(0) == 0, upper, lower)
    else:
        for piece in got:
            total += piece[...].astype(f32)
    rows = base[...].astype(f32)
    if kind == "sum":
        refs[0][...] = (rows + total).astype(bf16)
        return
    gain = refs[0][...]
    if kind == "norm":
        whole, *low = refs[1:]
        total = rows + total
        sent = normalize(total, gain)
    else:
        more, whole, *low = refs[1:]
        total = more[...].astype(f32) + norm_back(rows, gain, total)
        sent = total
    whole[...] = total
    for place, half in enumerate(low):

        @pl.when(pl.program_id(0) == place)
        def _():
            half[...] = sent.astype(bf16)


def rows_call(kind, own, base, got, gain, more, sent, name):
    rows, width = own.shape
    step = rows // 2
    strip = pl.BlockSpec((step, width), lambda i: (i, 0))
    half = resident((step, width))
    operands = [own, base] + list(got)
    in_specs = [strip, strip] + [half if len(got) == 4 else strip] * len(got)
    if gain is not None:
        operands.append(gain.reshape(1, width))
        in_specs.append(resident((1, width)))
    if more is not None:
        operands.append(more)
        in_specs.append(strip)
    out_specs, shapes = [strip], [jax.ShapeDtypeStruct((rows, width), bf16 if gain is None else f32)]
    if sent:
        out_specs += [half] * 2
        shapes += [jax.ShapeDtypeStruct((step, width), bf16)] * 2
    return list(
        pl.pallas_call(
            functools.partial(rows_kernel, kind, len(got)),
            grid=(2,),
            in_specs=in_specs,
            out_specs=out_specs,
            out_shape=shapes,
            compiler_params=pltpu.CompilerParams(vmem_limit_bytes=48 << 20),
            cost_estimate=BESIDE,
            name=name,
        )(*operands)
    )


def rows_product_kernel(count, normed, number, *refs):
    pieces, refs = refs[:count], list(refs[count:])
    gain = None
    if normed:
        source = refs.pop(0)
        gain = source[...]
        if len(source.shape) == 3:
            size = pieces[0].shape[1] // (source.shape[0] * normed)
            parts = [
                gain[i, j : j + 1, :size] for i in range(source.shape[0]) for j in range(normed)
            ]
            gain = jnp.concatenate(parts, axis=1).astype(f32)
    weights, refs = refs[:number], refs[number:]
    whole = pieces[0]
    if count > 1 or normed:
        whole = refs.pop(0)

        def change(rows):
            return normalize(rows.astype(f32), gain).astype(bf16) if normed else rows

        put_rows(whole, pieces, change)
    for weight, out in zip(weights, refs):
        matrix = weight[...].reshape(-1, weight.shape[2])
        out[...] = dot(whole[...], matrix).astype(out.dtype)


def rows_product(pieces, gain, weights, block, place, step, dtype, name):
    rows = sum(piece.shape[0] for piece in pieces)
    parts, width = weights[0].shape[0], pieces[0].shape[1]
    joined = len(pieces) > 1 or gain is not None
    shapes = [jax.ShapeDtypeStruct((rows, width), bf16)] if joined else []
    shapes += [jax.ShapeDtypeStruct((rows, block), dtype)] * len(weights)
    gains, gain_specs, normed = [], [], int(gain is not None)
    if isinstance(gain, tuple):
        array, first, normed = gain
        gains = [array]
        gain_specs = [pl.BlockSpec((parts, 16, array.shape[2]), lambda i: (0, first // 16, 0))]
    elif normed:
        gains, gain_specs = [gain.reshape(1, -1)], [resident((1, gain.shape[0]))]
    got = pl.pallas_call(
        functools.partial(rows_product_kernel, len(pieces), normed, len(weights)),
        grid=(1,),
        in_specs=[resident(piece.shape) for piece in pieces]
        + gain_specs
        + [
            pl.BlockSpec(
                (parts, step, block), lambda i: (0, 0, place), pipeline_mode=pl.Buffered(1)
            )
        ]
        * len(weights),
        out_specs=[resident(shape.shape) for shape in shapes],
        out_shape=shapes,
        compiler_params=pltpu.CompilerParams(vmem_limit_bytes=56 << 20),
        cost_estimate=BESIDE,
        name=name,
    )(*pieces, *gains, *weights)
    return (got[0], list(got[1:])) if joined else (pieces[0], list(got))


def weight_grad_kernel(counts, number, *refs):
    count = sum(counts)
    lefts, rights, refs = refs[:count], refs[count : 2 * count], refs[2 * count :]
    received, below, out = refs[:number], refs[number:-1], refs[-1]
    rows = lefts[0].shape[1]
    first = pair = 0
    for size in counts:
        total = dot_left_t(lefts[pair][...], rights[pair][...])
        for i in range(pair + 1, pair + size):
            total = total + dot_left_t(lefts[i][...], rights[i][...])
        pair += size
        at = slice(first, first + total.shape[1])
        for block in received:
            total = total + block[0, :, at].astype(f32)
        out[0, :rows, at] = total.astype(bf16)
        first += total.shape[1]
    for block in below:
        out[0, rows:] = block[...]


def weight_grad(groups, received, below, step, name):
    pairs = [pair for group in groups for pair in group]
    rows, width = pairs[0][0].shape
    columns = sum(group[0][1].shape[1] for group in groups)
    deep = step + sum(block.shape[0] for block in below)
    return pl.pallas_call(
        functools.partial(
            weight_grad_kernel, [len(group) for group in groups], len(received)
        ),
        grid=(width // step,),
        in_specs=[pl.BlockSpec((rows, step), lambda i: (0, i))] * len(pairs)
        + [resident(right.shape) for _, right in pairs]
        + [pl.BlockSpec((1, step, columns), lambda i: (i, 0, 0))] * len(received)
        + [resident(block.shape) for block in below],
        out_specs=pl.BlockSpec((1, deep, columns), lambda i: (i, 0, 0)),
        out_shape=jax.ShapeDtypeStruct((width // step, deep, columns), bf16),
        compiler_params=pltpu.CompilerParams(vmem_limit_bytes=56 << 20),
        cost_estimate=BESIDE,
        name=name,
    )(*[left for left, _ in pairs], *[right for _, right in pairs], *received, *below)


def cut_kernel(size, parts, me_ref, *refs):
    arrays, below, outs = refs[:parts], refs[parts], refs[parts + 1 :]
    rows = outs[0].shape[0] - below.shape[0]
    for k, out in enumerate(outs):
        owner = me_ref[0] ^ k
        first = 0
        for array in arrays:
            if array.shape[0] == rows:
                wide = array.shape[1] // size
                block = array[:, pl.ds(pl.multiple_of(owner * wide, 128), wide)]
            else:
                wide = array.shape[0] // size
                block = array[pl.ds(pl.multiple_of(owner * wide, 128), wide)]
                block = block.astype(f32).T.astype(bf16)
            out[:rows, first : first + wide] = block
            first += wide
        out[rows:] = below[...]


def cut_call(me, size, arrays, below, name):
    rows = arrays[0].shape[0]
    columns = sum(
        array.shape[1 if array.shape[0] == rows else 0] // size for array in arrays
    )
    shape = jax.ShapeDtypeStruct((rows + below.shape[0], columns), bf16)
    return list(
        pl.pallas_call(
            functools.partial(cut_kernel, size, len(arrays)),
            grid=(1,),
            in_specs=[pl.BlockSpec(memory_space=pltpu.SMEM)]
            + [resident(array.shape) for array in list(arrays) + [below]],
            out_specs=[resident(shape.shape)] * size,
            out_shape=[shape] * size,
            compiler_params=pltpu.CompilerParams(vmem_limit_bytes=32 << 20),
            cost_estimate=BESIDE,
            name=name,
        )(me.reshape(1), *arrays, below)
    )


def rows_cut_kernel(size, rows, me_ref, source, *outs):
    for k, out in enumerate(outs):
        first = pl.multiple_of((me_ref[0] ^ k) * rows, rows)
        out[:rows] = source[pl.ds(first, rows)]
        out[rows:] = source[size * rows :]


def rows_cut_call(me, size, source, rows, name):
    deep = source.shape[0] - (size - 1) * rows
    shape = jax.ShapeDtypeStruct((deep, source.shape[1]), bf16)
    return list(
        pl.pallas_call(
            functools.partial(rows_cut_kernel, size, rows),
            grid=(1,),
            in_specs=[pl.BlockSpec(memory_space=pltpu.SMEM), resident(source.shape)],
            out_specs=[resident(shape.shape)] * size,
            out_shape=[shape] * size,
            compiler_params=pltpu.CompilerParams(vmem_limit_bytes=32 << 20),
            cost_estimate=BESIDE,
            name=name,
        )(me.reshape(1), source)
    )


def stack_kernel(size, below, me_ref, *refs):
    pieces, out = refs[:size], refs[size]
    rows = pieces[0].shape[0] - 16
    under = jnp.zeros((16, out.shape[1]), f32)
    place = lax.broadcasted_iota(jnp.int32, under.shape, 0)
    for k, piece in enumerate(pieces):
        owner = me_ref[0] ^ k
        out[pl.ds(pl.multiple_of(owner * rows, rows), rows)] = piece[:rows]
        more = piece[rows:].astype(f32)
        for i in range(below):
            under = jnp.where(place == owner * below + i, more[i : i + 1], under)
    out[size * rows :] = under.astype(bf16)


def stack_call(me, pieces, below, name):
    size = len(pieces)
    shape = jax.ShapeDtypeStruct(
        (size * (pieces[0].shape[0] - 16) + 16, pieces[0].shape[1]), bf16
    )
    return pl.pallas_call(
        functools.partial(stack_kernel, size, below),
        grid=(1,),
        in_specs=[pl.BlockSpec(memory_space=pltpu.SMEM)]
        + [resident(piece.shape) for piece in pieces],
        out_specs=resident(shape.shape),
        out_shape=shape,
        compiler_params=pltpu.CompilerParams(vmem_limit_bytes=32 << 20),
        cost_estimate=BESIDE,
        name=name,
    )(me.reshape(1), *pieces)


def near_kernel(size, widths, me_ref, *refs):
    pieces, outs = refs[:size], refs[size:]
    rows = pieces[0].shape[0]
    for k, piece in enumerate(pieces):
        at = pl.ds(pl.multiple_of((me_ref[0] ^ k) * rows, rows), rows)
        first = 0
        for out, width in zip(outs, widths):
            out[at] = piece[:, first : first + width]
            first += width


def near_call(me, pieces, widths, name):
    rows = len(pieces) * pieces[0].shape[0]
    shapes = [jax.ShapeDtypeStruct((rows, width), bf16) for width in widths]
    return list(
        pl.pallas_call(
            functools.partial(near_kernel, len(pieces), widths),
            grid=(1,),
            in_specs=[pl.BlockSpec(memory_space=pltpu.SMEM)]
            + [resident(piece.shape) for piece in pieces],
            out_specs=[resident(shape.shape) for shape in shapes],
            out_shape=shapes,
            compiler_params=pltpu.CompilerParams(vmem_limit_bytes=32 << 20),
            cost_estimate=BESIDE,
            name=name,
        )(me.reshape(1), *pieces)
    )


def owned_kernel(size, layout, weighted, me_ref, *refs):
    count = size * len(layout)
    pieces, refs = refs[:count], refs[count:]
    weights, gain, refs = refs[:weighted], refs[weighted], refs[weighted + 1 :]
    outs, sums, below = refs[:-2], refs[-2], refs[-1]
    rows = gain.shape[0]
    total = jnp.zeros((rows, 1), f32)
    under = None
    for c, ranges in enumerate(layout):
        for k in range(size):
            piece = pieces[c * size + k]
            owner = me_ref[0] ^ k
            first = 0
            for number, place, wide, count, turned in ranges:
                block = piece[:rows, first : first + count].astype(f32)
                first += count
                at = pl.ds(pl.multiple_of(owner * wide + place, 128), count)
                if turned:
                    outs[number][at] = block.T
                    continue
                outs[number][:, at] = block
                if number < weighted:
                    product = weights[number][:, at].astype(f32) * block
                    total = total + jnp.sum(product, axis=1, keepdims=True)
            if piece.shape[0] > rows:
                more = piece[rows : rows + 8].astype(f32)
                under = more if under is None else under + more
    sums[...] = jnp.broadcast_to(total / gain[:, 0:1], sums.shape)
    below[...] = jnp.zeros_like(below) if under is None else under


def owned_call(me, chunks, layout, weights, gain, shapes, name):
    size = len(chunks[0])
    pieces = [piece for chunk in chunks for piece in chunk]
    rows = gain.shape[0]
    outs = [jax.ShapeDtypeStruct(shape, f32) for shape in shapes]
    outs += [jax.ShapeDtypeStruct((rows, 128), f32)]
    outs += [jax.ShapeDtypeStruct((8, pieces[0].shape[1]), f32)]
    column = jnp.broadcast_to(gain.astype(f32)[:, None], (rows, 128))
    operands = pieces + list(weights) + [column]
    return pl.pallas_call(
        functools.partial(owned_kernel, size, layout, len(weights)),
        grid=(1,),
        in_specs=[pl.BlockSpec(memory_space=pltpu.SMEM)]
        + [resident(array.shape) for array in operands],
        out_specs=[resident(shape.shape) for shape in outs],
        out_shape=outs,
        compiler_params=pltpu.CompilerParams(vmem_limit_bytes=48 << 20),
        cost_estimate=BESIDE,
        name=name,
    )(me.reshape(1), *operands)


def join_kernel(*refs):
    put_rows(refs[-1], refs[:-1], lambda rows: rows)


def join(pieces, name):
    rows, width = sum(piece.shape[0] for piece in pieces), pieces[0].shape[1]
    return pl.pallas_call(
        join_kernel,
        grid=(1,),
        in_specs=[resident(piece.shape) for piece in pieces],
        out_specs=resident((rows, width)),
        out_shape=jax.ShapeDtypeStruct((rows, width), pieces[0].dtype),
        compiler_params=pltpu.CompilerParams(vmem_limit_bytes=32 << 20),
        cost_estimate=BESIDE,
        name=name,
    )(*pieces)


def hidden_kernel(first, cores, x_count, tiles, *refs):
    refs = list(refs)

    def pop(number):
        taken, refs[:number] = refs[:number], []
        return taken

    x_pieces = pop(x_count)
    g_all = pop(1)[0]
    x_all = x_pieces[0]
    weights = [pop(3) for _ in range(cores)]
    if first:
        x_all = pop(1)[0]
    grads_out, acts_out = pop(cores), pop(cores)
    step = pl.program_id(0)

    if first:

        @pl.when(step == 0)
        def _():
            put_rows(x_all, x_pieces, lambda rows: rows)

    def one_core(j):
        w_gate, w_up, w_down = (ref[...].reshape(-1, ref.shape[2]) for ref in weights[j])
        tile = w_gate.shape[1]
        place = step - j * tiles
        gate_place = pl.ds(pl.multiple_of(place * tile, tile), tile)
        up_place = pl.ds(pl.multiple_of((tiles + place) * tile, tile), tile)
        rows = x_all.shape[0] // 2
        for at in (slice(0, rows), slice(rows, None)):
            gate = dot(x_all[at], w_gate)
            up = dot(x_all[at], w_up)
            act_grad = dot(g_all[at], w_down)
            sigma = 1.0 / (1.0 + jnp.exp(-gate))
            silu = gate * sigma
            gate_grad = act_grad * up * sigma * (1.0 + gate * (1.0 - sigma))
            acts_out[j][at, gate_place] = (silu * up).astype(bf16)
            grads_out[j][at, gate_place] = gate_grad.astype(bf16)
            grads_out[j][at, up_place] = (act_grad * silu).astype(bf16)

    for j in range(cores):
        pl.when((step >= j * tiles) & (step < (j + 1) * tiles))(functools.partial(one_core, j))


def hidden_call(x_pieces, g_all, weights, name):
    cores, first = len(weights), len(x_pieces) > 1
    data, near, columns = weights[0].shape
    width = data * near
    units = columns // 3
    tile = min(256, units)
    tiles = units // tile
    rows = sum(piece.shape[0] for piece in x_pieces)

    def weight_specs(j):
        return [
            pl.BlockSpec(
                (data, near, tile),
                lambda i, k=k: (0, 0, k * tiles + jnp.clip(i - j * tiles, 0, tiles - 1)),
            )
            for k in range(3)
        ]

    operands = list(x_pieces) + [g_all]
    in_specs = [resident(array.shape) for array in operands]
    for j, weight in enumerate(weights):
        in_specs += weight_specs(j)
        operands += [weight] * 3
    shapes = [jax.ShapeDtypeStruct((rows, width), bf16)] if first else []
    shapes += [jax.ShapeDtypeStruct((rows, 2 * units), bf16)] * cores
    shapes += [jax.ShapeDtypeStruct((rows, units), bf16)] * cores
    got = pl.pallas_call(
        functools.partial(
            hidden_kernel, first, cores, len(x_pieces), tiles
        ),
        grid=(cores * tiles,),
        in_specs=in_specs,
        out_specs=[resident(shape.shape) for shape in shapes],
        out_shape=shapes,
        compiler_params=pltpu.CompilerParams(vmem_limit_bytes=60 << 20),
        cost_estimate=BESIDE,
        name=name,
    )(*operands)
    got = list(got)
    whole, got = (got[0], got[1:]) if first else (x_pieces[0], got)
    return whole, got[:cores], got[cores:]


def phase(always, body):
    def never():
        return jax.tree.map(lambda leaf: jnp.zeros(leaf.shape, leaf.dtype), jax.eval_shape(body))

    return lax.cond(always, body, never)


def trade(block, axis, step):
    return lax.ppermute(block, axis, [(i, i ^ step) for i in range(lax.axis_size(axis))])


def halves(rows):
    middle = rows.shape[0] // 2
    return [rows[:middle], rows[middle:]]


def spread_near(own):
    if lax.axis_size("model") == 1:
        return list(own)
    return list(own) + [trade(half, "model", k) for k in (1, 2) for half in own]


def spread_far(near, *first):
    if len(near) == 2:
        return []
    upper, lower = near[2], near[5]
    if first:
        upper, lower = after((upper, lower), *first)
    return [trade(upper, "model", 2), trade(lower, "model", 1)]


def send_near(near, far):
    x_upper, x_lower, y_upper, y_lower = near
    x_upper, y_lower = after((x_upper, y_lower), *far)
    y_upper = (y_upper.astype(f32) + far[0].astype(f32)).astype(bf16)
    x_lower = (x_lower.astype(f32) + far[1].astype(f32)).astype(bf16)
    return [
        trade(x_upper, "model", 1),
        trade(y_upper, "model", 2),
        trade(x_lower, "model", 1),
        trade(y_lower, "model", 2),
    ]


def swap(piece_of):
    me = lax.axis_index("model")
    others = range(1, lax.axis_size("model"))
    return [piece_of(me)] + [trade(piece_of(me ^ k), "model", k) for k in others]


def swap_pieces(pieces):
    return [pieces[0]] + [trade(pieces[k], "model", k) for k in range(1, len(pieces))]


def take(array, index, count):
    size = array.shape[1] // count
    return lax.dynamic_slice_in_dim(array, index * size, size, 1)


def rows_at(array):
    return lambda i: lax.dynamic_index_in_dim(array, i, 0, keepdims=False)


def after(value, *first):
    return lax.optimization_barrier((value,) + first)[0]


def on_device(
    hidden_in,
    out_grad,
    segments,
    positions,
    w_query,
    key_weight,
    value_weight,
    w_output,
    w_gate,
    w_up,
    w_down,
    attn_gain,
    mlp_gain,
    query_gain,
    key_gain,
):
    data = lax.axis_size("data")
    model = lax.axis_size("model")
    cores = lax.axis_size("tp")
    core = lax.axis_index("tp")
    seq_len = positions.shape[0]
    half = seq_len // cores
    shard = w_query.shape[0]
    width = hidden_in.shape[1]
    head_size = query_gain.shape[0] * data * model
    q_heads = w_query.shape[1] // model // head_size
    kv_heads = key_weight.shape[1] // model // head_size
    repeat = q_heads // kv_heads
    q_cols = q_heads * head_size
    kv_cols = kv_heads * head_size
    cols = q_cols + 2 * kv_cols
    wide = cols + q_cols
    ff = w_gate.shape[1] // model
    always = (segments[0] * segments[0] + segments[0]) & 1 == 0

    small = jnp.concatenate([attn_gain, mlp_gain, query_gain, key_gain])
    small_rows = -(-small.shape[0] // wide)
    place_rows = -(-seq_len // wide)

    def as_rows(vector, rows):
        return jnp.pad(vector, (0, rows * wide - vector.shape[0])).reshape(rows, wide)

    extra = jnp.concatenate(
        [
            as_rows(small, small_rows),
            as_rows(segments.astype(bf16), place_rows),
            as_rows((positions // 8).astype(bf16), place_rows),
            as_rows((positions % 8).astype(bf16), place_rows),
        ]
    )
    extra = jnp.pad(extra, ((0, -extra.shape[0] % 16), (0, 0)))
    me = lax.axis_index("model")
    attn_arrays = [w_query, key_weight, value_weight, w_output]

    turned_down = w_down.T
    chunks = [ff - ff // 3, ff // 3] if ff % 768 == 0 else [ff]
    starts = [sum(chunks[:c]) for c in range(len(chunks))]

    def over_data(pieces):
        return lax.all_gather(pieces, "data", axis=0, tiled=False)

    attn_got = swap_pieces(cut_call(me, model, attn_arrays, extra, "attention_pieces"))
    tied = lax.optimization_barrier((halves(hidden_in), halves(out_grad), always, attn_got))
    grad_halves, always = tied[1:3]
    x_near = spread_near(tied[0])
    tied = lax.optimization_barrier((w_gate, w_up, turned_down, x_near))
    w_gate_sent, w_up_sent, turned_down, x_near = tied
    x_blocks = x_near + spread_far(x_near)
    mlp_got = swap(
        lambda i: jnp.concatenate(
            [
                take(weight, i, model)[:, first : first + count]
                for first, count in zip(starts, chunks)
                for weight in (w_gate_sent, w_up_sent, turned_down)
            ],
            axis=1,
        )
    )

    def places_of(first):
        rows = [
            got[shard + first : shard + first + place_rows].reshape(-1)[:seq_len]
            for got in attn_got
        ]
        return jnp.stack(rows).astype(f32)

    seg_all = places_of(small_rows)
    pos_all = 8.0 * places_of(small_rows + place_rows) + places_of(small_rows + 2 * place_rows)
    cosine, sine = tables(pos_all, head_size)

    near = stack_call(me, attn_got, small_rows, "attention_exchange")
    mlp_near = near_call(me, mlp_got, [3 * count for count in chunks], "hidden_exchange")
    attn_full = over_data(near)
    seg_rows = jnp.pad(seg_all[:, None], ((0, 0), (0, 7), (0, 0)))
    shared = [cosine, sine, seg_all[:, :, None], seg_rows]
    tied = lax.optimization_barrier((attn_full, mlp_near, x_blocks, shared))
    attn_full, mlp_near, x_blocks, shared = tied
    mlp_full = [over_data(piece) for piece in mlp_near]

    def with_cores(weight):
        return [weight] + [trade(weight, "tp", j) for j in range(1, cores)]

    near_rows = model * shard
    part = query_gain.shape[0]
    grad_near = spread_near(after(grad_halves, *x_blocks, *mlp_near))

    def gain_of(source, first, size):
        rows = source[:, near_rows : near_rows + model * small_rows]
        return rows.reshape(data * model, -1)[:, first : first + size].astype(f32).reshape(-1)

    o_place = [cols // q_cols] * cores

    def product_phase():
        w_attn = with_cores(attn_full)
        gain_in = (attn_full, near_rows, model)
        if shard % 128:
            gain_in = gain_of(attn_full, 0, shard)
        normed_in, first_raw = rows_product(
            x_blocks, gain_in, w_attn[:1], cols, 0, near_rows, f32, "query_key_value"
        )
        raw = [first_raw[0].reshape(model, half, cols)]
        for j in range(1, cores):
            mine = rows_product(
                [normed_in], None, [w_attn[j]], cols, 0, near_rows, f32, "query_key_value_other"
            )[1][0]
            raw.append(trade(mine, "tp", j).reshape(model, half, cols))
        source = after(attn_full, mine) if cores > 1 else attn_full
        head_gains = [gain_of(source, 2 * shard + i * part, part) for i in range(2)]
        head_gains = jnp.pad(jnp.stack(head_gains), ((0, 6), (0, 0)))
        gains = gain_of(source, 0, shard), gain_of(source, shard, shard)
        return w_attn[1:], normed_in, raw, head_gains, gains

    w_others, own_normed, raw, head_gains, gains = phase(always, product_phase)
    gain_in, gain_mid = gains
    w_attn = [attn_full] + w_others
    raw, grad_near = lax.optimization_barrier((raw, grad_near))

    def attention_phase():
        far = spread_far(grad_near)
        attended = attention_call(
            functools.partial(attend_kernel, cores, kv_heads, repeat),
            "attend",
            core,
            raw,
            shared,
            head_gains,
            [jax.ShapeDtypeStruct((model, half, q_cols), bf16)] * cores,
            [],
            [((seq_len, cols), f32), ((seq_len, q_cols), bf16)],
        )
        attended, far = lax.optimization_barrier((list(attended), far))
        got = [trade(attended[j], "tp", j) for j in range(1, cores)]
        return with_cores(own_normed)[1:], got, attended, far

    normed_others, got, attended, grad_far = phase(always, attention_phase)
    att_flat = [piece.reshape(-1, q_cols) for piece in [attended[0]] + got]
    normed_in = [own_normed] + normed_others
    grad_blocks = grad_near + grad_far

    def data_sum(total):
        return lax.psum_scatter(total, "data", scatter_dimension=0, tiled=False)

    def out_phase():
        own, _, got = project_and_send(
            att_flat, w_attn, o_place, half, near_rows, "attention_out"
        )
        own_grad = join(after(grad_blocks, own), "out_grad_rows")
        middle, *low = rows_call("norm", own, hidden_in, got, gain_mid, None, True, "middle")
        near = spread_near(low)
        return middle, near + spread_far(near), own_grad

    middle, mid_blocks, own_grad = phase(always, out_phase)

    def for_own_core(rows):
        return [
            [rows[k][0]] + [trade(rows[k][j], "tp", j) for j in range(1, cores)] for k in range(2)
        ]

    def hidden_weights(kept, rows, name):
        groups = [[(kept[k][j], rows[k][j]) for j in range(cores)] for k in range(2)]
        return weight_grad(groups, [], (), near_rows, name)

    def first_phase():
        weights = with_cores(mlp_full[0])
        whole, *by_core = hidden_call(mid_blocks, own_grad, weights[:1], "hidden_units_a")
        normed_mid, grad_all = with_cores(whole), with_cores(own_grad)
        by_core = [by_core]
        for weight in weights[1:]:
            got = hidden_call([whole], own_grad, [weight], "hidden_units_a_other")
            by_core.append(got[1:])
        first_rows = [[got[k][0] for got in by_core] for k in range(2)]
        kept = [normed_mid, grad_all]
        total = hidden_weights(kept, for_own_core(first_rows), "hidden_weights_a")
        return weights[1:], normed_mid, grad_all[1:], first_rows, total

    other_weights, normed_mid, grad_others, first_rows, total = phase(always, first_phase)
    kept = [normed_mid, [own_grad] + grad_others]
    w_mlp = [[mlp_full[0]] + other_weights]
    mlp_sums = []
    if len(chunks) > 1:
        mlp_sums.append(data_sum(total))
    count = cores * len(chunks)

    def hidden_phase():
        rows, weights = [first_rows], list(w_mlp)
        if len(chunks) > 1:
            weights.append(with_cores(mlp_full[1]))
            by_core = [
                hidden_call([normed_mid[0]], own_grad, [weight], "hidden_units_b")[1:]
                for weight in weights[1]
            ]
            rows.append([[got[k][0] for got in by_core] for k in range(2)])
        both_cores = [w for pair in weights for w in pair]
        own, _, got = project_and_send(
            [grads for pair in rows for grads in pair[0]],
            both_cores,
            [0] * count,
            half,
            near_rows,
            "normed_mid_grad",
        )
        last_rows = after(for_own_core(rows[-1]), own)
        total = hidden_weights(kept, last_rows, "hidden_weights_b")
        acts = [acts for pair in rows for acts in pair[1]]
        return own, got, total, acts, [w for pair in weights[1:] for w in pair[1:]]

    mid_part, mid_got, total, act_rows, other_weights = phase(always, hidden_phase)
    if len(chunks) > 1:
        mlp_sums.append(data_sum(total))
        w_mlp.append([mlp_full[1]] + other_weights)
    both_cores = [w for pair in w_mlp for w in pair]

    def branch_phase():
        middle_grad, *low = rows_call(
            "back", mid_part, middle, mid_got, gain_mid, out_grad, True, "middle_grad"
        )
        down_parts = project(
            act_rows, both_cores, [2] * count, 0, [half] * model, near_rows, "hidden_out"
        )
        near = spread_near(low)
        branch_blocks = near + spread_far(near, *down_parts)
        return middle_grad, branch_blocks, down_parts

    middle_grad, branch_blocks, down_parts = phase(always, branch_phase)
    tied = lax.optimization_barrier((branch_blocks, down_parts, mlp_sums[0]))
    branch_blocks, down_parts, mlp_sums[0] = tied
    down_got = [trade(down_parts[k], "model", k) for k in range(1, model)]

    def attend_back_phase():
        branch, products = rows_product(
            branch_blocks, None, w_attn, q_cols, o_place[0], near_rows, bf16, "attended_grad"
        )
        products = [piece.reshape(model, half, q_cols) for piece in products]
        att_grads = [trade(piece, "tp", j) if j else piece for j, piece in enumerate(products)]
        *qkv_back, head_grads = attention_call(
            functools.partial(attend_back_kernel, cores, kv_heads, repeat),
            "attend_back",
            core,
            raw + att_grads,
            shared,
            head_gains,
            [jax.ShapeDtypeStruct((model, half, cols), bf16)] * cores,
            [jax.ShapeDtypeStruct(head_gains.shape, f32)],
            [
                ((seq_len, cols), f32),
                ((seq_len, q_cols), bf16),
                ((seq_len, cols), f32),
                ((seq_len, cols), bf16),
            ],
        )
        sent = after(branch, *att_grads)
        branches = [branch] + [trade(sent, "tp", j) for j in range(1, cores)]
        return branches, list(qkv_back), head_grads

    branch, qkv_back, head_grads = phase(always, attend_back_phase)

    def attention_weights_phase():
        back_pieces = [qkv_back[0]] + [trade(qkv_back[j], "tp", j) for j in range(1, cores)]
        ride = head_grads[:2].reshape(-1)
        ride = jnp.pad(ride, (0, ride_rows * wide - ride.shape[0])).astype(bf16)
        ride = jnp.pad(ride.reshape(ride_rows, wide), ((0, -ride_rows % 16), (0, 0)))
        groups = [
            [(normed_in[j], qkv_back[j].reshape(-1, cols)) for j in range(cores)],
            [(branch[j], attended[j].reshape(-1, q_cols)) for j in range(cores)],
        ]
        attn_total = weight_grad(groups, [], [ride], near_rows, "attention_weights")
        return attn_total, [piece.reshape(-1, cols) for piece in back_pieces]

    ride_rows = -(-2 * head_size // wide)
    attn_total, back_flat = phase(always, attention_weights_phase)
    attn_total, down_got = lax.optimization_barrier((attn_total, down_got))
    attn_sum = data_sum(attn_total)
    def in_grad_phase():
        return project_and_send(
            back_flat, w_attn, [0] * cores, half, near_rows, "normed_in_grad", False
        )

    in_part, in_far, in_near = phase(always, in_grad_phase)
    in_near, sums = lax.optimization_barrier((in_near, mlp_sums))

    def last_phase():
        in_got = send_near(in_near, in_far) if model > 1 else []
        rows = jnp.concatenate([total.reshape(model, shard, -1) for total in sums], axis=2)
        mlp_got = swap(rows_at(after(rows, *in_got)))
        hidden_out = rows_call(
            "sum", down_parts[0], middle, after(down_got, *in_got), None, None, False, "hidden_out_sum"
        )[0]
        grad_in = rows_call(
            "back", in_part, hidden_in, in_got, gain_in, middle_grad, False, "grad_in"
        )[0]
        return hidden_out, grad_in, mlp_got

    hidden_out, grad_in, mlp_got = phase(always, last_phase)
    attn_sum = after(attn_sum, grad_in)
    attn_pieces = rows_cut_call(me, model, attn_sum, shard, "attention_sums")
    attn_got = swap_pieces(attn_pieces)
    layout = [
        [
            (kind, first, ff, size, kind == 2)
            for first, size in zip(starts, chunks)
            for kind in range(3)
        ]
    ]
    shapes = [w_gate.shape, w_up.shape, w_down.shape]
    mlp_got = after(mlp_got, attn_pieces[0])
    owned = owned_call(
        me, [mlp_got], layout, [w_gate, w_up], mlp_gain, shapes, "hidden_owned"
    )
    grad_gate, grad_up, grad_down, mlp_part = owned[:4]
    layout = [
        [
            (0, 0, q_cols, q_cols, False),
            (1, 0, kv_cols, kv_cols, False),
            (2, 0, kv_cols, kv_cols, False),
            (3, 0, q_cols, q_cols, True),
        ]
    ]
    weights = [w_query, key_weight, value_weight]
    shapes = [weight.shape for weight in weights] + [w_output.shape]
    owned = owned_call(me, [attn_got], layout, weights, attn_gain, shapes, "attention_owned")
    grad_query, grad_key, grad_value, grad_output, attn_part, gain_sums = owned
    gain_sums = gain_sums[:ride_rows].reshape(-1)[: 2 * head_size]
    sums = lax.psum(jnp.concatenate([attn_part[:, 0], mlp_part[:, 0], gain_sums]), "tp")
    where = lax.axis_index("data") * model + lax.axis_index("model")
    first = 2 * shard + where * part
    return (
        hidden_out,
        grad_in,
        grad_query,
        grad_key,
        grad_value,
        grad_output,
        grad_gate,
        grad_up,
        grad_down,
        sums[:shard],
        sums[shard : 2 * shard],
        lax.dynamic_slice_in_dim(sums, first, part),
        lax.dynamic_slice_in_dim(sums, first + head_size, part),
    )


def solution(mesh):
    fsdp, tp = mesh.shape["fsdp"], mesh.shape["tp"]
    model = 4 if fsdp % 4 == 0 else 1
    split = Mesh(mesh.devices.reshape(fsdp // model, model, tp), ("data", "model", "tp"))
    batch = ("data", "model")
    rows = P(("data", "model", "tp"), None)
    into = P(batch, "tp")
    back = P("tp", batch)
    in_specs = (rows, rows, P(batch), P(batch), into, into, into, back, into, into, back)
    in_specs = in_specs + (P(batch),) * 4
    out_specs = (rows, rows, into, into, into, back, into, into, back) + (P(batch),) * 4
    return jax.shard_map(
        on_device, mesh=split, in_specs=in_specs, out_specs=out_specs, check_vma=False
    )
```

```python
import functools

import jax
import jax.numpy as jnp
from jax import lax
from jax.experimental import pallas as pl
from jax.experimental.pallas import tpu as pltpu
from jax.sharding import Mesh, PartitionSpec as P

epsilon = 1e-06
rope_base = 1000000.0
bf16 = jnp.bfloat16
f32 = jnp.float32
BESIDE = pl.CostEstimate(flops=1 << 20, bytes_accessed=1 << 16, transcendentals=0)


def dot(left, right):
    return jnp.dot(left, right, preferred_element_type=f32)


def dot_right_t(left, right):
    return lax.dot_general(left, right, (((1,), (1,)), ((), ())), preferred_element_type=f32)


def dot_left_t(left, right):
    return lax.dot_general(left, right, (((0,), (0,)), ((), ())), preferred_element_type=f32)


def normalize(operand, norm_gain):
    return (
        operand
        * lax.rsqrt(jnp.mean(operand * operand, axis=-1, keepdims=True) + epsilon)
        * norm_gain
    )


def norm_back(operand, norm_gain, upstream):
    factor = lax.rsqrt(jnp.mean(operand * operand, axis=-1, keepdims=True) + epsilon)
    weighted = upstream * norm_gain
    inner = jnp.mean(weighted * operand, axis=-1, keepdims=True)
    return factor * weighted - operand * factor * factor * factor * inner


def tables(positions, head_size):
    indices = jnp.arange(head_size // 2).astype(f32)
    frequency = rope_base ** (-2.0 * indices / head_size)
    angles = positions.astype(f32)[..., None] * frequency
    cosine, sine = jnp.cos(angles), jnp.sin(angles)
    return (jnp.concatenate([cosine, cosine], -1), jnp.concatenate([-sine, sine], -1))


def half_turn(operand):
    return pltpu.roll(operand, operand.shape[-1] // 2, 1)


def lay_in_order(scratch, refs, core):
    half = refs[0].shape[1]
    for j, ref in enumerate(refs):
        scratch[pl.ds(pl.multiple_of((core ^ j) * half, half), half)] = ref[0]


def head_rows(raw, heads, repeat, gains, cosine, sine):
    size = gains.shape[1]

    def turned(column, gain):
        rows = normalize(raw[:, column * size : (column + 1) * size], gain)
        return (rows * cosine + half_turn(rows) * sine).astype(bf16)

    queries = [turned(h, gains[0:1]) for h in range(heads * repeat)]
    keys = [turned(heads * repeat + g, gains[1:2]) for g in range(heads)]
    first = heads * repeat + heads
    values = [
        raw[:, (first + g) * size : (first + g + 1) * size].astype(bf16) for g in range(heads)
    ]
    return queries, keys, values


def masked_probs(key, query, allowed):
    scores = dot_right_t(key, query) * query.shape[1] ** (-0.5)
    scores = jnp.where(allowed, scores, -1e30)
    exp_terms = jnp.exp(scores - jnp.max(scores, axis=0, keepdims=True))
    return exp_terms * (1.0 / jnp.sum(exp_terms, axis=0, keepdims=True))


def query_strips(rows, column_ref, row_ref):
    step = min(256, rows)
    for first in range(0, rows, step):
        seen = first + step
        keys = lax.broadcasted_iota(jnp.int32, (seen, step), 0)
        queries = lax.broadcasted_iota(jnp.int32, (seen, step), 1) + first
        same = column_ref[0, :seen, 0:1] == row_ref[0, 0:1, first:seen]
        yield slice(first, seen), seen, same & (keys <= queries)


def attend_kernel(cores, heads, repeat, core_ref, *refs):
    raws, refs = refs[:cores], refs[cores:]
    cos_ref, sin_ref, column_ref, row_ref, gain_ref = refs[:5]
    outs, raw, rows_out = refs[5:-2], refs[-2], refs[-1]
    core = core_ref[0]
    half = raws[0].shape[1]
    lay_in_order(raw, raws, core)
    queries, keys, values = head_rows(
        raw, heads, repeat, gain_ref[...], cos_ref[0], sin_ref[0]
    )
    size = gain_ref.shape[1]
    turned = [value.astype(f32).T.astype(bf16) for value in values]
    for at, seen, allowed in query_strips(raw.shape[0], column_ref, row_ref):
        for h, query in enumerate(queries):
            g = h // repeat
            probs = masked_probs(keys[g][:seen], query[at], allowed).astype(bf16)
            rows = dot(turned[g][:, :seen], probs).T
            rows_out[at, h * size : (h + 1) * size] = rows.astype(bf16)
    for j, out in enumerate(outs):
        out[0] = rows_out[pl.ds(pl.multiple_of((core ^ j) * half, half), half)]


def attend_back_kernel(cores, heads, repeat, core_ref, *refs):
    raws, grads, refs = refs[:cores], refs[cores : 2 * cores], refs[2 * cores :]
    cos_ref, sin_ref, column_ref, row_ref, gain_ref = refs[:5]
    outs, gain_out = refs[5 : 5 + cores], refs[5 + cores]
    raw, grad, totals, rows_out = refs[6 + cores :]
    core = core_ref[0]
    half = raws[0].shape[1]
    cosine, sine, gains = cos_ref[0], sin_ref[0], gain_ref[...]
    lay_in_order(raw, raws, core)
    lay_in_order(grad, grads, core)
    queries, keys, values = head_rows(raw, heads, repeat, gains, cosine, sine)
    size = gains.shape[1]
    scale = size ** (-0.5)
    count = heads * repeat

    @pl.when(pl.program_id(0) == 0)
    def _():
        gain_out[...] = jnp.zeros_like(gain_out)

    def columns(i):
        return slice(i * size, (i + 1) * size)

    turned_keys = [key.astype(f32).T.astype(bf16) for key in keys]
    totals[:, count * size :] = jnp.zeros_like(totals[:, count * size :])
    for at, seen, allowed in query_strips(raw.shape[0], column_ref, row_ref):
        for g in range(heads):
            key_grad = value_grad = None
            for h in range(g * repeat, (g + 1) * repeat):
                probs = masked_probs(keys[g][:seen], queries[h][at], allowed)
                out_grad = grad[at, columns(h)]
                prob_grad = dot_right_t(values[g][:seen], out_grad)
                delta = jnp.sum(probs * prob_grad, axis=0, keepdims=True)
                score_grad = (probs * (prob_grad - delta)).astype(bf16)
                totals[at, columns(h)] = dot(turned_keys[g][:, :seen], score_grad).T * scale
                key_part = dot(score_grad, queries[h][at])
                value_part = dot(probs.astype(bf16), out_grad)
                key_grad = key_part if key_grad is None else key_grad + key_part
                value_grad = value_part if value_grad is None else value_grad + value_part
            totals[:seen, columns(count + g)] += key_grad * scale
            totals[:seen, columns(count + heads + g)] += value_grad
    for i in range(count + heads):
        row = 0 if i < count else 1
        upstream = totals[:, columns(i)]
        turned = upstream * cosine - half_turn(upstream) * sine
        rows = raw[:, columns(i)]
        factor = lax.rsqrt(jnp.mean(rows * rows, axis=-1, keepdims=True) + epsilon)
        gain_out[row : row + 1] += jnp.sum(turned * rows * factor, axis=0, keepdims=True)
        back = norm_back(rows, gains[row : row + 1], turned)
        rows_out[:, columns(i)] = back.astype(bf16)
    rows_out[:, (count + heads) * size :] = totals[:, (count + heads) * size :].astype(bf16)
    for j, out in enumerate(outs):
        out[0] = rows_out[pl.ds(pl.multiple_of((core ^ j) * half, half), half)]


def attention_call(kernel, name, core, halves, shared, gains, outs, extra_out, scratch):
    def per_sequence(array):
        return pl.BlockSpec((1,) + array.shape[1:], lambda i: (i, 0, 0))

    whole = pl.BlockSpec(gains.shape, lambda i: (0, 0))
    out_specs = [per_sequence(shape) for shape in outs] + [
        pl.BlockSpec(shape.shape, lambda i: (0, 0)) for shape in extra_out
    ]
    return pl.pallas_call(
        kernel,
        grid=(halves[0].shape[0],),
        in_specs=[pl.BlockSpec(memory_space=pltpu.SMEM)]
        + [per_sequence(array) for array in halves + shared]
        + [whole],
        out_specs=out_specs,
        out_shape=outs + extra_out,
        scratch_shapes=[pltpu.VMEM(shape, dtype) for shape, dtype in scratch],
        compiler_params=pltpu.CompilerParams(vmem_limit_bytes=48 << 20),
        cost_estimate=BESIDE,
        name=name,
    )(core.reshape(1), *halves, *shared, gains)


def resident(shape):
    zeros = (0,) * len(shape)
    return pl.BlockSpec(shape, lambda i: zeros, pipeline_mode=pl.Buffered(1))


def project_kernel(count, *refs):
    lefts, rights, outs = refs[:count], refs[count : 2 * count], refs[2 * count :]

    total = dot_right_t(lefts[0][...], rights[0][0])
    for left, right in zip(lefts[1:], rights[1:]):
        total = total + dot_right_t(left[...], right[0])
    first = 0
    for out in outs:
        out[...] = total[first : first + out.shape[0]].astype(out.dtype)
        first += out.shape[0]


def project(lefts, rights, places, first, sizes, step, name):
    parts = rights[0].shape[0]
    rows = sum(sizes)

    def left_spec(left):
        return pl.BlockSpec(
            (rows, left.shape[1]), lambda i: (first // rows, 0), pipeline_mode=pl.Buffered(1)
        )

    def right_spec(left, place):
        return pl.BlockSpec((1, step, left.shape[1]), lambda i: (i, 0, place))

    return list(
        pl.pallas_call(
            functools.partial(project_kernel, len(lefts)),
            grid=(parts,),
            in_specs=[left_spec(left) for left in lefts]
            + [right_spec(left, place) for left, place in zip(lefts, places)],
            out_specs=[pl.BlockSpec((size, step), lambda i: (0, i)) for size in sizes],
            out_shape=[
                jax.ShapeDtypeStruct((size, parts * step), bf16 if first or k else f32)
                for k, size in enumerate(sizes)
            ],
            compiler_params=pltpu.CompilerParams(vmem_limit_bytes=56 << 20),
            cost_estimate=BESIDE,
            name=name,
        )(*lefts, *rights)
    )


def project_and_send(lefts, rights, places, rows, step, name, near_too=True):
    if lax.axis_size("model") == 1:
        return project(lefts, rights, places, 0, [rows], step, name)[0], [], []
    half = rows // 2
    far = project(lefts, rights, places, 3 * rows, [half] * 2, step, name + "_far")
    got = [trade(far[0], "model", 1), trade(far[1], "model", 2)]
    own, *near = project(lefts, rights, places, 0, [rows] + [half] * 4, step, name)
    return own, got, send_near(near, got) if near_too else near


def put_rows(whole, pieces, change):
    first = 0
    for piece in pieces:
        whole[first : first + piece.shape[0]] = change(piece[...])
        first += piece.shape[0]


def rows_kernel(kind, count, *refs):
    (own, base), got, refs = refs[:2], refs[2 : 2 + count], list(refs[2 + count :])
    total = own[...]
    if count == 4:
        upper = got[0][...].astype(f32) + got[1][...].astype(f32)
        lower = got[2][...].astype(f32) + got[3][...].astype(f32)
        total += jnp.where(pl.program_id(0) == 0, upper, lower)
    else:
        for piece in got:
            total += piece[...].astype(f32)
    rows = base[...].astype(f32)
    if kind == "sum":
        refs[0][...] = (rows + total).astype(bf16)
        return
    gain = refs[0][...]
    if kind == "norm":
        whole, *low = refs[1:]
        total = rows + total
        sent = normalize(total, gain)
    else:
        more, whole, *low = refs[1:]
        total = more[...].astype(f32) + norm_back(rows, gain, total)
        sent = total
    whole[...] = total
    for place, half in enumerate(low):

        @pl.when(pl.program_id(0) == place)
        def _():
            half[...] = sent.astype(bf16)


def rows_call(kind, own, base, got, gain, more, sent, name):
    rows, width = own.shape
    step = rows // 2
    strip = pl.BlockSpec((step, width), lambda i: (i, 0))
    half = resident((step, width))
    operands = [own, base] + list(got)
    in_specs = [strip, strip] + [half if len(got) == 4 else strip] * len(got)
    if gain is not None:
        operands.append(gain.reshape(1, width))
        in_specs.append(resident((1, width)))
    if more is not None:
        operands.append(more)
        in_specs.append(strip)
    out_specs, shapes = [strip], [jax.ShapeDtypeStruct((rows, width), bf16 if gain is None else f32)]
    if sent:
        out_specs += [half] * 2
        shapes += [jax.ShapeDtypeStruct((step, width), bf16)] * 2
    return list(
        pl.pallas_call(
            functools.partial(rows_kernel, kind, len(got)),
            grid=(2,),
            in_specs=in_specs,
            out_specs=out_specs,
            out_shape=shapes,
            compiler_params=pltpu.CompilerParams(vmem_limit_bytes=48 << 20),
            cost_estimate=BESIDE,
            name=name,
        )(*operands)
    )


def rows_product_kernel(count, normed, number, *refs):
    pieces, refs = refs[:count], list(refs[count:])
    gain = None
    if normed:
        source = refs.pop(0)
        gain = source[...]
        if len(source.shape) == 3:
            size = pieces[0].shape[1] // (source.shape[0] * normed)
            parts = [
                gain[i, j : j + 1, :size] for i in range(source.shape[0]) for j in range(normed)
            ]
            gain = jnp.concatenate(parts, axis=1).astype(f32)
    weights, refs = refs[:number], refs[number:]
    whole = pieces[0]
    if count > 1 or normed:
        whole = refs.pop(0)

        def change(rows):
            return normalize(rows.astype(f32), gain).astype(bf16) if normed else rows

        put_rows(whole, pieces, change)
    for weight, out in zip(weights, refs):
        matrix = weight[...].reshape(-1, weight.shape[2])
        out[...] = dot(whole[...], matrix).astype(out.dtype)


def rows_product(pieces, gain, weights, block, place, step, dtype, name):
    rows = sum(piece.shape[0] for piece in pieces)
    parts, width = weights[0].shape[0], pieces[0].shape[1]
    joined = len(pieces) > 1 or gain is not None
    shapes = [jax.ShapeDtypeStruct((rows, width), bf16)] if joined else []
    shapes += [jax.ShapeDtypeStruct((rows, block), dtype)] * len(weights)
    gains, gain_specs, normed = [], [], int(gain is not None)
    if isinstance(gain, tuple):
        array, first, normed = gain
        gains = [array]
        gain_specs = [pl.BlockSpec((parts, 16, array.shape[2]), lambda i: (0, first // 16, 0))]
    elif normed:
        gains, gain_specs = [gain.reshape(1, -1)], [resident((1, gain.shape[0]))]
    got = pl.pallas_call(
        functools.partial(rows_product_kernel, len(pieces), normed, len(weights)),
        grid=(1,),
        in_specs=[resident(piece.shape) for piece in pieces]
        + gain_specs
        + [
            pl.BlockSpec(
                (parts, step, block), lambda i: (0, 0, place), pipeline_mode=pl.Buffered(1)
            )
        ]
        * len(weights),
        out_specs=[resident(shape.shape) for shape in shapes],
        out_shape=shapes,
        compiler_params=pltpu.CompilerParams(vmem_limit_bytes=56 << 20),
        cost_estimate=BESIDE,
        name=name,
    )(*pieces, *gains, *weights)
    return (got[0], list(got[1:])) if joined else (pieces[0], list(got))


def weight_grad_kernel(counts, number, *refs):
    count = sum(counts)
    lefts, rights, refs = refs[:count], refs[count : 2 * count], refs[2 * count :]
    received, below, out = refs[:number], refs[number:-1], refs[-1]
    rows = lefts[0].shape[1]
    first = pair = 0
    for size in counts:
        total = dot_left_t(lefts[pair][...], rights[pair][...])
        for i in range(pair + 1, pair + size):
            total = total + dot_left_t(lefts[i][...], rights[i][...])
        pair += size
        at = slice(first, first + total.shape[1])
        for block in received:
            total = total + block[0, :, at].astype(f32)
        out[0, :rows, at] = total.astype(bf16)
        first += total.shape[1]
    for block in below:
        out[0, rows:] = block[...]


def weight_grad(groups, received, below, step, name):
    pairs = [pair for group in groups for pair in group]
    rows, width = pairs[0][0].shape
    columns = sum(group[0][1].shape[1] for group in groups)
    deep = step + sum(block.shape[0] for block in below)
    return pl.pallas_call(
        functools.partial(
            weight_grad_kernel, [len(group) for group in groups], len(received)
        ),
        grid=(width // step,),
        in_specs=[pl.BlockSpec((rows, step), lambda i: (0, i))] * len(pairs)
        + [resident(right.shape) for _, right in pairs]
        + [pl.BlockSpec((1, step, columns), lambda i: (i, 0, 0))] * len(received)
        + [resident(block.shape) for block in below],
        out_specs=pl.BlockSpec((1, deep, columns), lambda i: (i, 0, 0)),
        out_shape=jax.ShapeDtypeStruct((width // step, deep, columns), bf16),
        compiler_params=pltpu.CompilerParams(vmem_limit_bytes=56 << 20),
        cost_estimate=BESIDE,
        name=name,
    )(*[left for left, _ in pairs], *[right for _, right in pairs], *received, *below)


def cut_kernel(size, parts, me_ref, *refs):
    arrays, below, outs = refs[:parts], refs[parts], refs[parts + 1 :]
    rows = outs[0].shape[0] - below.shape[0]
    for k, out in enumerate(outs):
        owner = me_ref[0] ^ k
        first = 0
        for array in arrays:
            if array.shape[0] == rows:
                wide = array.shape[1] // size
                block = array[:, pl.ds(pl.multiple_of(owner * wide, 128), wide)]
            else:
                wide = array.shape[0] // size
                block = array[pl.ds(pl.multiple_of(owner * wide, 128), wide)]
                block = block.astype(f32).T.astype(bf16)
            out[:rows, first : first + wide] = block
            first += wide
        out[rows:] = below[...]


def cut_call(me, size, arrays, below, name):
    rows = arrays[0].shape[0]
    columns = sum(
        array.shape[1 if array.shape[0] == rows else 0] // size for array in arrays
    )
    shape = jax.ShapeDtypeStruct((rows + below.shape[0], columns), bf16)
    return list(
        pl.pallas_call(
            functools.partial(cut_kernel, size, len(arrays)),
            grid=(1,),
            in_specs=[pl.BlockSpec(memory_space=pltpu.SMEM)]
            + [resident(array.shape) for array in list(arrays) + [below]],
            out_specs=[resident(shape.shape)] * size,
            out_shape=[shape] * size,
            compiler_params=pltpu.CompilerParams(vmem_limit_bytes=32 << 20),
            cost_estimate=BESIDE,
            name=name,
        )(me.reshape(1), *arrays, below)
    )


def rows_cut_kernel(size, rows, me_ref, source, *outs):
    for k, out in enumerate(outs):
        first = pl.multiple_of((me_ref[0] ^ k) * rows, rows)
        out[:rows] = source[pl.ds(first, rows)]
        out[rows:] = source[size * rows :]


def rows_cut_call(me, size, source, rows, name):
    deep = source.shape[0] - (size - 1) * rows
    shape = jax.ShapeDtypeStruct((deep, source.shape[1]), bf16)
    return list(
        pl.pallas_call(
            functools.partial(rows_cut_kernel, size, rows),
            grid=(1,),
            in_specs=[pl.BlockSpec(memory_space=pltpu.SMEM), resident(source.shape)],
            out_specs=[resident(shape.shape)] * size,
            out_shape=[shape] * size,
            compiler_params=pltpu.CompilerParams(vmem_limit_bytes=32 << 20),
            cost_estimate=BESIDE,
            name=name,
        )(me.reshape(1), source)
    )


def stack_kernel(size, below, me_ref, *refs):
    pieces, out = refs[:size], refs[size]
    rows = pieces[0].shape[0] - 16
    under = jnp.zeros((16, out.shape[1]), f32)
    place = lax.broadcasted_iota(jnp.int32, under.shape, 0)
    for k, piece in enumerate(pieces):
        owner = me_ref[0] ^ k
        out[pl.ds(pl.multiple_of(owner * rows, rows), rows)] = piece[:rows]
        more = piece[rows:].astype(f32)
        for i in range(below):
            under = jnp.where(place == owner * below + i, more[i : i + 1], under)
    out[size * rows :] = under.astype(bf16)


def stack_call(me, pieces, below, name):
    size = len(pieces)
    shape = jax.ShapeDtypeStruct(
        (size * (pieces[0].shape[0] - 16) + 16, pieces[0].shape[1]), bf16
    )
    return pl.pallas_call(
        functools.partial(stack_kernel, size, below),
        grid=(1,),
        in_specs=[pl.BlockSpec(memory_space=pltpu.SMEM)]
        + [resident(piece.shape) for piece in pieces],
        out_specs=resident(shape.shape),
        out_shape=shape,
        compiler_params=pltpu.CompilerParams(vmem_limit_bytes=32 << 20),
        cost_estimate=BESIDE,
        name=name,
    )(me.reshape(1), *pieces)


def near_kernel(size, widths, me_ref, *refs):
    pieces, outs = refs[:size], refs[size:]
    rows = pieces[0].shape[0]
    for k, piece in enumerate(pieces):
        at = pl.ds(pl.multiple_of((me_ref[0] ^ k) * rows, rows), rows)
        first = 0
        for out, width in zip(outs, widths):
            out[at] = piece[:, first : first + width]
            first += width


def near_call(me, pieces, widths, name):
    rows = len(pieces) * pieces[0].shape[0]
    shapes = [jax.ShapeDtypeStruct((rows, width), bf16) for width in widths]
    return list(
        pl.pallas_call(
            functools.partial(near_kernel, len(pieces), widths),
            grid=(1,),
            in_specs=[pl.BlockSpec(memory_space=pltpu.SMEM)]
            + [resident(piece.shape) for piece in pieces],
            out_specs=[resident(shape.shape) for shape in shapes],
            out_shape=shapes,
            compiler_params=pltpu.CompilerParams(vmem_limit_bytes=32 << 20),
            cost_estimate=BESIDE,
            name=name,
        )(me.reshape(1), *pieces)
    )


def owned_kernel(size, layout, weighted, me_ref, *refs):
    count = size * len(layout)
    pieces, refs = refs[:count], refs[count:]
    weights, gain, refs = refs[:weighted], refs[weighted], refs[weighted + 1 :]
    outs, sums, below = refs[:-2], refs[-2], refs[-1]
    rows = gain.shape[0]
    total = jnp.zeros((rows, 1), f32)
    under = None
    for c, ranges in enumerate(layout):
        for k in range(size):
            piece = pieces[c * size + k]
            owner = me_ref[0] ^ k
            first = 0
            for number, place, wide, count, turned in ranges:
                block = piece[:rows, first : first + count].astype(f32)
                first += count
                at = pl.ds(pl.multiple_of(owner * wide + place, 128), count)
                if turned:
                    outs[number][at] = block.T
                    continue
                outs[number][:, at] = block
                if number < weighted:
                    product = weights[number][:, at].astype(f32) * block
                    total = total + jnp.sum(product, axis=1, keepdims=True)
            if piece.shape[0] > rows:
                more = piece[rows : rows + 8].astype(f32)
                under = more if under is None else under + more
    sums[...] = jnp.broadcast_to(total / gain[:, 0:1], sums.shape)
    below[...] = jnp.zeros_like(below) if under is None else under


def owned_call(me, chunks, layout, weights, gain, shapes, name):
    size = len(chunks[0])
    pieces = [piece for chunk in chunks for piece in chunk]
    rows = gain.shape[0]
    outs = [jax.ShapeDtypeStruct(shape, f32) for shape in shapes]
    outs += [jax.ShapeDtypeStruct((rows, 128), f32)]
    outs += [jax.ShapeDtypeStruct((8, pieces[0].shape[1]), f32)]
    column = jnp.broadcast_to(gain.astype(f32)[:, None], (rows, 128))
    operands = pieces + list(weights) + [column]
    return pl.pallas_call(
        functools.partial(owned_kernel, size, layout, len(weights)),
        grid=(1,),
        in_specs=[pl.BlockSpec(memory_space=pltpu.SMEM)]
        + [resident(array.shape) for array in operands],
        out_specs=[resident(shape.shape) for shape in outs],
        out_shape=outs,
        compiler_params=pltpu.CompilerParams(vmem_limit_bytes=48 << 20),
        cost_estimate=BESIDE,
        name=name,
    )(me.reshape(1), *operands)


def join_kernel(*refs):
    put_rows(refs[-1], refs[:-1], lambda rows: rows)


def join(pieces, name):
    rows, width = sum(piece.shape[0] for piece in pieces), pieces[0].shape[1]
    return pl.pallas_call(
        join_kernel,
        grid=(1,),
        in_specs=[resident(piece.shape) for piece in pieces],
        out_specs=resident((rows, width)),
        out_shape=jax.ShapeDtypeStruct((rows, width), pieces[0].dtype),
        compiler_params=pltpu.CompilerParams(vmem_limit_bytes=32 << 20),
        cost_estimate=BESIDE,
        name=name,
    )(*pieces)


def hidden_kernel(first, cores, x_count, tiles, *refs):
    refs = list(refs)

    def pop(number):
        taken, refs[:number] = refs[:number], []
        return taken

    x_pieces = pop(x_count)
    g_all = pop(1)[0]
    x_all = x_pieces[0]
    weights = [pop(3) for _ in range(cores)]
    if first:
        x_all = pop(1)[0]
    grads_out, acts_out = pop(cores), pop(cores)
    step = pl.program_id(0)

    if first:

        @pl.when(step == 0)
        def _():
            put_rows(x_all, x_pieces, lambda rows: rows)

    def one_core(j):
        w_gate, w_up, w_down = (ref[...].reshape(-1, ref.shape[2]) for ref in weights[j])
        tile = w_gate.shape[1]
        place = step - j * tiles
        gate_place = pl.ds(pl.multiple_of(place * tile, tile), tile)
        up_place = pl.ds(pl.multiple_of((tiles + place) * tile, tile), tile)
        rows = x_all.shape[0] // 2
        for at in (slice(0, rows), slice(rows, None)):
            gate = dot(x_all[at], w_gate)
            up = dot(x_all[at], w_up)
            act_grad = dot(g_all[at], w_down)
            sigma = 1.0 / (1.0 + jnp.exp(-gate))
            silu = gate * sigma
            gate_grad = act_grad * up * sigma * (1.0 + gate * (1.0 - sigma))
            acts_out[j][at, gate_place] = (silu * up).astype(bf16)
            grads_out[j][at, gate_place] = gate_grad.astype(bf16)
            grads_out[j][at, up_place] = (act_grad * silu).astype(bf16)

    for j in range(cores):
        pl.when((step >= j * tiles) & (step < (j + 1) * tiles))(functools.partial(one_core, j))


def hidden_call(x_pieces, g_all, weights, name):
    cores, first = len(weights), len(x_pieces) > 1
    data, near, columns = weights[0].shape
    width = data * near
    units = columns // 3
    tile = min(256, units)
    tiles = units // tile
    rows = sum(piece.shape[0] for piece in x_pieces)

    def weight_specs(j):
        return [
            pl.BlockSpec(
                (data, near, tile),
                lambda i, k=k: (0, 0, k * tiles + jnp.clip(i - j * tiles, 0, tiles - 1)),
            )
            for k in range(3)
        ]

    operands = list(x_pieces) + [g_all]
    in_specs = [resident(array.shape) for array in operands]
    for j, weight in enumerate(weights):
        in_specs += weight_specs(j)
        operands += [weight] * 3
    shapes = [jax.ShapeDtypeStruct((rows, width), bf16)] if first else []
    shapes += [jax.ShapeDtypeStruct((rows, 2 * units), bf16)] * cores
    shapes += [jax.ShapeDtypeStruct((rows, units), bf16)] * cores
    got = pl.pallas_call(
        functools.partial(
            hidden_kernel, first, cores, len(x_pieces), tiles
        ),
        grid=(cores * tiles,),
        in_specs=in_specs,
        out_specs=[resident(shape.shape) for shape in shapes],
        out_shape=shapes,
        compiler_params=pltpu.CompilerParams(vmem_limit_bytes=60 << 20),
        cost_estimate=BESIDE,
        name=name,
    )(*operands)
    got = list(got)
    whole, got = (got[0], got[1:]) if first else (x_pieces[0], got)
    return whole, got[:cores], got[cores:]


def phase(always, body):
    def never():
        return jax.tree.map(lambda leaf: jnp.zeros(leaf.shape, leaf.dtype), jax.eval_shape(body))

    return lax.cond(always, body, never)


def trade(block, axis, step):
    return lax.ppermute(block, axis, [(i, i ^ step) for i in range(lax.axis_size(axis))])


def halves(rows):
    middle = rows.shape[0] // 2
    return [rows[:middle], rows[middle:]]


def spread_near(own):
    if lax.axis_size("model") == 1:
        return list(own)
    return list(own) + [trade(half, "model", k) for k in (1, 2) for half in own]


def spread_far(near, *first):
    if len(near) == 2:
        return []
    upper, lower = near[2], near[5]
    if first:
        upper, lower = after((upper, lower), *first)
    return [trade(upper, "model", 2), trade(lower, "model", 1)]


def send_near(near, far):
    x_upper, x_lower, y_upper, y_lower = near
    x_upper, y_lower = after((x_upper, y_lower), *far)
    y_upper = (y_upper.astype(f32) + far[0].astype(f32)).astype(bf16)
    x_lower = (x_lower.astype(f32) + far[1].astype(f32)).astype(bf16)
    return [
        trade(x_upper, "model", 1),
        trade(y_upper, "model", 2),
        trade(x_lower, "model", 1),
        trade(y_lower, "model", 2),
    ]


def swap(piece_of):
    me = lax.axis_index("model")
    others = range(1, lax.axis_size("model"))
    return [piece_of(me)] + [trade(piece_of(me ^ k), "model", k) for k in others]


def swap_pieces(pieces):
    return [pieces[0]] + [trade(pieces[k], "model", k) for k in range(1, len(pieces))]


def take(array, index, count):
    size = array.shape[1] // count
    return lax.dynamic_slice_in_dim(array, index * size, size, 1)


def rows_at(array):
    return lambda i: lax.dynamic_index_in_dim(array, i, 0, keepdims=False)


def after(value, *first):
    return lax.optimization_barrier((value,) + first)[0]


def on_device(
    hidden_in,
    out_grad,
    segments,
    positions,
    w_query,
    key_weight,
    value_weight,
    w_output,
    w_gate,
    w_up,
    w_down,
    attn_gain,
    mlp_gain,
    query_gain,
    key_gain,
):
    data = lax.axis_size("data")
    model = lax.axis_size("model")
    cores = lax.axis_size("tp")
    core = lax.axis_index("tp")
    seq_len = positions.shape[0]
    half = seq_len // cores
    shard = w_query.shape[0]
    width = hidden_in.shape[1]
    head_size = query_gain.shape[0] * data * model
    q_heads = w_query.shape[1] // model // head_size
    kv_heads = key_weight.shape[1] // model // head_size
    repeat = q_heads // kv_heads
    q_cols = q_heads * head_size
    kv_cols = kv_heads * head_size
    cols = q_cols + 2 * kv_cols
    wide = cols + q_cols
    ff = w_gate.shape[1] // model
    always = (segments[0] * segments[0] + segments[0]) & 1 == 0

    small = jnp.concatenate([attn_gain, mlp_gain, query_gain, key_gain])
    small_rows = -(-small.shape[0] // wide)
    place_rows = -(-seq_len // wide)

    def as_rows(vector, rows):
        return jnp.pad(vector, (0, rows * wide - vector.shape[0])).reshape(rows, wide)

    extra = jnp.concatenate(
        [
            as_rows(small, small_rows),
            as_rows(segments.astype(bf16), place_rows),
            as_rows((positions // 8).astype(bf16), place_rows),
            as_rows((positions % 8).astype(bf16), place_rows),
        ]
    )
    extra = jnp.pad(extra, ((0, -extra.shape[0] % 16), (0, 0)))
    me = lax.axis_index("model")
    attn_arrays = [w_query, key_weight, value_weight, w_output]

    turned_down = w_down.T
    chunks = [ff - ff // 3, ff // 3] if ff % 768 == 0 else [ff]
    starts = [sum(chunks[:c]) for c in range(len(chunks))]

    def over_data(pieces):
        return lax.all_gather(pieces, "data", axis=0, tiled=False)

    attn_got = swap_pieces(cut_call(me, model, attn_arrays, extra, "attention_pieces"))
    tied = lax.optimization_barrier(
        (halves(hidden_in), halves(out_grad), turned_down, always, attn_got)
    )
    x_halves, grad_halves, turned_down, always, attn_got = tied
    x_near = spread_near(x_halves)
    tied = lax.optimization_barrier((w_gate, w_up, turned_down, x_near))
    w_gate_sent, w_up_sent, turned_down, x_near = tied
    x_blocks = x_near + spread_far(x_near)
    mlp_got = swap(
        lambda i: jnp.concatenate(
            [
                take(weight, i, model)[:, first : first + count]
                for first, count in zip(starts, chunks)
                for weight in (w_gate_sent, w_up_sent, turned_down)
            ],
            axis=1,
        )
    )

    def places_of(first):
        rows = [
            got[shard + first : shard + first + place_rows].reshape(-1)[:seq_len]
            for got in attn_got
        ]
        return jnp.stack(rows).astype(f32)

    seg_all = places_of(small_rows)
    pos_all = 8.0 * places_of(small_rows + place_rows) + places_of(small_rows + 2 * place_rows)
    cosine, sine = tables(pos_all, head_size)

    near = stack_call(me, attn_got, small_rows, "attention_exchange")
    mlp_near = near_call(me, mlp_got, [3 * count for count in chunks], "hidden_exchange")
    attn_full = over_data(near)
    seg_rows = jnp.pad(seg_all[:, None], ((0, 0), (0, 7), (0, 0)))
    shared = [cosine, sine, seg_all[:, :, None], seg_rows]
    tied = lax.optimization_barrier((attn_full, mlp_near, x_blocks, shared))
    attn_full, mlp_near, x_blocks, shared = tied
    mlp_full = [over_data(piece) for piece in mlp_near]

    def with_cores(weight):
        return [weight] + [trade(weight, "tp", j) for j in range(1, cores)]

    near_rows = model * shard
    part = query_gain.shape[0]
    grad_near = spread_near(after(grad_halves, *x_blocks, *mlp_near))

    def gain_of(source, first, size):
        rows = source[:, near_rows : near_rows + model * small_rows]
        return rows.reshape(data * model, -1)[:, first : first + size].astype(f32).reshape(-1)

    o_place = [cols // q_cols] * cores

    def product_phase():
        w_attn = with_cores(attn_full)
        gain_in = (attn_full, near_rows, model)
        if shard % 128:
            gain_in = gain_of(attn_full, 0, shard)
        normed_in, first_raw = rows_product(
            x_blocks, gain_in, w_attn[:1], cols, 0, near_rows, f32, "query_key_value"
        )
        raw = [first_raw[0].reshape(model, half, cols)]
        for j in range(1, cores):
            mine = rows_product(
                [normed_in], None, [w_attn[j]], cols, 0, near_rows, f32, "query_key_value_other"
            )[1][0]
            raw.append(trade(mine, "tp", j).reshape(model, half, cols))
        source = after(attn_full, mine) if cores > 1 else attn_full
        head_gains = [gain_of(source, 2 * shard + i * part, part) for i in range(2)]
        head_gains = jnp.pad(jnp.stack(head_gains), ((0, 6), (0, 0)))
        gains = gain_of(source, 0, shard), gain_of(source, shard, shard)
        return w_attn[1:], normed_in, raw, head_gains, gains

    w_others, own_normed, raw, head_gains, gains = phase(always, product_phase)
    gain_in, gain_mid = gains
    w_attn = [attn_full] + w_others
    raw, grad_near = lax.optimization_barrier((raw, grad_near))

    def attention_phase():
        far = spread_far(grad_near)
        attended = attention_call(
            functools.partial(attend_kernel, cores, kv_heads, repeat),
            "attend",
            core,
            raw,
            shared,
            head_gains,
            [jax.ShapeDtypeStruct((model, half, q_cols), bf16)] * cores,
            [],
            [((seq_len, cols), f32), ((seq_len, q_cols), bf16)],
        )
        attended, far = lax.optimization_barrier((list(attended), far))
        got = [trade(attended[j], "tp", j) for j in range(1, cores)]
        return with_cores(own_normed)[1:], got, attended, far

    normed_others, got, attended, grad_far = phase(always, attention_phase)
    att_flat = [piece.reshape(-1, q_cols) for piece in [attended[0]] + got]
    normed_in = [own_normed] + normed_others
    grad_blocks = grad_near + grad_far

    def data_sum(total):
        return lax.psum_scatter(total, "data", scatter_dimension=0, tiled=False)

    def out_phase():
        own, _, got = project_and_send(
            att_flat, w_attn, o_place, half, near_rows, "attention_out"
        )
        own_grad = join(after(grad_blocks, own), "out_grad_rows")
        middle, *low = rows_call("norm", own, hidden_in, got, gain_mid, None, True, "middle")
        near = spread_near(low)
        return middle, near + spread_far(near), own_grad

    middle, mid_blocks, own_grad = phase(always, out_phase)

    def for_own_core(rows):
        return [
            [rows[k][0]] + [trade(rows[k][j], "tp", j) for j in range(1, cores)] for k in range(2)
        ]

    def hidden_weights(kept, rows, name):
        groups = [[(kept[k][j], rows[k][j]) for j in range(cores)] for k in range(2)]
        return weight_grad(groups, [], (), near_rows, name)

    def first_phase():
        weights = with_cores(mlp_full[0])
        whole, *by_core = hidden_call(mid_blocks, own_grad, weights[:1], "hidden_units_a")
        normed_mid, grad_all = with_cores(whole), with_cores(own_grad)
        by_core = [by_core]
        for weight in weights[1:]:
            got = hidden_call([whole], own_grad, [weight], "hidden_units_a_other")
            by_core.append(got[1:])
        first_rows = [[got[k][0] for got in by_core] for k in range(2)]
        kept = [normed_mid, grad_all]
        total = hidden_weights(kept, for_own_core(first_rows), "hidden_weights_a")
        return weights[1:], normed_mid, grad_all[1:], first_rows, total

    other_weights, normed_mid, grad_others, first_rows, total = phase(always, first_phase)
    kept = [normed_mid, [own_grad] + grad_others]
    w_mlp = [[mlp_full[0]] + other_weights]
    mlp_sums = []
    if len(chunks) > 1:
        mlp_sums.append(data_sum(total))
    count = cores * len(chunks)

    def hidden_phase():
        rows, weights = [first_rows], list(w_mlp)
        if len(chunks) > 1:
            weights.append(with_cores(mlp_full[1]))
            by_core = [
                hidden_call([normed_mid[0]], own_grad, [weight], "hidden_units_b")[1:]
                for weight in weights[1]
            ]
            rows.append([[got[k][0] for got in by_core] for k in range(2)])
        both_cores = [w for pair in weights for w in pair]
        own, _, got = project_and_send(
            [grads for pair in rows for grads in pair[0]],
            both_cores,
            [0] * count,
            half,
            near_rows,
            "normed_mid_grad",
        )
        last_rows = after(for_own_core(rows[-1]), own)
        total = hidden_weights(kept, last_rows, "hidden_weights_b")
        acts = [acts for pair in rows for acts in pair[1]]
        return own, got, total, acts, [w for pair in weights[1:] for w in pair[1:]]

    mid_part, mid_got, total, act_rows, other_weights = phase(always, hidden_phase)
    if len(chunks) > 1:
        mlp_sums.append(data_sum(total))
        w_mlp.append([mlp_full[1]] + other_weights)
    both_cores = [w for pair in w_mlp for w in pair]

    def branch_phase():
        middle_grad, *low = rows_call(
            "back", mid_part, middle, mid_got, gain_mid, out_grad, True, "middle_grad"
        )
        down_parts = project(
            act_rows, both_cores, [2] * count, 0, [half] * model, near_rows, "hidden_out"
        )
        near = spread_near(low)
        branch_blocks = near + spread_far(near, *down_parts)
        return middle_grad, branch_blocks, down_parts

    middle_grad, branch_blocks, down_parts = phase(always, branch_phase)
    tied = lax.optimization_barrier((branch_blocks, down_parts, mlp_sums[0]))
    branch_blocks, down_parts, mlp_sums[0] = tied
    down_got = [trade(down_parts[k], "model", k) for k in range(1, model)]

    def attend_back_phase():
        branch, products = rows_product(
            branch_blocks, None, w_attn, q_cols, o_place[0], near_rows, bf16, "attended_grad"
        )
        products = [piece.reshape(model, half, q_cols) for piece in products]
        att_grads = [trade(piece, "tp", j) if j else piece for j, piece in enumerate(products)]
        *qkv_back, head_grads = attention_call(
            functools.partial(attend_back_kernel, cores, kv_heads, repeat),
            "attend_back",
            core,
            raw + att_grads,
            shared,
            head_gains,
            [jax.ShapeDtypeStruct((model, half, cols), bf16)] * cores,
            [jax.ShapeDtypeStruct(head_gains.shape, f32)],
            [
                ((seq_len, cols), f32),
                ((seq_len, q_cols), bf16),
                ((seq_len, cols), f32),
                ((seq_len, cols), bf16),
            ],
        )
        sent = after(branch, *att_grads)
        branches = [branch] + [trade(sent, "tp", j) for j in range(1, cores)]
        return branches, list(qkv_back), head_grads

    branch, qkv_back, head_grads = phase(always, attend_back_phase)

    def attention_weights_phase():
        back_pieces = [qkv_back[0]] + [trade(qkv_back[j], "tp", j) for j in range(1, cores)]
        ride = head_grads[:2].reshape(-1)
        ride = jnp.pad(ride, (0, ride_rows * wide - ride.shape[0])).astype(bf16)
        ride = jnp.pad(ride.reshape(ride_rows, wide), ((0, -ride_rows % 16), (0, 0)))
        groups = [
            [(normed_in[j], qkv_back[j].reshape(-1, cols)) for j in range(cores)],
            [(branch[j], attended[j].reshape(-1, q_cols)) for j in range(cores)],
        ]
        attn_total = weight_grad(groups, [], [ride], near_rows, "attention_weights")
        return attn_total, [piece.reshape(-1, cols) for piece in back_pieces]

    ride_rows = -(-2 * head_size // wide)
    attn_total, back_flat = phase(always, attention_weights_phase)
    attn_total, down_got = lax.optimization_barrier((attn_total, down_got))
    attn_sum = data_sum(attn_total)
    def in_grad_phase():
        return project_and_send(
            back_flat, w_attn, [0] * cores, half, near_rows, "normed_in_grad", False
        )

    in_part, in_far, in_near = phase(always, in_grad_phase)
    in_near, sums = lax.optimization_barrier((in_near, mlp_sums))

    def last_phase():
        in_got = send_near(in_near, in_far) if model > 1 else []
        rows = jnp.concatenate([total.reshape(model, shard, -1) for total in sums], axis=2)
        mlp_got = swap(rows_at(after(rows, *in_got)))
        hidden_out = rows_call(
            "sum", down_parts[0], middle, after(down_got, *in_got), None, None, False, "hidden_out_sum"
        )[0]
        grad_in = rows_call(
            "back", in_part, hidden_in, in_got, gain_in, middle_grad, False, "grad_in"
        )[0]
        return hidden_out, grad_in, mlp_got

    hidden_out, grad_in, mlp_got = phase(always, last_phase)
    attn_sum = after(attn_sum, grad_in)
    attn_pieces = rows_cut_call(me, model, attn_sum, shard, "attention_sums")
    attn_got = swap_pieces(attn_pieces)
    layout = [
        [
            (kind, first, ff, size, kind == 2)
            for first, size in zip(starts, chunks)
            for kind in range(3)
        ]
    ]
    shapes = [w_gate.shape, w_up.shape, w_down.shape]
    mlp_got = after(mlp_got, attn_pieces[0])
    owned = owned_call(
        me, [mlp_got], layout, [w_gate, w_up], mlp_gain, shapes, "hidden_owned"
    )
    grad_gate, grad_up, grad_down, mlp_part = owned[:4]
    layout = [
        [
            (0, 0, q_cols, q_cols, False),
            (1, 0, kv_cols, kv_cols, False),
            (2, 0, kv_cols, kv_cols, False),
            (3, 0, q_cols, q_cols, True),
        ]
    ]
    weights = [w_query, key_weight, value_weight]
    shapes = [weight.shape for weight in weights] + [w_output.shape]
    owned = owned_call(me, [attn_got], layout, weights, attn_gain, shapes, "attention_owned")
    grad_query, grad_key, grad_value, grad_output, attn_part, gain_sums = owned
    gain_sums = gain_sums[:ride_rows].reshape(-1)[: 2 * head_size]
    sums = lax.psum(jnp.concatenate([attn_part[:, 0], mlp_part[:, 0], gain_sums]), "tp")
    where = lax.axis_index("data") * model + lax.axis_index("model")
    first = 2 * shard + where * part
    return (
        hidden_out,
        grad_in,
        grad_query,
        grad_key,
        grad_value,
        grad_output,
        grad_gate,
        grad_up,
        grad_down,
        sums[:shard],
        sums[shard : 2 * shard],
        lax.dynamic_slice_in_dim(sums, first, part),
        lax.dynamic_slice_in_dim(sums, first + head_size, part),
    )


def solution(mesh):
    fsdp, tp = mesh.shape["fsdp"], mesh.shape["tp"]
    model = 4 if fsdp % 4 == 0 else 1
    split = Mesh(mesh.devices.reshape(fsdp // model, model, tp), ("data", "model", "tp"))
    batch = ("data", "model")
    rows = P(("data", "model", "tp"), None)
    into = P(batch, "tp")
    back = P("tp", batch)
    in_specs = (rows, rows, P(batch), P(batch), into, into, into, back, into, into, back)
    in_specs = in_specs + (P(batch),) * 4
    out_specs = (rows, rows, into, into, into, back, into, into, back) + (P(batch),) * 4
    return jax.shard_map(
        on_device, mesh=split, in_specs=in_specs, out_specs=out_specs, check_vma=False
    )
```
